512 devices in a mesh: gx: 64 (over z_hi, x, y), gy: 8 (over z_lo, core).
Axes of the slice: x: 4, y: 4, z: 16 (z_hi: 4, z_lo: 4; z = z_hi * 4 + z_lo), core: 2. Of those that a mesh axis runs over, the one named last changes fastest.
Arguments:
- velocity: float32 [3, 256, 128, 128], P(None, 'gx', 'gy'), may hold values from -6 to 6
- canopy: int32 [256, 128, 128], P('gx', 'gy'), may hold values 0 or 1
- weight_in: bfloat16 [648, 512], replicated, may hold values from -0.25 to 0.25
- bias_in: float32 [512], replicated, may hold values from -6 to 6
- weight_out: bfloat16 [512, 384], replicated, may hold values from -0.25 to 0.25
- bias_out: float32 [384], replicated, may hold values from -6 to 6
- cotangent: bfloat16 [3, 256, 128, 128], P(None, 'gx', 'gy'), may hold values from -24 to 24
Outputs:
- new_velocity: float32 [3, 256, 128, 128], P(None, 'gx', 'gy')
- velocity_grad: float32 [3, 256, 128, 128], P(None, 'gx', 'gy')
- weight_in_grad: float32 [648, 512], replicated
- bias_in_grad: float32 [512], replicated
- weight_out_grad: float32 [512, 384], replicated
- bias_out_grad: float32 [384], replicated
The draws below stay inside these ranges and needn't reach their ends.
Inputs may be any that keep to these rules, and one draw needn't show every extreme that they name: canopy holds only 0 and 1.
All inputs are finite; a program needn't handle non-finite values. No bound on the sum of `canopy` on one device may be relied on, other than what follows from the above.
Results may differ from the reference program's by a relative error of at most 0.0056.
Values sent between devices are 32-bit elements; how exact they have to be, the bound alone decides.
No kernel may reach another device: no remote copies, remote signals or barrier semaphores. Data moves between devices by JAX's collectives and lax.ppermute only.
A program may use at most 128 MiB of HBM per device.

```python
import jax
import jax.numpy as jnp
from jax import lax

IN = 648
HID = 512
OUTW = 384
NX = 256
NY = 128
NZ = 128
BLOCKS = 65536


def with_ends(array, key, low, high):
    spot = [jax.random.randint(jax.random.fold_in(key, axis), (), 0, length) for axis, length in enumerate(array.shape)]
    longest = array.shape.index(max(array.shape))
    neighbour = spot[:longest] + [(spot[longest] + 1) % array.shape[longest]] + spot[longest + 1:]
    return array.at[tuple(spot)].set(low).at[tuple(neighbour)].set(high)


def levels(stream_key, dims, shards, least, top_value):
    loudness = 1.0
    for position, parts in shards:
        heights = jax.random.uniform(jax.random.fold_in(jax.random.fold_in(stream_key, 6), position), (parts,), jnp.float32, least / len(shards), top_value / len(shards))
        loudness = loudness * jnp.repeat(jnp.exp(heights), dims[position] // parts).reshape((-1,) + (1,) * (len(dims) - 1 - position))
    return loudness


def noise(own_key, extent, deviation, limit, shards=(), kind=jnp.bfloat16):
    entries = jax.random.normal(own_key, extent, jnp.float32) * deviation
    if len(shards) > 0:
        entries = levels(own_key, extent, shards, -0.22, 0.18) * entries
    return jnp.clip(entries, min=-limit, max=limit).astype(kind)


def setup_inputs(seed: int = 0) -> dict:
    keys = jax.random.split(jax.random.key(seed), 8)
    velocity = noise(keys[0], (3, NX, NY, NZ), 1.0, 6.0, ((1, 64), (2, 8)), jnp.float32)
    canopy = with_ends((jax.random.randint(keys[1], (NX, NY, NZ), 0, 3) < 1).astype(jnp.int32), jax.random.fold_in(keys[1], 1), 0, 1)
    weight_in = noise(keys[2], (IN, HID), IN ** -0.5, 0.25)
    bias_in = noise(keys[3], (HID,), 1.0, 6.0, (), jnp.float32)
    weight_out = noise(keys[4], (HID, OUTW), HID ** -0.5, 0.25)
    bias_out = noise(keys[5], (OUTW,), 1.0, 6.0, (), jnp.float32)
    cotangent = noise(keys[6], (3, NX, NY, NZ), 4.0, 24.0, ((1, 64), (2, 8)))
    return dict(velocity=velocity, canopy=canopy, weight_in=weight_in, bias_in=bias_in, weight_out=weight_out, bias_out=bias_out, cotangent=cotangent)


time_step = 0.25
viscosity = 0.2
penalty_eta = 0.05


def pad_depth(field):
    return jnp.pad(field, ((0, 0), (0, 0), (0, 0), (1, 1)))


def pad_whole(field):
    wrapped = jnp.pad(field, ((0, 0), (1, 1), (1, 1), (0, 0)), mode="wrap")
    return pad_depth(wrapped)


def centred(padded, axis):
    if axis == 1:
        return (padded[:, 2:, 1:-1, 1:-1] - padded[:, :-2, 1:-1, 1:-1]) * 0.5
    if axis == 2:
        return (padded[:, 1:-1, 2:, 1:-1] - padded[:, 1:-1, :-2, 1:-1]) * 0.5
    return (padded[:, 1:-1, 1:-1, 2:] - padded[:, 1:-1, 1:-1, :-2]) * 0.5


def laplace(padded):
    middle = padded[:, 1:-1, 1:-1, 1:-1]
    total = padded[:, 2:, 1:-1, 1:-1] + padded[:, :-2, 1:-1, 1:-1]
    total = total + padded[:, 1:-1, 2:, 1:-1] + padded[:, 1:-1, :-2, 1:-1]
    total = total + padded[:, 1:-1, 1:-1, 2:] + padded[:, 1:-1, 1:-1, :-2]
    return total - 6.0 * middle


def advect(padded):
    first = centred(padded[0:1] * padded, 1)
    second = centred(padded[1:2] * padded, 2)
    third = centred(padded[2:3] * padded, 3)
    return first + second + third


def divergence(along_x, along_y, along_z):
    part_x = (along_x[:, 2:] - along_x[:, :-2]) * 0.5
    part_y = (along_y[:, :, 2:] - along_y[:, :, :-2]) * 0.5
    part_z = (along_z[:, :, :, 2:] - along_z[:, :, :, :-2]) * 0.5
    return part_x + part_y + part_z


def select(stack_in, indices):
    return jnp.stack([stack_in[entry] for entry in indices])


def to_blocks(padded):
    count_x = (padded.shape[1] - 2) // 4
    count_y = (padded.shape[2] - 2) // 4
    count_z = (padded.shape[3] - 2) // 4
    stacked = jnp.stack([padded[:, offset:offset + 4 * count_x:4] for offset in range(6)], axis=1)
    stacked = jnp.stack([stacked[:, :, :, offset:offset + 4 * count_y:4] for offset in range(6)], axis=3)
    stacked = jnp.stack([stacked[..., offset:offset + 4 * count_z:4] for offset in range(6)], axis=5)
    stacked = stacked.transpose(0, 1, 3, 5, 2, 4, 6)
    return stacked.reshape(stacked.shape[0] * 216, -1)


def from_rows(outputs, count_x, count_y, count_z):
    shaped = outputs.reshape(6, 4, 4, 4, count_x, count_y, count_z).transpose(0, 4, 1, 5, 2, 6, 3)
    return shaped.reshape(6, 4 * count_x, 4 * count_y, 4 * count_z)


def to_rows(stress_grad):
    count_x = stress_grad.shape[1] // 4
    count_y = stress_grad.shape[2] // 4
    count_z = stress_grad.shape[3] // 4
    shaped = stress_grad.reshape(6, count_x, 4, count_y, 4, count_z, 4).transpose(0, 2, 4, 6, 1, 3, 5)
    return shaped.reshape(384, count_x * count_y * count_z)


def fold_last(stacked):
    count = stacked.shape[-1]
    leading = stacked.shape[:-2]
    main = jnp.stack([stacked[..., offset, :] for offset in range(4)], axis=-1).reshape(leading + (4 * count,))
    blank = jnp.zeros_like(stacked[..., 0, :])
    extra = jnp.stack([stacked[..., 4, :], stacked[..., 5, :], blank, blank], axis=-1).reshape(leading + (4 * count,))
    main = jnp.concatenate([main, jnp.zeros(leading + (2,), main.dtype)], axis=-1)
    extra = jnp.concatenate([jnp.zeros(leading + (4,), extra.dtype), extra[..., :4 * count - 2]], axis=-1)
    return main + extra


def fold_depth_side(column_grad, count_x, count_y, count_z):
    shaped = column_grad.reshape(3, 6, 6, 6, count_x, count_y, count_z).transpose(0, 1, 4, 2, 5, 3, 6)
    shaped = fold_last(shaped)
    shaped = jnp.moveaxis(shaped, (3, 4), (4, 5))
    return fold_last(shaped)


def fold_across(shaped):
    moved = jnp.moveaxis(shaped, (1, 2), (3, 4))
    return fold_last(moved).transpose(0, 3, 2, 1)


def closure(columns, stress_rows, weight_in, bias_in, weight_out, bias_out):
    pre_act = lax.dot_general(weight_in, columns, (((0,), (0,)), ((), ())), preferred_element_type=jnp.float32) + bias_in[:, None]
    hidden = jax.nn.silu(pre_act).astype(jnp.bfloat16)
    outputs = lax.dot_general(weight_out, hidden, (((0,), (0,)), ((), ())), preferred_element_type=jnp.float32) + bias_out[:, None]
    bias_out_sum = jnp.sum(stress_rows, axis=1)
    rows_low = stress_rows.astype(jnp.bfloat16)
    weight_out_sum = lax.dot_general(hidden, rows_low, (((1,), (1,)), ((), ())), preferred_element_type=jnp.float32)
    hidden_grad = lax.dot_general(weight_out, rows_low, (((1,), (0,)), ((), ())), preferred_element_type=jnp.float32)
    sigmoid_pre = jax.nn.sigmoid(pre_act)
    pre_grad = hidden_grad * (sigmoid_pre * (1.0 + pre_act * (1.0 - sigmoid_pre)))
    bias_in_sum = jnp.sum(pre_grad, axis=1)
    pre_low = pre_grad.astype(jnp.bfloat16)
    weight_in_sum = lax.dot_general(columns, pre_low, (((1,), (1,)), ((), ())), preferred_element_type=jnp.float32)
    column_grad = lax.dot_general(weight_in, pre_low, (((1,), (0,)), ((), ())), preferred_element_type=jnp.float32)
    return outputs, column_grad, weight_in_sum, bias_in_sum, weight_out_sum, bias_out_sum


def stress_from_slopes(grad_x, grad_y, grad_z):
    return -jnp.stack([grad_x[0], grad_y[1], grad_z[2], grad_y[0] + grad_x[1], grad_z[0] + grad_x[2], grad_z[1] + grad_y[2]])


def reference(velocity, canopy, weight_in, bias_in, weight_out, bias_out, cotangent):
    padded = pad_whole(velocity)
    factor = 1.0 + time_step * canopy.astype(jnp.float32) / penalty_eta
    incoming = cotangent.astype(jnp.float32)
    direct = incoming / factor
    adjoint = time_step * direct
    adj_pad = pad_whole(adjoint)
    grad_x = centred(adj_pad, 1)
    grad_y = centred(adj_pad, 2)
    grad_z = centred(adj_pad, 3)
    stress_grad = stress_from_slopes(grad_x, grad_y, grad_z)
    count_x = NX // 4
    count_y = NY // 4
    count_z = NZ // 4

    def slab_work(index):
        piece = lax.dynamic_slice_in_dim(padded, index * 4, 6, axis=1)
        columns = to_blocks(piece).astype(jnp.bfloat16)
        stress_piece = lax.dynamic_slice_in_dim(stress_grad, index * 4, 4, axis=1)
        outputs, column_grad, w_in_s, b_in_s, w_out_s, b_out_s = closure(columns, to_rows(stress_piece), weight_in, bias_in, weight_out, bias_out)
        stress_slab = from_rows(outputs, 1, count_y, count_z)
        ghost_slab = fold_depth_side(column_grad, 1, count_y, count_z)
        return stress_slab, ghost_slab, w_in_s, b_in_s, w_out_s, b_out_s

    slabs = lax.map(slab_work, jnp.arange(count_x, dtype=jnp.int32))
    stress = slabs[0].transpose(1, 0, 2, 3, 4).reshape(6, NX, NY, NZ)
    ghost_parts = slabs[1][:, :, :, 0].transpose(1, 2, 0, 3, 4)
    ghost = fold_across(ghost_parts)[..., 1:-1]
    stress_pad = pad_whole(stress)
    along_x = select(stress_pad, (0, 3, 4))[:, :, 1:-1, 1:-1]
    along_y = select(stress_pad, (3, 1, 5))[:, 1:-1, :, 1:-1]
    along_z = select(stress_pad, (4, 5, 2))[:, 1:-1, 1:-1, :]
    force = divergence(along_x, along_y, along_z)
    rhs = -advect(padded) + viscosity * laplace(padded) + force
    new_velocity = (velocity + time_step * rhs) / factor
    transport_a = jnp.stack([jnp.sum(grad_x * velocity, axis=0), jnp.sum(grad_y * velocity, axis=0), jnp.sum(grad_z * velocity, axis=0)])
    transport_b = grad_x * velocity[0:1] + grad_y * velocity[1:2] + grad_z * velocity[2:3]
    stencil_grad = direct + transport_a + transport_b + viscosity * laplace(adj_pad)
    core = ghost[:, 1:-1]
    core = core.at[:, 0].add(ghost[:, -1]).at[:, -1].add(ghost[:, 0])
    folded = core[:, :, 1:-1]
    folded = folded.at[:, :, 0].add(core[:, :, -1]).at[:, :, -1].add(core[:, :, 0])
    velocity_grad = stencil_grad + folded
    scale = float(BLOCKS) ** -0.5
    weight_in_grad = jnp.sum(slabs[2], axis=0) * scale
    bias_in_grad = jnp.sum(slabs[3], axis=0) * scale
    weight_out_grad = jnp.sum(slabs[4], axis=0) * scale
    bias_out_grad = jnp.sum(slabs[5], axis=0) * scale
    return new_velocity, velocity_grad, weight_in_grad, bias_in_grad, weight_out_grad, bias_out_grad
```

```python
import jax
import jax.numpy as jnp
from jax import lax
from jax.sharding import Mesh, PartitionSpec as P

time_step = 0.25
viscosity = 0.2
penalty_eta = 0.05


GX = ("zh", "x", "y")
GY = ("zl", "core")
ROWS = 136
PARTS = 16


def flatten(weight_in_sum, bias_in_sum, weight_out_sum, bias_out_sum):
    pieces = [weight_in_sum[:, start : start + 128] for start in range(0, 512, 128)]
    pieces += [weight_out_sum[:, start : start + 128] for start in range(0, 384, 128)]
    pieces += [bias_in_sum.reshape(4, 128), bias_out_sum.reshape(3, 128)]
    rows = sum(piece.shape[0] for piece in pieces)
    pieces.append(jnp.zeros((2 * PARTS * ROWS - rows, 128), jnp.float32))
    return jnp.concatenate(pieces, axis=0)


def unflatten(flat):
    weight_in_sum = jnp.concatenate([flat[648 * i : 648 * i + 648] for i in range(4)], axis=1)
    base = 4 * 648
    weight_out_sum = jnp.concatenate(
        [flat[base + 512 * i : base + 512 * i + 512] for i in range(3)], axis=1
    )
    base = base + 3 * 512
    bias_in_sum = flat[base : base + 4].reshape(512)
    bias_out_sum = flat[base + 4 : base + 7].reshape(384)
    return weight_in_sum, bias_in_sum, weight_out_sum, bias_out_sum


def sum_everywhere(flat):
    core = lax.axis_index("core")
    swap = [(0, 1), (1, 0)]
    halves = flat.reshape(2, PARTS, ROWS, 128)
    got = lax.ppermute(halves[1 - core], "core", swap)
    half = halves[core] + got
    part = jnp.sum(lax.all_to_all(half, ("x", "y"), 0, 0), axis=0)
    part = jnp.pad(part, ((0, 144 - ROWS), (0, 0))).reshape(16, 9, 128)
    piece = jnp.sum(lax.all_to_all(part, ("zh", "zl"), 0, 0), axis=0)
    part = lax.all_to_all(jnp.broadcast_to(piece, part.shape), ("zh", "zl"), 0, 0)
    part = part.reshape(144, 128)[:ROWS]
    half = lax.all_to_all(jnp.broadcast_to(part, half.shape), ("x", "y"), 0, 0)
    other = lax.ppermute(half, "core", swap)
    first = jnp.where(core == 0, half, other)
    second = jnp.where(core == 0, other, half)
    return jnp.stack([first, second]).reshape(2 * PARTS * ROWS, 128)


def extended(block, sides, width):
    for axis, dim in sides:
        count = lax.axis_size(axis)
        forward = [(i, i + 1) for i in range(count - 1)]
        forward.append((count - 1, 0))
        backward = [(target, source) for source, target in forward]
        low = lax.ppermute(
            lax.slice_in_dim(block, block.shape[dim] - width, None, axis=dim), axis, forward
        )
        high = lax.ppermute(lax.slice_in_dim(block, 0, width, axis=dim), axis, backward)
        block = jnp.concatenate([low, block, high], axis=dim)
    return block


def pad_depth(field):
    return jnp.pad(field, ((0, 0), (0, 0), (0, 0), (1, 1)))


def centred(padded, axis):
    if axis == 1:
        return (padded[:, 2:, 1:-1, 1:-1] - padded[:, :-2, 1:-1, 1:-1]) * 0.5
    if axis == 2:
        return (padded[:, 1:-1, 2:, 1:-1] - padded[:, 1:-1, :-2, 1:-1]) * 0.5
    return (padded[:, 1:-1, 1:-1, 2:] - padded[:, 1:-1, 1:-1, :-2]) * 0.5


def laplace(padded):
    middle = padded[:, 1:-1, 1:-1, 1:-1]
    total = padded[:, 2:, 1:-1, 1:-1] + padded[:, :-2, 1:-1, 1:-1]
    total = total + padded[:, 1:-1, 2:, 1:-1] + padded[:, 1:-1, :-2, 1:-1]
    total = total + padded[:, 1:-1, 1:-1, 2:] + padded[:, 1:-1, 1:-1, :-2]
    return total - 6.0 * middle


def advect(padded):
    first = centred(padded[0:1] * padded, 1)
    second = centred(padded[1:2] * padded, 2)
    third = centred(padded[2:3] * padded, 3)
    return first + second + third


def divergence(along_x, along_y, along_z):
    part_x = (along_x[:, 2:] - along_x[:, :-2]) * 0.5
    part_y = (along_y[:, :, 2:] - along_y[:, :, :-2]) * 0.5
    part_z = (along_z[:, :, :, 2:] - along_z[:, :, :, :-2]) * 0.5
    return part_x + part_y + part_z


def select(stack_in, indices):
    return jnp.stack([stack_in[entry] for entry in indices])


def to_blocks(padded):
    count_x = (padded.shape[1] - 2) // 4
    count_y = (padded.shape[2] - 2) // 4
    count_z = (padded.shape[3] - 2) // 4
    stacked = jnp.stack(
        [padded[:, offset : offset + 4 * count_x : 4] for offset in range(6)], axis=1
    )
    stacked = jnp.stack(
        [stacked[:, :, :, offset : offset + 4 * count_y : 4] for offset in range(6)], axis=3
    )
    stacked = jnp.stack(
        [stacked[..., offset : offset + 4 * count_z : 4] for offset in range(6)], axis=5
    )
    stacked = stacked.transpose(0, 1, 3, 5, 2, 4, 6)
    return stacked.reshape(stacked.shape[0] * 216, -1)


def from_rows(outputs, count_x, count_y, count_z):
    shaped = outputs.reshape(6, 4, 4, 4, count_x, count_y, count_z).transpose(0, 4, 1, 5, 2, 6, 3)
    return shaped.reshape(6, 4 * count_x, 4 * count_y, 4 * count_z)


def to_rows(stress_grad):
    count_x = stress_grad.shape[1] // 4
    count_y = stress_grad.shape[2] // 4
    count_z = stress_grad.shape[3] // 4
    shaped = stress_grad.reshape(6, count_x, 4, count_y, 4, count_z, 4).transpose(
        0, 2, 4, 6, 1, 3, 5
    )
    return shaped.reshape(384, count_x * count_y * count_z)


def fold_last(stacked):
    count = stacked.shape[-1]
    leading = stacked.shape[:-2]
    main = jnp.stack([stacked[..., offset, :] for offset in range(4)], axis=-1).reshape(
        leading + (4 * count,)
    )
    blank = jnp.zeros_like(stacked[..., 0, :])
    extra = jnp.stack([stacked[..., 4, :], stacked[..., 5, :], blank, blank], axis=-1).reshape(
        leading + (4 * count,)
    )
    main = jnp.concatenate([main, jnp.zeros(leading + (2,), main.dtype)], axis=-1)
    extra = jnp.concatenate(
        [jnp.zeros(leading + (4,), extra.dtype), extra[..., : 4 * count - 2]], axis=-1
    )
    return main + extra


def fold_depth_side(column_grad, count_x, count_y, count_z):
    shaped = column_grad.reshape(3, 6, 6, 6, count_x, count_y, count_z).transpose(
        0, 1, 4, 2, 5, 3, 6
    )
    shaped = fold_last(shaped)
    shaped = jnp.moveaxis(shaped, (3, 4), (4, 5))
    return fold_last(shaped)


def fold_across(shaped):
    moved = jnp.moveaxis(shaped, (1, 2), (3, 4))
    return fold_last(moved).transpose(0, 3, 2, 1)


def closure(columns, stress_rows, weight_in, bias_in, weight_out, bias_out):
    pre_act = (
        lax.dot_general(
            weight_in, columns, (((0,), (0,)), ((), ())), preferred_element_type=jnp.float32
        )
        + bias_in[:, None]
    )
    hidden = jax.nn.silu(pre_act).astype(jnp.bfloat16)
    outputs = (
        lax.dot_general(
            weight_out, hidden, (((0,), (0,)), ((), ())), preferred_element_type=jnp.float32
        )
        + bias_out[:, None]
    )
    bias_out_sum = jnp.sum(stress_rows, axis=1)
    rows_low = stress_rows.astype(jnp.bfloat16)
    weight_out_sum = lax.dot_general(
        hidden, rows_low, (((1,), (1,)), ((), ())), preferred_element_type=jnp.float32
    )
    hidden_grad = lax.dot_general(
        weight_out, rows_low, (((1,), (0,)), ((), ())), preferred_element_type=jnp.float32
    )
    sigmoid_pre = jax.nn.sigmoid(pre_act)
    pre_grad = hidden_grad * (sigmoid_pre * (1.0 + pre_act * (1.0 - sigmoid_pre)))
    bias_in_sum = jnp.sum(pre_grad, axis=1)
    pre_low = pre_grad.astype(jnp.bfloat16)
    weight_in_sum = lax.dot_general(
        columns, pre_low, (((1,), (1,)), ((), ())), preferred_element_type=jnp.float32
    )
    column_grad = lax.dot_general(
        weight_in, pre_low, (((1,), (0,)), ((), ())), preferred_element_type=jnp.float32
    )
    return (outputs, column_grad, weight_in_sum, bias_in_sum, weight_out_sum, bias_out_sum)


def stress_from_slopes(grad_x, grad_y, grad_z):
    return -jnp.stack(
        [
            grad_x[0],
            grad_y[1],
            grad_z[2],
            grad_y[0] + grad_x[1],
            grad_z[0] + grad_x[2],
            grad_z[1] + grad_y[2],
        ]
    )


def on_device(velocity, canopy, weight_in, bias_in, weight_out, bias_out, cotangent):
    count_x = velocity.shape[1] // 4
    count_y = velocity.shape[2] // 4
    count_z = velocity.shape[3] // 4
    rimmed = extended(velocity, ((GX, 1), (GY, 2)), 1)
    padded = pad_depth(rimmed)
    factor = 1.0 + time_step * canopy.astype(jnp.float32) / penalty_eta
    incoming = cotangent.astype(jnp.float32)
    direct = incoming / factor
    adjoint = time_step * direct
    adj_pad = pad_depth(extended(adjoint, ((GX, 1), (GY, 2)), 1))
    grad_x = centred(adj_pad, 1)
    grad_y = centred(adj_pad, 2)
    grad_z = centred(adj_pad, 3)
    stress_grad = stress_from_slopes(grad_x, grad_y, grad_z)
    columns = to_blocks(padded).astype(jnp.bfloat16)
    outputs, column_grad, w_in_s, b_in_s, w_out_s, b_out_s = closure(
        columns, to_rows(stress_grad), weight_in, bias_in, weight_out, bias_out
    )
    stress = from_rows(outputs, count_x, count_y, count_z)
    stress_pad = pad_depth(extended(stress, ((GX, 1), (GY, 2)), 1))
    along_x = select(stress_pad, (0, 3, 4))[:, :, 1:-1, 1:-1]
    along_y = select(stress_pad, (3, 1, 5))[:, 1:-1, :, 1:-1]
    along_z = pad_depth(select(stress, (4, 5, 2)))
    force = divergence(along_x, along_y, along_z)
    rhs = -advect(padded) + viscosity * laplace(padded) + force
    new_velocity = (velocity + time_step * rhs) / factor
    transport_a = jnp.stack(
        [
            jnp.sum(grad_x * velocity, axis=0),
            jnp.sum(grad_y * velocity, axis=0),
            jnp.sum(grad_z * velocity, axis=0),
        ]
    )
    transport_b = grad_x * velocity[0:1] + grad_y * velocity[1:2] + grad_z * velocity[2:3]
    stencil_grad = direct + transport_a + transport_b + viscosity * laplace(adj_pad)
    ghost = fold_across(fold_depth_side(column_grad, count_x, count_y, count_z))[..., 1:-1]
    widened = extended(ghost, ((GX, 1), (GY, 2)), 1)
    middle = widened[:, 2:-2]
    middle = middle.at[:, 0].add(widened[:, 0]).at[:, -1].add(widened[:, -1])
    folded = middle[:, :, 2:-2]
    folded = folded.at[:, :, 0].add(middle[:, :, 0]).at[:, :, -1].add(middle[:, :, -1])
    velocity_grad = stencil_grad + folded
    totals = unflatten(sum_everywhere(flatten(w_in_s, b_in_s, w_out_s, b_out_s)))
    blocks_total = columns.shape[1] * lax.axis_size(GX) * lax.axis_size(GY)
    scale = float(blocks_total) ** (-0.5)
    weight_in_grad = totals[0] * scale
    bias_in_grad = totals[1] * scale
    weight_out_grad = totals[2] * scale
    bias_out_grad = totals[3] * scale
    return (
        new_velocity,
        velocity_grad,
        weight_in_grad,
        bias_in_grad,
        weight_out_grad,
        bias_out_grad,
    )


def solution(mesh):
    mesh = Mesh(mesh.devices.reshape(4, 4, 4, 4, 2), GX + GY)
    placed = (
        P(None, GX, GY, None),
        P(GX, GY, None),
        P(),
        P(),
        P(),
        P(),
        P(None, GX, GY, None),
    )
    return jax.shard_map(
        on_device,
        mesh=mesh,
        in_specs=placed,
        out_specs=(P(None, GX, GY, None), P(None, GX, GY, None), P(), P(), P(), P()),
        check_vma=False,
    )
```

```python
import jax
import jax.numpy as jnp
import numpy as np
from jax import lax
from jax.experimental import pallas as pl
from jax.experimental.pallas import tpu as pltpu
from jax.sharding import Mesh, PartitionSpec as P

time_step = 0.25
viscosity = 0.2
penalty_eta = 0.05

GX = ("zh", "x", "y")
GY = ("zl", "core")
FLAT = 4352
HALF = FLAT // 2
WIN_ROWS = 648
WOUT_BASE = 4 * WIN_ROWS
BIAS_BASE = WOUT_BASE + 3 * 512
F32 = jnp.float32
BF16 = jnp.bfloat16


def selector():
    table = np.zeros((4, 128, 6, 4, 32), np.float32)
    for offset in range(6):
        for block in range(32):
            z = 4 * block + offset - 1
            if 0 <= z < 128:
                for row in range(4):
                    table[row, z, offset, row, block] = 1.0
    return table.reshape(512, 768).astype(jnp.bfloat16)


def z_next(field):
    lane = lax.broadcasted_iota(jnp.int32, field.shape, field.ndim - 1)
    return jnp.where(lane < 127, pltpu.roll(field, 127, field.ndim - 1), 0.0)


def z_before(field):
    lane = lax.broadcasted_iota(jnp.int32, field.shape, field.ndim - 1)
    return jnp.where(lane > 0, pltpu.roll(field, 1, field.ndim - 1), 0.0)


def split(value):
    high = value.astype(BF16)
    low = (value - high.astype(F32)).astype(BF16)
    return high, low


def dot(left, right, left_dim, right_dim):
    return lax.dot_general(
        left, right, (((left_dim,), (right_dim,)), ((), ())), preferred_element_type=F32
    )


def damping(canopy):
    return 1.0 + time_step * canopy.astype(F32) / penalty_eta


def start_kernel(v_ref, canopy_ref, cot_ref, direct_ref, m1_ref, m2_ref):
    core = lax.axis_index("core")
    factor = damping(canopy_ref[...])
    for i in range(3):
        direct_ref[i] = cot_ref[i].astype(F32) / factor
    for out, row in ((m1_ref, 15 * (1 - core)), (m2_ref, 15 * core)):
        for i in range(3):
            for x in range(4):
                out[pl.ds(i * 4 + x, 1), :] = v_ref[i, x, pl.ds(row, 1), :]
                out[pl.ds(12 + i * 4 + x, 1), :] = (
                    direct_ref[i, x, pl.ds(row, 1), :] * time_step
                )


def layer_kernel(v_ref, direct_ref, r1_ref, r2_ref, m1_ref, m2_ref):
    core = lax.axis_index("core")
    parity = lax.rem(lax.axis_index("y"), 2)
    for out, x in ((m1_ref, 3 * (1 - parity)), (m2_ref, 3 * parity)):
        for k in range(6):
            out[k, 16:24, :] = jnp.zeros((8, 128), F32)
            if k < 3:
                out[k, 1:17, :] = v_ref[k, x]
            else:
                out[k, 1:17, :] = direct_ref[k - 3, x] * time_step
            row1 = r1_ref[pl.ds(k * 4 + x, 1), :]
            row2 = r2_ref[pl.ds(k * 4 + x, 1), :]
            out[k, 0:1, :] = jnp.where(core == 0, row2, row1)
            out[k, 17:18, :] = jnp.where(core == 0, row1, row2)


def main_kernel(
    v_ref, direct_ref, r1_ref, r2_ref, x1_ref, x2_ref,
    win_ref, bin_ref, wout_ref, bout_ref, sel_ref,
    keep_ref, send_ref, nv_ref, vg_ref, m1_ref, m2_ref, ylow_ref, yhigh_ref,
    ext, sgrad, cols, rows, cgrad, cpad, opad, ghost, tau, flat,
):
    core = lax.axis_index("core")
    parity = lax.rem(lax.axis_index("y"), 2)

    for k in range(6):
        ext[k * 6] = jnp.where(parity == 0, x2_ref[k], x1_ref[k])
        ext[k * 6 + 5] = jnp.where(parity == 0, x1_ref[k], x2_ref[k])
        for x in range(4):
            spot = k * 6 + 1 + x
            ext[spot, 16:24, :] = jnp.zeros((8, 128), F32)
            ext[spot, 1:17, :] = v_ref[k, x] if k < 3 else direct_ref[k - 3, x] * time_step
            row1 = r1_ref[k * 4 + x : k * 4 + x + 1, :]
            row2 = r2_ref[k * 4 + x : k * 4 + x + 1, :]
            ext[spot, 0:1, :] = jnp.where(core == 0, row2, row1)
            ext[spot, 17:18, :] = jnp.where(core == 0, row1, row2)

    def at(k, dx, dy):
        return ext[k * 6 + 1 + dx : k * 6 + 5 + dx, 1 + dy : 17 + dy, :]

    def laplace(k):
        middle = at(k, 0, 0)
        total = at(k, 1, 0) + at(k, -1, 0) + at(k, 0, 1) + at(k, 0, -1)
        return total + z_next(middle) + z_before(middle) - 6.0 * middle

    grad_x = [(at(3 + i, 1, 0) - at(3 + i, -1, 0)) * 0.5 for i in range(3)]
    grad_y = [(at(3 + i, 0, 1) - at(3 + i, 0, -1)) * 0.5 for i in range(3)]
    grad_z = [(z_next(at(3 + i, 0, 0)) - z_before(at(3 + i, 0, 0))) * 0.5 for i in range(3)]
    stress_grad = (
        grad_x[0],
        grad_y[1],
        grad_z[2],
        grad_y[0] + grad_x[1],
        grad_z[0] + grad_x[2],
        grad_z[1] + grad_y[2],
    )
    sgrad[:, 16:24, :] = jnp.zeros((24, 8, 128), F32)
    for s in range(6):
        sgrad[s * 4 : s * 4 + 4, 0:16, :] = -stress_grad[s]
    for j in range(3):
        velocity = [at(i, 0, 0) for i in range(3)]
        slope = (grad_x, grad_y, grad_z)[j]
        total = direct_ref[j] + viscosity * laplace(3 + j)
        total = total + slope[0] * velocity[0] + slope[1] * velocity[1] + slope[2] * velocity[2]
        total = total + grad_x[j] * velocity[0] + grad_y[j] * velocity[1] + grad_z[j] * velocity[2]
        vg_ref[j] = total

    selection = sel_ref[...]
    inner = sel_ref[:, 128:640]

    parts = [sgrad[:, 4 * b : 4 * b + 8, :].reshape(192, 128) for b in range(4)]
    high, low = split(jnp.concatenate(parts, axis=1))
    picked = dot(high, inner, 1, 0) + dot(low, inner, 1, 0)
    for sa in range(24):
        for c in range(4):
            rows[pl.ds(sa * 16 + c, 4, stride=4), :] = picked[
                sa * 8 : sa * 8 + 4, c * 128 : c * 128 + 128
            ]
    rows_t = rows[...].T
    rows_low = rows_t.astype(BF16)
    bias_out_sum = jnp.sum(rows_t, axis=0, keepdims=True)

    parts = [
        ext[0:18, 4 * b : 4 * b + 8, :].reshape(144, 128).astype(BF16) for b in range(4)
    ]
    picked = dot(jnp.concatenate(parts, axis=1), selection, 1, 0)
    for g in range(18):
        for z in range(6):
            cols[pl.ds(g * 36 + z, 6, stride=6), :] = picked[
                g * 8 : g * 8 + 6, z * 128 : z * 128 + 128
            ]
    columns = cols[...].astype(BF16)

    pre_act = dot(columns, win_ref[...], 0, 0) + bin_ref[...]
    sigmoid_pre = jax.nn.sigmoid(pre_act)
    hidden = (pre_act * sigmoid_pre).astype(BF16)
    hidden_grad = dot(rows_low, wout_ref[...], 1, 1)
    pre_grad = hidden_grad * (sigmoid_pre * (1.0 + pre_act * (1.0 - sigmoid_pre)))
    pre_low = pre_grad.astype(BF16)
    bias_in_sum = jnp.sum(pre_grad, axis=0, keepdims=True)

    weight_in_sum = dot(columns, pre_low, 1, 0)
    for q in range(4):
        flat[q * WIN_ROWS : (q + 1) * WIN_ROWS, :] = weight_in_sum[:, q * 128 : q * 128 + 128]
    weight_out_sum = dot(hidden, rows_low, 0, 0)
    for q in range(3):
        flat[WOUT_BASE + q * 512 : WOUT_BASE + q * 512 + 512, :] = weight_out_sum[
            :, q * 128 : q * 128 + 128
        ]
    flat[BIAS_BASE:FLAT, :] = jnp.zeros((FLAT - BIAS_BASE, 128), F32)
    for q in range(4):
        flat[BIAS_BASE + q : BIAS_BASE + q + 1, :] = bias_in_sum[:, q * 128 : q * 128 + 128]
    for q in range(3):
        flat[BIAS_BASE + 4 + q : BIAS_BASE + 5 + q, :] = bias_out_sum[:, q * 128 : q * 128 + 128]
    keep_ref[...] = flat[pl.ds(pl.multiple_of(core * HALF, 8), HALF), :]
    send_ref[...] = flat[pl.ds(pl.multiple_of((1 - core) * HALF, 8), HALF), :]

    cgrad[...] = dot(win_ref[...], pre_low, 1, 1)
    for g in range(18):
        for z in range(6):
            cpad[g * 8 : g * 8 + 6, z * 128 : z * 128 + 128] = cgrad[
                pl.ds(g * 36 + z, 6, stride=6), :
            ]
            cpad[g * 8 + 6 : g * 8 + 8, z * 128 : z * 128 + 128] = jnp.zeros((2, 128), F32)
    high, low = split(cpad[...])
    spread = dot(high, selection, 1, 1) + dot(low, selection, 1, 1)
    spread = spread.reshape(18, 8, 512)
    ghost[...] = jnp.zeros((18, 24, 128), F32)
    for b in range(4):
        ghost[:, 4 * b : 4 * b + 8, :] += spread[:, :, b * 128 : b * 128 + 128]
    for j in range(3):
        vg_ref[j] += ghost[j * 6 + 1 : j * 6 + 5, 1:17, :]

    outputs = dot(hidden, wout_ref[...], 1, 0) + bout_ref[...]
    rows[...] = outputs.T
    for sa in range(24):
        for c in range(4):
            opad[sa * 8 : sa * 8 + 4, c * 128 : c * 128 + 128] = rows[
                pl.ds(sa * 16 + c, 4, stride=4), :
            ]
            opad[sa * 8 + 4 : sa * 8 + 8, c * 128 : c * 128 + 128] = jnp.zeros((4, 128), F32)
    high, low = split(opad[...])
    spread = dot(high, inner, 1, 1) + dot(low, inner, 1, 1)
    spread = spread.reshape(24, 8, 512)
    tau[:, 0:8, :] = jnp.zeros((24, 8, 128), F32)
    tau[:, 24:32, :] = jnp.zeros((24, 8, 128), F32)
    for b in range(4):
        tau[:, 8 + 4 * b : 12 + 4 * b, :] = spread[:, 0:4, b * 128 : b * 128 + 128]

    blank = jnp.zeros((1, 16, 128), F32)
    for i, (along_x, along_y, along_z) in enumerate(((0, 3, 4), (3, 1, 5), (4, 5, 2))):
        inside = tau[along_x * 4 : along_x * 4 + 4, 8:24, :]
        force = jnp.concatenate([inside[1:4], blank]) - jnp.concatenate([blank, inside[0:3]])
        force = force + tau[along_y * 4 : along_y * 4 + 4, 9:25, :]
        force = force - tau[along_y * 4 : along_y * 4 + 4, 7:23, :]
        inside = tau[along_z * 4 : along_z * 4 + 4, 8:24, :]
        force = (force + z_next(inside) - z_before(inside)) * 0.5
        product = at(2, 0, 0) * at(i, 0, 0)
        flow = at(0, 1, 0) * at(i, 1, 0) - at(0, -1, 0) * at(i, -1, 0)
        flow = flow + at(1, 0, 1) * at(i, 0, 1) - at(1, 0, -1) * at(i, 0, -1)
        flow = (flow + z_next(product) - z_before(product)) * 0.5
        nv_ref[i] = at(i, 0, 0) + time_step * (viscosity * laplace(i) - flow + force)

    for out, side in ((m1_ref, 1 - parity), (m2_ref, parity)):
        for j, s in enumerate((0, 3, 4)):
            out[j, 0:16, :] = tau[s * 4 + 3 * side, 8:24, :]
            out[j, 16:24, :] = jnp.zeros((8, 128), F32)
            out[3 + j] = ghost[j * 6 + 5 * side]
    for j, s in enumerate((3, 1, 5)):
        for x in range(4):
            spot = j * 4 + x
            ylow_ref[spot : spot + 1, :] = tau[s * 4 + x, 8:9, :]
            yhigh_ref[spot : spot + 1, :] = tau[s * 4 + x, 23:24, :]
            ylow_ref[12 + spot : 13 + spot, :] = ghost[j * 6 + 1 + x, 0:1, :]
            yhigh_ref[12 + spot : 13 + spot, :] = ghost[j * 6 + 1 + x, 17:18, :]


def side_kernel(x1_ref, x2_ref, ylow_ref, yhigh_ref, m1_ref, m2_ref, low, high):
    core = lax.axis_index("core")
    parity = lax.rem(lax.axis_index("y"), 2)
    low[...] = ylow_ref[...]
    high[...] = yhigh_ref[...]
    for j in range(3):
        from_low = jnp.where(parity == 0, x2_ref[3 + j], x1_ref[3 + j])
        from_high = jnp.where(parity == 0, x1_ref[3 + j], x2_ref[3 + j])
        first, last = 12 + j * 4, 15 + j * 4
        low[first : first + 1, :] += from_low[0:1]
        low[last : last + 1, :] += from_high[0:1]
        high[first : first + 1, :] += from_low[17:18]
        high[last : last + 1, :] += from_high[17:18]
    m1_ref[...] = jnp.where(core == 0, high[...], low[...])
    m2_ref[...] = jnp.where(core == 0, low[...], high[...])


def end_kernel(
    nv_ref, vg_ref, canopy_ref, x1_ref, x2_ref, y1_ref, y2_ref, new_ref, grad_ref, part
):
    core = lax.axis_index("core")
    parity = lax.rem(lax.axis_index("y"), 2)
    factor = damping(canopy_ref[...])
    y_low = jnp.where(core == 0, y2_ref[...], y1_ref[...])
    y_high = jnp.where(core == 0, y1_ref[...], y2_ref[...])
    step = time_step * 0.5
    for i in range(3):
        part[...] = nv_ref[i]
        part[0] -= step * jnp.where(parity == 0, x2_ref[i, 0:16, :], x1_ref[i, 0:16, :])
        part[3] += step * jnp.where(parity == 0, x1_ref[i, 0:16, :], x2_ref[i, 0:16, :])
        for x in range(4):
            spot = i * 4 + x
            part[x, 0:1, :] -= step * y_low[spot : spot + 1]
            part[x, 15:16, :] += step * y_high[spot : spot + 1]
        new_ref[i] = part[...] / factor
        part[...] = vg_ref[i]
        part[0] += jnp.where(parity == 0, x2_ref[3 + i, 1:17, :], x1_ref[3 + i, 1:17, :])
        part[3] += jnp.where(parity == 0, x1_ref[3 + i, 1:17, :], x2_ref[3 + i, 1:17, :])
        for x in range(4):
            spot = 12 + i * 4 + x
            part[x, 0:1, :] += y_low[spot : spot + 1]
            part[x, 15:16, :] += y_high[spot : spot + 1]
        grad_ref[i] = part[...]


def weights_kernel(scale, mine_ref, other_ref, win_ref, bin_ref, wout_ref, bout_ref):
    core = lax.axis_index("core")

    def put(out, lanes, start, count, first, second):
        done = 0
        while done < count:
            spot = start + done
            source, spot, room = (
                (first, spot, HALF - spot) if spot < HALF else (second, spot - HALF, count)
            )
            size = min(count - done, room)
            out[done : done + size, lanes * 128 : lanes * 128 + 128] = (
                source[spot : spot + size, :] * scale
            )
            done += size

    def write(first, second):
        for q in range(4):
            put(win_ref, q, q * WIN_ROWS, WIN_ROWS, first, second)
            put(bin_ref, q, BIAS_BASE + q, 1, first, second)
        for q in range(3):
            put(wout_ref, q, WOUT_BASE + q * 512, 512, first, second)
            put(bout_ref, q, BIAS_BASE + 4 + q, 1, first, second)

    @pl.when(core == 0)
    def _():
        write(mine_ref, other_ref)

    @pl.when(core == 1)
    def _():
        write(other_ref, mine_ref)


def call(kernel, outs, scratch=()):
    return pl.pallas_call(
        kernel,
        out_shape=[jax.ShapeDtypeStruct(shape, F32) for shape in outs],
        scratch_shapes=[pltpu.VMEM(shape, F32) for shape in scratch],
        compiler_params=pltpu.CompilerParams(vmem_limit_bytes=48 * 1024 * 1024),
    )


def pairs(axes):
    count = lax.axis_size(axes)
    inner = [(i, i ^ 1) for i in range(count)]
    outer = [(i, (i + 1) % count if i % 2 else (i - 1) % count) for i in range(count)]
    return inner, outer


def exchange(first, second, axes):
    inner, outer = pairs(axes)
    return lax.ppermute(first, axes, inner), lax.ppermute(second, axes, outer)


def sum_everywhere(keep, send):
    across, along = ("x", "y"), ("zh", "zl")
    swap = [(0, 1), (1, 0)]
    parts = lax.axis_size(across)
    depth = lax.axis_size(along)
    count = HALF // parts
    short = -(-count // depth)
    half = (keep + lax.ppermute(send, "core", swap)).reshape(parts, count, 128)
    part = jnp.sum(lax.all_to_all(half, across, 0, 0), axis=0)
    part = jnp.pad(part, ((0, short * depth - count), (0, 0))).reshape(depth, short, 128)
    piece = jnp.sum(lax.all_to_all(part, along, 0, 0), axis=0)
    part = lax.all_to_all(jnp.broadcast_to(piece, part.shape), along, 0, 0)
    part = part.reshape(short * depth, 128)[:count]
    half = lax.all_to_all(jnp.broadcast_to(part, half.shape), across, 0, 0)
    half = half.reshape(HALF, 128)
    return half, lax.ppermute(half, "core", swap)


def on_device(velocity, canopy, weight_in, bias_in, weight_out, bias_out, cotangent):
    field = (3, 4, 16, 128)
    rows = (24, 128)
    layers = (6, 24, 128)
    direct, m1, m2 = call(start_kernel, (field, rows, rows))(velocity, canopy, cotangent)
    y1, y2 = exchange(m1, m2, GY)
    m1, m2 = call(layer_kernel, (layers, layers))(velocity, direct, y1, y2)
    x1, x2 = exchange(m1, m2, GX)
    keep, send, nv, vg, m1, m2, ylow, yhigh = call(
        main_kernel,
        ((HALF, 128), (HALF, 128), field, field, layers, layers, rows, rows),
        (
            (36, 24, 128),
            (24, 24, 128),
            (648, 128),
            (384, 128),
            (648, 128),
            (144, 768),
            (192, 512),
            (18, 24, 128),
            (24, 32, 128),
            (FLAT, 128),
        ),
    )(
        velocity, direct, y1, y2, x1, x2,
        weight_in, bias_in[None], weight_out, bias_out[None], jnp.asarray(selector()),
    )
    x1, x2 = exchange(m1, m2, GX)
    m1, m2 = call(side_kernel, (rows, rows), (rows, rows))(x1, x2, ylow, yhigh)
    y1, y2 = exchange(m1, m2, GY)
    new_velocity, velocity_grad = call(end_kernel, (field, field), ((4, 16, 128),))(
        nv, vg, canopy, x1, x2, y1, y2
    )
    mine, other = sum_everywhere(keep, send)
    blocks = 128 * lax.axis_size(GX) * lax.axis_size(GY)
    scale = float(blocks) ** -0.5
    weight_in_grad, bias_in_grad, weight_out_grad, bias_out_grad = call(
        lambda *refs: weights_kernel(scale, *refs), ((648, 512), (1, 512), (512, 384), (1, 384))
    )(mine, other)
    return (
        new_velocity,
        velocity_grad,
        weight_in_grad,
        bias_in_grad[0],
        weight_out_grad,
        bias_out_grad[0],
    )


def solution(mesh):
    if mesh.devices.size == 512:
        mesh = Mesh(mesh.devices.reshape(4, 4, 4, 4, 2), GX + GY)
    placed = (
        P(None, GX, GY, None),
        P(GX, GY, None),
        P(),
        P(),
        P(),
        P(),
        P(None, GX, GY, None),
    )
    return jax.shard_map(
        on_device,
        mesh=mesh,
        in_specs=placed,
        out_specs=(P(None, GX, GY, None), P(None, GX, GY, None), P(), P(), P(), P()),
        check_vma=False,
    )
```

```python
import jax
import jax.numpy as jnp
import numpy as np
from jax import lax
from jax.experimental import pallas as pl
from jax.experimental.pallas import tpu as pltpu
from jax.sharding import Mesh, PartitionSpec as P

time_step = 0.25
viscosity = 0.2
penalty_eta = 0.05

GX = ("zh", "x", "y")
GY = ("zl", "core")
FLAT = 4352
HALF = FLAT // 2
WIN_ROWS = 648
WOUT_BASE = 4 * WIN_ROWS
BIAS_BASE = WOUT_BASE + 3 * 512
F32 = jnp.float32
BF16 = jnp.bfloat16


def selector():
    table = np.zeros((4, 128, 6, 4, 32), np.float32)
    for offset in range(6):
        for block in range(32):
            z = 4 * block + offset - 1
            if 0 <= z < 128:
                for row in range(4):
                    table[row, z, offset, row, block] = 1.0
    return table.reshape(512, 768).astype(jnp.bfloat16)


def z_next(field):
    lane = lax.broadcasted_iota(jnp.int32, field.shape, field.ndim - 1)
    return jnp.where(lane < 127, pltpu.roll(field, 127, field.ndim - 1), 0.0)


def z_before(field):
    lane = lax.broadcasted_iota(jnp.int32, field.shape, field.ndim - 1)
    return jnp.where(lane > 0, pltpu.roll(field, 1, field.ndim - 1), 0.0)


def split(value):
    high = value.astype(BF16)
    low = (value - high.astype(F32)).astype(BF16)
    return high, low


def dot(left, right, left_dim, right_dim):
    return lax.dot_general(
        left, right, (((left_dim,), (right_dim,)), ((), ())), preferred_element_type=F32
    )


def damping(canopy):
    return 1.0 + time_step * canopy.astype(F32) / penalty_eta


def start_kernel(v_ref, canopy_ref, cot_ref, direct_ref, factor_ref, m1_ref, m2_ref):
    core = lax.axis_index("core")
    factor = damping(canopy_ref[...])
    factor_ref[...] = factor
    for i in range(3):
        direct_ref[i] = cot_ref[i].astype(F32) / factor
    for out, row in ((m1_ref, 15 * (1 - core)), (m2_ref, 15 * core)):
        for i in range(3):
            for x in range(4):
                out[pl.ds(i * 4 + x, 1), :] = v_ref[i, x, pl.ds(row, 1), :]
                out[pl.ds(12 + i * 4 + x, 1), :] = (
                    direct_ref[i, x, pl.ds(row, 1), :] * time_step
                )


def weights_in_kernel(after, win_hbm, wout_hbm, sel_hbm, win_ref, wout_ref, sel_ref, sems):
    copies = [
        pltpu.make_async_copy(source, target, sems.at[i])
        for i, (source, target) in enumerate(
            ((win_hbm, win_ref), (wout_hbm, wout_ref), (sel_hbm, sel_ref))
        )
    ]
    for copy in copies:
        copy.start()
    for copy in copies:
        copy.wait()


def layer_kernel(v_ref, direct_ref, r1_ref, r2_ref, m1_ref, m2_ref):
    core = lax.axis_index("core")
    parity = lax.rem(lax.axis_index("y"), 2)
    for out, x in ((m1_ref, 3 * (1 - parity)), (m2_ref, 3 * parity)):
        for k in range(6):
            out[k, 16:24, :] = jnp.zeros((8, 128), F32)
            if k < 3:
                out[k, 1:17, :] = v_ref[k, x]
            else:
                out[k, 1:17, :] = direct_ref[k - 3, x] * time_step
            row1 = r1_ref[pl.ds(k * 4 + x, 1), :]
            row2 = r2_ref[pl.ds(k * 4 + x, 1), :]
            out[k, 0:1, :] = jnp.where(core == 0, row2, row1)
            out[k, 17:18, :] = jnp.where(core == 0, row1, row2)


def main_kernel(
    v_ref, direct_ref, r1_ref, r2_ref, x1_ref, x2_ref,
    win_ref, bin_ref, wout_ref, bout_ref, sel_ref,
    keep_ref, send_ref, nv_ref, vg_ref, m1_ref, m2_ref, ylow_ref, yhigh_ref,
    ext, sgrad, cols, rows, cgrad, cpad, opad, ghost, tau, flat,
):
    core = lax.axis_index("core")
    parity = lax.rem(lax.axis_index("y"), 2)

    for k in range(6):
        ext[k * 6] = jnp.where(parity == 0, x2_ref[k], x1_ref[k])
        ext[k * 6 + 5] = jnp.where(parity == 0, x1_ref[k], x2_ref[k])
        for x in range(4):
            spot = k * 6 + 1 + x
            ext[spot, 16:24, :] = jnp.zeros((8, 128), F32)
            ext[spot, 1:17, :] = v_ref[k, x] if k < 3 else direct_ref[k - 3, x] * time_step
            row1 = r1_ref[k * 4 + x : k * 4 + x + 1, :]
            row2 = r2_ref[k * 4 + x : k * 4 + x + 1, :]
            ext[spot, 0:1, :] = jnp.where(core == 0, row2, row1)
            ext[spot, 17:18, :] = jnp.where(core == 0, row1, row2)

    def at(k, dx, dy):
        return ext[k * 6 + 1 + dx : k * 6 + 5 + dx, 1 + dy : 17 + dy, :]

    def laplace(k):
        middle = at(k, 0, 0)
        total = at(k, 1, 0) + at(k, -1, 0) + at(k, 0, 1) + at(k, 0, -1)
        return total + z_next(middle) + z_before(middle) - 6.0 * middle

    grad_x = [(at(3 + i, 1, 0) - at(3 + i, -1, 0)) * 0.5 for i in range(3)]
    grad_y = [(at(3 + i, 0, 1) - at(3 + i, 0, -1)) * 0.5 for i in range(3)]
    grad_z = [(z_next(at(3 + i, 0, 0)) - z_before(at(3 + i, 0, 0))) * 0.5 for i in range(3)]
    stress_grad = (
        grad_x[0],
        grad_y[1],
        grad_z[2],
        grad_y[0] + grad_x[1],
        grad_z[0] + grad_x[2],
        grad_z[1] + grad_y[2],
    )
    sgrad[:, 16:24, :] = jnp.zeros((24, 8, 128), F32)
    for s in range(6):
        sgrad[s * 4 : s * 4 + 4, 0:16, :] = -stress_grad[s]
    for j in range(3):
        velocity = [at(i, 0, 0) for i in range(3)]
        slope = (grad_x, grad_y, grad_z)[j]
        total = direct_ref[j] + viscosity * laplace(3 + j)
        total = total + slope[0] * velocity[0] + slope[1] * velocity[1] + slope[2] * velocity[2]
        total = total + grad_x[j] * velocity[0] + grad_y[j] * velocity[1] + grad_z[j] * velocity[2]
        vg_ref[j] = total

    selection = sel_ref[...]
    inner = sel_ref[:, 128:640]

    parts = [sgrad[:, 4 * b : 4 * b + 8, :].reshape(192, 128) for b in range(4)]
    high, low = split(jnp.concatenate(parts, axis=1))
    picked = dot(high, inner, 1, 0) + dot(low, inner, 1, 0)
    for sa in range(24):
        for c in range(4):
            rows[pl.ds(sa * 16 + c, 4, stride=4), :] = picked[
                sa * 8 : sa * 8 + 4, c * 128 : c * 128 + 128
            ]
    rows_t = rows[...].T
    rows_low = rows_t.astype(BF16)
    bias_out_sum = jnp.sum(rows_t, axis=0, keepdims=True)

    parts = [
        ext[0:18, 4 * b : 4 * b + 8, :].reshape(144, 128).astype(BF16) for b in range(4)
    ]
    picked = dot(jnp.concatenate(parts, axis=1), selection, 1, 0)
    for g in range(18):
        for z in range(6):
            cols[pl.ds(g * 36 + z, 6, stride=6), :] = picked[
                g * 8 : g * 8 + 6, z * 128 : z * 128 + 128
            ]
    columns = cols[...].astype(BF16)

    pre_act = dot(columns, win_ref[...], 0, 0) + bin_ref[...]
    sigmoid_pre = jax.nn.sigmoid(pre_act)
    hidden = (pre_act * sigmoid_pre).astype(BF16)
    hidden_grad = dot(rows_low, wout_ref[...], 1, 1)
    pre_grad = hidden_grad * (sigmoid_pre * (1.0 + pre_act * (1.0 - sigmoid_pre)))
    pre_low = pre_grad.astype(BF16)
    bias_in_sum = jnp.sum(pre_grad, axis=0, keepdims=True)

    weight_in_sum = dot(columns, pre_low, 1, 0)
    for q in range(4):
        flat[q * WIN_ROWS : (q + 1) * WIN_ROWS, :] = weight_in_sum[:, q * 128 : q * 128 + 128]
    weight_out_sum = dot(hidden, rows_low, 0, 0)
    for q in range(3):
        flat[WOUT_BASE + q * 512 : WOUT_BASE + q * 512 + 512, :] = weight_out_sum[
            :, q * 128 : q * 128 + 128
        ]
    flat[BIAS_BASE:FLAT, :] = jnp.zeros((FLAT - BIAS_BASE, 128), F32)
    for q in range(4):
        flat[BIAS_BASE + q : BIAS_BASE + q + 1, :] = bias_in_sum[:, q * 128 : q * 128 + 128]
    for q in range(3):
        flat[BIAS_BASE + 4 + q : BIAS_BASE + 5 + q, :] = bias_out_sum[:, q * 128 : q * 128 + 128]
    keep_ref[...] = flat[pl.ds(pl.multiple_of(core * HALF, 8), HALF), :]
    send_ref[...] = flat[pl.ds(pl.multiple_of((1 - core) * HALF, 8), HALF), :]

    cgrad[...] = dot(win_ref[...], pre_low, 1, 1)
    for g in range(18):
        for z in range(6):
            cpad[g * 8 : g * 8 + 6, z * 128 : z * 128 + 128] = cgrad[
                pl.ds(g * 36 + z, 6, stride=6), :
            ]
            cpad[g * 8 + 6 : g * 8 + 8, z * 128 : z * 128 + 128] = jnp.zeros((2, 128), F32)
    high, low = split(cpad[...])
    spread = dot(high, selection, 1, 1) + dot(low, selection, 1, 1)
    spread = spread.reshape(18, 8, 512)
    ghost[...] = jnp.zeros((18, 24, 128), F32)
    for b in range(4):
        ghost[:, 4 * b : 4 * b + 8, :] += spread[:, :, b * 128 : b * 128 + 128]
    for j in range(3):
        vg_ref[j] += ghost[j * 6 + 1 : j * 6 + 5, 1:17, :]

    outputs = dot(hidden, wout_ref[...], 1, 0) + bout_ref[...]
    rows[...] = outputs.T
    for sa in range(24):
        for c in range(4):
            opad[sa * 8 : sa * 8 + 4, c * 128 : c * 128 + 128] = rows[
                pl.ds(sa * 16 + c, 4, stride=4), :
            ]
            opad[sa * 8 + 4 : sa * 8 + 8, c * 128 : c * 128 + 128] = jnp.zeros((4, 128), F32)
    high, low = split(opad[...])
    spread = dot(high, inner, 1, 1) + dot(low, inner, 1, 1)
    spread = spread.reshape(24, 8, 512)
    tau[:, 0:8, :] = jnp.zeros((24, 8, 128), F32)
    tau[:, 24:32, :] = jnp.zeros((24, 8, 128), F32)
    for b in range(4):
        tau[:, 8 + 4 * b : 12 + 4 * b, :] = spread[:, 0:4, b * 128 : b * 128 + 128]

    blank = jnp.zeros((1, 16, 128), F32)
    for i, (along_x, along_y, along_z) in enumerate(((0, 3, 4), (3, 1, 5), (4, 5, 2))):
        inside = tau[along_x * 4 : along_x * 4 + 4, 8:24, :]
        force = jnp.concatenate([inside[1:4], blank]) - jnp.concatenate([blank, inside[0:3]])
        force = force + tau[along_y * 4 : along_y * 4 + 4, 9:25, :]
        force = force - tau[along_y * 4 : along_y * 4 + 4, 7:23, :]
        inside = tau[along_z * 4 : along_z * 4 + 4, 8:24, :]
        force = (force + z_next(inside) - z_before(inside)) * 0.5
        product = at(2, 0, 0) * at(i, 0, 0)
        flow = at(0, 1, 0) * at(i, 1, 0) - at(0, -1, 0) * at(i, -1, 0)
        flow = flow + at(1, 0, 1) * at(i, 0, 1) - at(1, 0, -1) * at(i, 0, -1)
        flow = (flow + z_next(product) - z_before(product)) * 0.5
        nv_ref[i] = at(i, 0, 0) + time_step * (viscosity * laplace(i) - flow + force)

    for out, side in ((m1_ref, 1 - parity), (m2_ref, parity)):
        for j, s in enumerate((0, 3, 4)):
            out[j, 0:16, :] = tau[s * 4 + 3 * side, 8:24, :]
            out[j, 16:24, :] = jnp.zeros((8, 128), F32)
            out[3 + j] = ghost[j * 6 + 5 * side]
    for j, s in enumerate((3, 1, 5)):
        for x in range(4):
            spot = j * 4 + x
            ylow_ref[spot : spot + 1, :] = tau[s * 4 + x, 8:9, :]
            yhigh_ref[spot : spot + 1, :] = tau[s * 4 + x, 23:24, :]
            ylow_ref[12 + spot : 13 + spot, :] = ghost[j * 6 + 1 + x, 0:1, :]
            yhigh_ref[12 + spot : 13 + spot, :] = ghost[j * 6 + 1 + x, 17:18, :]


def side_kernel(x1_ref, x2_ref, ylow_ref, yhigh_ref, m1_ref, m2_ref, low, high):
    core = lax.axis_index("core")
    parity = lax.rem(lax.axis_index("y"), 2)
    low[...] = ylow_ref[...]
    high[...] = yhigh_ref[...]
    for j in range(3):
        from_low = jnp.where(parity == 0, x2_ref[3 + j], x1_ref[3 + j])
        from_high = jnp.where(parity == 0, x1_ref[3 + j], x2_ref[3 + j])
        first, last = 12 + j * 4, 15 + j * 4
        low[first : first + 1, :] += from_low[0:1]
        low[last : last + 1, :] += from_high[0:1]
        high[first : first + 1, :] += from_low[17:18]
        high[last : last + 1, :] += from_high[17:18]
    m1_ref[...] = jnp.where(core == 0, high[...], low[...])
    m2_ref[...] = jnp.where(core == 0, low[...], high[...])


def end_kernel(
    nv_ref, vg_ref, factor_ref, x1_ref, x2_ref, y1_ref, y2_ref, new_ref, grad_ref, done_ref, part
):
    core = lax.axis_index("core")
    parity = lax.rem(lax.axis_index("y"), 2)
    factor = factor_ref[...]
    y_low = jnp.where(core == 0, y2_ref[...], y1_ref[...])
    y_high = jnp.where(core == 0, y1_ref[...], y2_ref[...])
    step = time_step * 0.5
    for i in range(3):
        part[...] = nv_ref[i]
        part[0] -= step * jnp.where(parity == 0, x2_ref[i, 0:16, :], x1_ref[i, 0:16, :])
        part[3] += step * jnp.where(parity == 0, x1_ref[i, 0:16, :], x2_ref[i, 0:16, :])
        for x in range(4):
            spot = i * 4 + x
            part[x, 0:1, :] -= step * y_low[spot : spot + 1]
            part[x, 15:16, :] += step * y_high[spot : spot + 1]
        new_ref[i] = part[...] / factor
        part[...] = vg_ref[i]
        part[0] += jnp.where(parity == 0, x2_ref[3 + i, 1:17, :], x1_ref[3 + i, 1:17, :])
        part[3] += jnp.where(parity == 0, x1_ref[3 + i, 1:17, :], x2_ref[3 + i, 1:17, :])
        for x in range(4):
            spot = 12 + i * 4 + x
            part[x, 0:1, :] += y_low[spot : spot + 1]
            part[x, 15:16, :] += y_high[spot : spot + 1]
        grad_ref[i] = part[...]
    done_ref[...] = y_low[0:8]


def weights_kernel(scale, mine_ref, other_ref, win_ref, bin_ref, wout_ref, bout_ref):
    core = lax.axis_index("core")

    def put(out, lanes, start, count, first, second):
        done = 0
        while done < count:
            spot = start + done
            source, spot, room = (
                (first, spot, HALF - spot) if spot < HALF else (second, spot - HALF, count)
            )
            size = min(count - done, room)
            out[done : done + size, lanes * 128 : lanes * 128 + 128] = (
                source[spot : spot + size, :] * scale
            )
            done += size

    def write(first, second):
        for q in range(4):
            put(win_ref, q, q * WIN_ROWS, WIN_ROWS, first, second)
            put(bin_ref, q, BIAS_BASE + q, 1, first, second)
        for q in range(3):
            put(wout_ref, q, WOUT_BASE + q * 512, 512, first, second)
            put(bout_ref, q, BIAS_BASE + 4 + q, 1, first, second)

    @pl.when(core == 0)
    def _():
        write(mine_ref, other_ref)

    @pl.when(core == 1)
    def _():
        write(other_ref, mine_ref)


def across_kernel(got_ref, *rest):
    out_ref, part = rest[-2:]
    count = got_ref.shape[1]
    depth, _, width = out_ref.shape
    short = width // 128
    part[...] = jnp.zeros(part.shape, F32)
    part[0:count, :] = jnp.sum(got_ref[...], axis=0)
    for i in range(depth):
        for j in range(short):
            out_ref[i, 0:1, j * 128 : j * 128 + 128] = part[i * short + j : i * short + j + 1, :]


def along_kernel(got_ref, *rest):
    out_ref = rest[-1]
    total = jnp.sum(got_ref[...], axis=0, keepdims=True)
    out_ref[...] = jnp.broadcast_to(total, out_ref.shape)


def spread_kernel(got_ref, *rest):
    out_ref, part = rest[-2:]
    depth, _, width = got_ref.shape
    short = width // 128
    count = out_ref.shape[1]
    for i in range(depth):
        for j in range(short):
            part[i * short + j : i * short + j + 1, :] = got_ref[i, 0:1, j * 128 : j * 128 + 128]
    for i in range(out_ref.shape[0]):
        out_ref[i] = part[0:count, :]


def call(kernel, outs, scratch=(), places=None):
    spaces = {"v": pltpu.VMEM, "h": pltpu.HBM, "a": pl.ANY}
    specs = {}
    if places is not None:
        specs["in_specs"] = [pl.BlockSpec(memory_space=spaces[place]) for place in places]
    return pl.pallas_call(
        kernel,
        out_shape=[
            out if hasattr(out, "dtype") else jax.ShapeDtypeStruct(out, F32) for out in outs
        ],
        scratch_shapes=[
            pltpu.VMEM(shape, F32) if isinstance(shape, tuple) else shape for shape in scratch
        ],
        compiler_params=pltpu.CompilerParams(vmem_limit_bytes=48 * 1024 * 1024),
        **specs,
    )


def pairs(axes):
    count = lax.axis_size(axes)
    inner = [(i, i ^ 1) for i in range(count)]
    outer = [(i, (i + 1) % count if i % 2 else (i - 1) % count) for i in range(count)]
    return inner, outer


def exchange(first, second, axes):
    inner, outer = pairs(axes)
    return lax.ppermute(first, axes, inner), lax.ppermute(second, axes, outer)


def on_device(velocity, canopy, weight_in, bias_in, weight_out, bias_out, cotangent):
    field = (3, 4, 16, 128)
    rows = (24, 128)
    layers = (6, 24, 128)
    across, along = ("x", "y"), ("zh", "zl")
    swap = [(0, 1), (1, 0)]
    parts = lax.axis_size(across)
    depth = lax.axis_size(along)
    count = HALF // parts
    short = -(-count // depth)

    direct, factor, m1, m2 = call(start_kernel, (field, field[1:], rows, rows))(
        velocity, canopy, cotangent
    )
    y1, y2 = exchange(m1, m2, GY)
    m1, m2 = call(layer_kernel, (layers, layers))(velocity, direct, y1, y2)
    x1, x2 = exchange(m1, m2, GX)
    selection = jnp.asarray(selector())
    weight_in, weight_out, selection = call(
        weights_in_kernel,
        (weight_in, weight_out, selection),
        (pltpu.SemaphoreType.DMA((3,)),),
        "ahhh",
    )(m1, weight_in, weight_out, selection)
    keep, send, nv, vg, m1, m2, ylow, yhigh = call(
        main_kernel,
        ((HALF, 128), (HALF, 128), field, field, layers, layers, rows, rows),
        (
            (36, 24, 128),
            (24, 24, 128),
            (648, 128),
            (384, 128),
            (648, 128),
            (144, 768),
            (192, 512),
            (18, 24, 128),
            (24, 32, 128),
            (FLAT, 128),
        ),
    )(
        velocity, direct, y1, y2, x1, x2,
        weight_in, bias_in[None], weight_out, bias_out[None], selection,
    )

    half = (keep + lax.ppermute(send, "core", swap)).reshape(parts, count, 128)
    got = lax.all_to_all(half, across, 0, 0)
    x1, x2 = exchange(m1, m2, GX)
    m1, m2 = call(side_kernel, (rows, rows), (rows, rows))(x1, x2, ylow, yhigh)
    cut = (depth, 1, short * 128)
    (part,) = call(across_kernel, (cut,), ((short * depth, 128),), "vaa")(got, x1, x2)
    got = lax.all_to_all(part, along, 0, 0)
    y1, y2 = exchange(m1, m2, GY)
    (part,) = call(along_kernel, (cut,), (), "vaa")(got, y1, y2)
    got = lax.all_to_all(part, along, 0, 0)
    new_velocity, velocity_grad, done = call(
        end_kernel, (field, field, (8, 128)), ((4, 16, 128),)
    )(
        nv, vg, factor, x1, x2, y1, y2
    )
    (half,) = call(spread_kernel, (half.shape,), ((short * depth, 128),), "va")(got, done)
    mine = lax.all_to_all(half, across, 0, 0).reshape(HALF, 128)
    other = lax.ppermute(mine, "core", swap)
    blocks = 128 * lax.axis_size(GX) * lax.axis_size(GY)
    scale = float(blocks) ** -0.5
    weight_in_grad, bias_in_grad, weight_out_grad, bias_out_grad = call(
        lambda *refs: weights_kernel(scale, *refs), ((648, 512), (1, 512), (512, 384), (1, 384))
    )(mine, other)
    return (
        new_velocity,
        velocity_grad,
        weight_in_grad,
        bias_in_grad[0],
        weight_out_grad,
        bias_out_grad[0],
    )


def solution(mesh):
    if mesh.devices.size == 512:
        mesh = Mesh(mesh.devices.reshape(4, 4, 4, 4, 2), GX + GY)
    placed = (
        P(None, GX, GY, None),
        P(GX, GY, None),
        P(),
        P(),
        P(),
        P(),
        P(None, GX, GY, None),
    )
    return jax.shard_map(
        on_device,
        mesh=mesh,
        in_specs=placed,
        out_specs=(P(None, GX, GY, None), P(None, GX, GY, None), P(), P(), P(), P()),
        check_vma=False,
    )
```

```python
import jax
import jax.numpy as jnp
import numpy as np
from jax import lax
from jax.experimental import pallas as pl
from jax.experimental.pallas import tpu as pltpu
from jax.sharding import Mesh, PartitionSpec as P

time_step = 0.25
viscosity = 0.2
penalty_eta = 0.05

GX = ("zh", "x", "y")
GY = ("zl", "core")
FLAT = 4352
HALF = FLAT // 2
WIN_ROWS = 648
WOUT_BASE = 4 * WIN_ROWS
BIAS_BASE = WOUT_BASE + 3 * 512
F32 = jnp.float32
BF16 = jnp.bfloat16


def selector():
    table = np.zeros((4, 128, 6, 4, 32), np.float32)
    for offset in range(6):
        for block in range(32):
            z = 4 * block + offset - 1
            if 0 <= z < 128:
                for row in range(4):
                    table[row, z, offset, row, block] = 1.0
    return table.reshape(512, 768).astype(jnp.bfloat16)


def z_next(field):
    lane = lax.broadcasted_iota(jnp.int32, field.shape, field.ndim - 1)
    return jnp.where(lane < 127, pltpu.roll(field, 127, field.ndim - 1), 0.0)


def z_before(field):
    lane = lax.broadcasted_iota(jnp.int32, field.shape, field.ndim - 1)
    return jnp.where(lane > 0, pltpu.roll(field, 1, field.ndim - 1), 0.0)


def split(value):
    high = value.astype(BF16)
    low = (value - high.astype(F32)).astype(BF16)
    return high, low


def dot(left, right, left_dim, right_dim):
    return lax.dot_general(
        left, right, (((left_dim,), (right_dim,)), ((), ())), preferred_element_type=F32
    )


def damping(canopy):
    return 1.0 + time_step * canopy.astype(F32) / penalty_eta


def start_kernel(v_ref, canopy_ref, cot_ref, direct_ref, factor_ref, m1_ref, m2_ref):
    core = lax.axis_index("core")
    factor = damping(canopy_ref[...])
    factor_ref[...] = factor
    for i in range(3):
        direct_ref[i] = cot_ref[i].astype(F32) / factor
    for out, row in ((m1_ref, 15 * (1 - core)), (m2_ref, 15 * core)):
        for i in range(3):
            for x in range(4):
                out[pl.ds(i * 4 + x, 1), :] = v_ref[i, x, pl.ds(row, 1), :]
                out[pl.ds(12 + i * 4 + x, 1), :] = (
                    direct_ref[i, x, pl.ds(row, 1), :] * time_step
                )


def weights_in_kernel(after, win_hbm, wout_hbm, sel_hbm, win_ref, wout_ref, sel_ref, sems):
    copies = [
        pltpu.make_async_copy(source, target, sems.at[i])
        for i, (source, target) in enumerate(
            ((win_hbm, win_ref), (wout_hbm, wout_ref), (sel_hbm, sel_ref))
        )
    ]
    for copy in copies:
        copy.start()
    for copy in copies:
        copy.wait()


def layer_kernel(v_ref, direct_ref, r1_ref, r2_ref, m1_ref, m2_ref):
    core = lax.axis_index("core")
    parity = lax.rem(lax.axis_index("y"), 2)
    for out, x in ((m1_ref, 3 * (1 - parity)), (m2_ref, 3 * parity)):
        for k in range(6):
            out[k, 16:24, :] = jnp.zeros((8, 128), F32)
            if k < 3:
                out[k, 1:17, :] = v_ref[k, x]
            else:
                out[k, 1:17, :] = direct_ref[k - 3, x] * time_step
            row1 = r1_ref[pl.ds(k * 4 + x, 1), :]
            row2 = r2_ref[pl.ds(k * 4 + x, 1), :]
            out[k, 0:1, :] = jnp.where(core == 0, row2, row1)
            out[k, 17:18, :] = jnp.where(core == 0, row1, row2)


def main_kernel(
    v_ref, direct_ref, r1_ref, r2_ref, x1_ref, x2_ref,
    win_ref, bin_ref, wout_ref, bout_ref, sel_ref,
    keep_ref, send_ref, nv_ref, vg_ref, m1_ref, m2_ref, ylow_ref, yhigh_ref,
    ext, sgrad, cols, rows, cgrad, cpad, opad, ghost, tau, flat,
):
    core = lax.axis_index("core")
    parity = lax.rem(lax.axis_index("y"), 2)

    for k in range(6):
        ext[k * 6] = jnp.where(parity == 0, x2_ref[k], x1_ref[k])
        ext[k * 6 + 5] = jnp.where(parity == 0, x1_ref[k], x2_ref[k])
        for x in range(4):
            spot = k * 6 + 1 + x
            ext[spot, 16:24, :] = jnp.zeros((8, 128), F32)
            ext[spot, 1:17, :] = v_ref[k, x] if k < 3 else direct_ref[k - 3, x] * time_step
            row1 = r1_ref[k * 4 + x : k * 4 + x + 1, :]
            row2 = r2_ref[k * 4 + x : k * 4 + x + 1, :]
            ext[spot, 0:1, :] = jnp.where(core == 0, row2, row1)
            ext[spot, 17:18, :] = jnp.where(core == 0, row1, row2)

    def at(k, dx, dy):
        return ext[k * 6 + 1 + dx : k * 6 + 5 + dx, 1 + dy : 17 + dy, :]

    def laplace(k):
        middle = at(k, 0, 0)
        total = at(k, 1, 0) + at(k, -1, 0) + at(k, 0, 1) + at(k, 0, -1)
        return total + z_next(middle) + z_before(middle) - 6.0 * middle

    grad_x = [(at(3 + i, 1, 0) - at(3 + i, -1, 0)) * 0.5 for i in range(3)]
    grad_y = [(at(3 + i, 0, 1) - at(3 + i, 0, -1)) * 0.5 for i in range(3)]
    grad_z = [(z_next(at(3 + i, 0, 0)) - z_before(at(3 + i, 0, 0))) * 0.5 for i in range(3)]
    stress_grad = (
        grad_x[0],
        grad_y[1],
        grad_z[2],
        grad_y[0] + grad_x[1],
        grad_z[0] + grad_x[2],
        grad_z[1] + grad_y[2],
    )
    sgrad[:, 16:24, :] = jnp.zeros((24, 8, 128), F32)
    for s in range(6):
        sgrad[s * 4 : s * 4 + 4, 0:16, :] = -stress_grad[s]
    for j in range(3):
        velocity = [at(i, 0, 0) for i in range(3)]
        slope = (grad_x, grad_y, grad_z)[j]
        total = direct_ref[j] + viscosity * laplace(3 + j)
        total = total + slope[0] * velocity[0] + slope[1] * velocity[1] + slope[2] * velocity[2]
        total = total + grad_x[j] * velocity[0] + grad_y[j] * velocity[1] + grad_z[j] * velocity[2]
        vg_ref[j] = total

    selection = sel_ref[...]
    inner = sel_ref[:, 128:640]

    parts = [sgrad[:, 4 * b : 4 * b + 8, :].reshape(192, 128) for b in range(4)]
    high, low = split(jnp.concatenate(parts, axis=1))
    picked = dot(high, inner, 1, 0) + dot(low, inner, 1, 0)
    for sa in range(24):
        for c in range(4):
            rows[pl.ds(sa * 16 + c, 4, stride=4), :] = picked[
                sa * 8 : sa * 8 + 4, c * 128 : c * 128 + 128
            ]
    rows_t = rows[...].T
    rows_low = rows_t.astype(BF16)
    bias_out_sum = jnp.sum(rows_t, axis=0, keepdims=True)

    parts = [
        ext[0:18, 4 * b : 4 * b + 8, :].reshape(144, 128).astype(BF16) for b in range(4)
    ]
    picked = dot(jnp.concatenate(parts, axis=1), selection, 1, 0)
    for g in range(18):
        for z in range(6):
            cols[pl.ds(g * 36 + z, 6, stride=6), :] = picked[
                g * 8 : g * 8 + 6, z * 128 : z * 128 + 128
            ]
    columns = cols[...].astype(BF16)

    pre_act = dot(columns, win_ref[...], 0, 0) + bin_ref[...]
    sigmoid_pre = jax.nn.sigmoid(pre_act)
    hidden = (pre_act * sigmoid_pre).astype(BF16)
    hidden_grad = dot(rows_low, wout_ref[...], 1, 1)
    pre_grad = hidden_grad * (sigmoid_pre * (1.0 + pre_act * (1.0 - sigmoid_pre)))
    pre_low = pre_grad.astype(BF16)
    bias_in_sum = jnp.sum(pre_grad, axis=0, keepdims=True)

    weight_in_sum = dot(columns, pre_low, 1, 0)
    for q in range(4):
        flat[q * WIN_ROWS : (q + 1) * WIN_ROWS, :] = weight_in_sum[:, q * 128 : q * 128 + 128]
    weight_out_sum = dot(hidden, rows_low, 0, 0)
    for q in range(3):
        flat[WOUT_BASE + q * 512 : WOUT_BASE + q * 512 + 512, :] = weight_out_sum[
            :, q * 128 : q * 128 + 128
        ]
    flat[BIAS_BASE:FLAT, :] = jnp.zeros((FLAT - BIAS_BASE, 128), F32)
    for q in range(4):
        flat[BIAS_BASE + q : BIAS_BASE + q + 1, :] = bias_in_sum[:, q * 128 : q * 128 + 128]
    for q in range(3):
        flat[BIAS_BASE + 4 + q : BIAS_BASE + 5 + q, :] = bias_out_sum[:, q * 128 : q * 128 + 128]
    keep_ref[...] = flat[pl.ds(pl.multiple_of(core * HALF, 8), HALF), :]
    send_ref[...] = flat[pl.ds(pl.multiple_of((1 - core) * HALF, 8), HALF), :]

    cgrad[...] = dot(win_ref[...], pre_low, 1, 1)
    for g in range(18):
        for z in range(6):
            cpad[g * 8 : g * 8 + 6, z * 128 : z * 128 + 128] = cgrad[
                pl.ds(g * 36 + z, 6, stride=6), :
            ]
            cpad[g * 8 + 6 : g * 8 + 8, z * 128 : z * 128 + 128] = jnp.zeros((2, 128), F32)
    high, low = split(cpad[...])
    spread = dot(high, selection, 1, 1) + dot(low, selection, 1, 1)
    spread = spread.reshape(18, 8, 512)
    ghost[...] = jnp.zeros((18, 24, 128), F32)
    for b in range(4):
        ghost[:, 4 * b : 4 * b + 8, :] += spread[:, :, b * 128 : b * 128 + 128]
    for j in range(3):
        vg_ref[j] += ghost[j * 6 + 1 : j * 6 + 5, 1:17, :]

    outputs = dot(hidden, wout_ref[...], 1, 0) + bout_ref[...]
    rows[...] = outputs.T
    for sa in range(24):
        for c in range(4):
            opad[sa * 8 : sa * 8 + 4, c * 128 : c * 128 + 128] = rows[
                pl.ds(sa * 16 + c, 4, stride=4), :
            ]
            opad[sa * 8 + 4 : sa * 8 + 8, c * 128 : c * 128 + 128] = jnp.zeros((4, 128), F32)
    high, low = split(opad[...])
    spread = dot(high, inner, 1, 1) + dot(low, inner, 1, 1)
    spread = spread.reshape(24, 8, 512)
    tau[:, 0:8, :] = jnp.zeros((24, 8, 128), F32)
    tau[:, 24:32, :] = jnp.zeros((24, 8, 128), F32)
    for b in range(4):
        tau[:, 8 + 4 * b : 12 + 4 * b, :] = spread[:, 0:4, b * 128 : b * 128 + 128]

    blank = jnp.zeros((1, 16, 128), F32)
    for i, (along_x, along_y, along_z) in enumerate(((0, 3, 4), (3, 1, 5), (4, 5, 2))):
        inside = tau[along_x * 4 : along_x * 4 + 4, 8:24, :]
        force = jnp.concatenate([inside[1:4], blank]) - jnp.concatenate([blank, inside[0:3]])
        force = force + tau[along_y * 4 : along_y * 4 + 4, 9:25, :]
        force = force - tau[along_y * 4 : along_y * 4 + 4, 7:23, :]
        inside = tau[along_z * 4 : along_z * 4 + 4, 8:24, :]
        force = (force + z_next(inside) - z_before(inside)) * 0.5
        product = at(2, 0, 0) * at(i, 0, 0)
        flow = at(0, 1, 0) * at(i, 1, 0) - at(0, -1, 0) * at(i, -1, 0)
        flow = flow + at(1, 0, 1) * at(i, 0, 1) - at(1, 0, -1) * at(i, 0, -1)
        flow = (flow + z_next(product) - z_before(product)) * 0.5
        nv_ref[i] = at(i, 0, 0) + time_step * (viscosity * laplace(i) - flow + force)

    for out, side in ((m1_ref, 1 - parity), (m2_ref, parity)):
        for j, s in enumerate((0, 3, 4)):
            out[j, 0:16, :] = tau[s * 4 + 3 * side, 8:24, :]
            out[j, 16:24, :] = jnp.zeros((8, 128), F32)
            out[3 + j] = ghost[j * 6 + 5 * side]
    for j, s in enumerate((3, 1, 5)):
        for x in range(4):
            spot = j * 4 + x
            ylow_ref[spot : spot + 1, :] = tau[s * 4 + x, 8:9, :]
            yhigh_ref[spot : spot + 1, :] = tau[s * 4 + x, 23:24, :]
            ylow_ref[12 + spot : 13 + spot, :] = ghost[j * 6 + 1 + x, 0:1, :]
            yhigh_ref[12 + spot : 13 + spot, :] = ghost[j * 6 + 1 + x, 17:18, :]


def side_kernel(x1_ref, x2_ref, ylow_ref, yhigh_ref, m1_ref, m2_ref, low, high):
    core = lax.axis_index("core")
    parity = lax.rem(lax.axis_index("y"), 2)
    low[...] = ylow_ref[...]
    high[...] = yhigh_ref[...]
    for j in range(3):
        from_low = jnp.where(parity == 0, x2_ref[3 + j], x1_ref[3 + j])
        from_high = jnp.where(parity == 0, x1_ref[3 + j], x2_ref[3 + j])
        first, last = 12 + j * 4, 15 + j * 4
        low[first : first + 1, :] += from_low[0:1]
        low[last : last + 1, :] += from_high[0:1]
        high[first : first + 1, :] += from_low[17:18]
        high[last : last + 1, :] += from_high[17:18]
    m1_ref[...] = jnp.where(core == 0, high[...], low[...])
    m2_ref[...] = jnp.where(core == 0, low[...], high[...])


def end_kernel(
    nv_ref, vg_ref, factor_ref, x1_ref, x2_ref, y1_ref, y2_ref, new_ref, grad_ref, done_ref, part
):
    core = lax.axis_index("core")
    parity = lax.rem(lax.axis_index("y"), 2)
    factor = factor_ref[...]
    y_low = jnp.where(core == 0, y2_ref[...], y1_ref[...])
    y_high = jnp.where(core == 0, y1_ref[...], y2_ref[...])
    step = time_step * 0.5
    for i in range(3):
        part[...] = nv_ref[i]
        part[0] -= step * jnp.where(parity == 0, x2_ref[i, 0:16, :], x1_ref[i, 0:16, :])
        part[3] += step * jnp.where(parity == 0, x1_ref[i, 0:16, :], x2_ref[i, 0:16, :])
        for x in range(4):
            spot = i * 4 + x
            part[x, 0:1, :] -= step * y_low[spot : spot + 1]
            part[x, 15:16, :] += step * y_high[spot : spot + 1]
        new_ref[i] = part[...] / factor
        part[...] = vg_ref[i]
        part[0] += jnp.where(parity == 0, x2_ref[3 + i, 1:17, :], x1_ref[3 + i, 1:17, :])
        part[3] += jnp.where(parity == 0, x1_ref[3 + i, 1:17, :], x2_ref[3 + i, 1:17, :])
        for x in range(4):
            spot = 12 + i * 4 + x
            part[x, 0:1, :] += y_low[spot : spot + 1]
            part[x, 15:16, :] += y_high[spot : spot + 1]
        grad_ref[i] = part[...]
    done_ref[...] = y_low[0:8]


def weights_kernel(scale, mine_ref, other_ref, win_ref, bin_ref, wout_ref, bout_ref):
    core = lax.axis_index("core")

    def put(out, lanes, start, count, first, second):
        done = 0
        while done < count:
            spot = start + done
            source, spot, room = (
                (first, spot, HALF - spot) if spot < HALF else (second, spot - HALF, count)
            )
            size = min(count - done, room)
            out[done : done + size, lanes * 128 : lanes * 128 + 128] = (
                source[spot : spot + size, :] * scale
            )
            done += size

    def write(first, second):
        for q in range(4):
            put(win_ref, q, q * WIN_ROWS, WIN_ROWS, first, second)
            put(bin_ref, q, BIAS_BASE + q, 1, first, second)
        for q in range(3):
            put(wout_ref, q, WOUT_BASE + q * 512, 512, first, second)
            put(bout_ref, q, BIAS_BASE + 4 + q, 1, first, second)

    @pl.when(core == 0)
    def _():
        write(mine_ref, other_ref)

    @pl.when(core == 1)
    def _():
        write(other_ref, mine_ref)


def across_kernel(got_ref, *rest):
    out_ref, part = rest[-2:]
    count = got_ref.shape[1]
    depth, _, width = out_ref.shape
    short = width // 128
    part[...] = jnp.zeros(part.shape, F32)
    part[0:count, :] = jnp.sum(got_ref[...], axis=0)
    for i in range(depth):
        for j in range(short):
            out_ref[i, 0:1, j * 128 : j * 128 + 128] = part[i * short + j : i * short + j + 1, :]


def along_kernel(got_ref, *rest):
    out_ref = rest[-1]
    total = jnp.sum(got_ref[...], axis=0, keepdims=True)
    out_ref[...] = jnp.broadcast_to(total, out_ref.shape)


def spread_kernel(got_ref, *rest):
    out_ref, part = rest[-2:]
    depth, _, width = got_ref.shape
    short = width // 128
    count = out_ref.shape[1]
    for i in range(depth):
        for j in range(short):
            part[i * short + j : i * short + j + 1, :] = got_ref[i, 0:1, j * 128 : j * 128 + 128]
    for i in range(out_ref.shape[0]):
        out_ref[i] = part[0:count, :]


def call(kernel, outs, scratch=(), places=None, room=48):
    spaces = {"v": pltpu.VMEM, "h": pltpu.HBM, "a": pl.ANY}
    specs = {}
    if places is not None:
        specs["in_specs"] = [pl.BlockSpec(memory_space=spaces[place]) for place in places]
    return pl.pallas_call(
        kernel,
        out_shape=[
            out if hasattr(out, "dtype") else jax.ShapeDtypeStruct(out, F32) for out in outs
        ],
        scratch_shapes=[
            pltpu.VMEM(shape, F32) if isinstance(shape, tuple) else shape for shape in scratch
        ],
        compiler_params=pltpu.CompilerParams(vmem_limit_bytes=room * 1024 * 1024),
        **specs,
    )


def in_order(array, first):
    def kernel(array_ref, first_ref, out_ref):
        out_ref[...] = array_ref[...]

    (array,) = call(kernel, (array.shape,), (), "va", 12)(array, first)
    return array


def pairs(axes):
    count = lax.axis_size(axes)
    inner = [(i, i ^ 1) for i in range(count)]
    outer = [(i, (i + 1) % count if i % 2 else (i - 1) % count) for i in range(count)]
    return inner, outer


def exchange(first, second, axes):
    inner, outer = pairs(axes)
    return lax.ppermute(first, axes, inner), lax.ppermute(second, axes, outer)


def on_device(velocity, canopy, weight_in, bias_in, weight_out, bias_out, cotangent):
    field = (3, 4, 16, 128)
    rows = (24, 128)
    layers = (6, 24, 128)
    across, along = ("x", "y"), ("zh", "zl")
    swap = [(0, 1), (1, 0)]
    parts = lax.axis_size(across)
    depth = lax.axis_size(along)
    count = HALF // parts
    short = -(-count // depth)

    direct, factor, m1, m2 = call(start_kernel, (field, field[1:], rows, rows))(
        velocity, canopy, cotangent
    )
    y1, y2 = exchange(m1, m2, GY)
    m1, m2 = call(layer_kernel, (layers, layers))(velocity, direct, y1, y2)
    x1, x2 = exchange(m1, m2, GX)
    selection = jnp.asarray(selector())
    weight_in, weight_out, selection = call(
        weights_in_kernel,
        (weight_in, weight_out, selection),
        (pltpu.SemaphoreType.DMA((3,)),),
        "ahhh",
    )(m1, weight_in, weight_out, selection)
    keep, send, nv, vg, m1, m2, ylow, yhigh = call(
        main_kernel,
        ((HALF, 128), (HALF, 128), field, field, layers, layers, rows, rows),
        (
            (36, 24, 128),
            (24, 24, 128),
            (648, 128),
            (384, 128),
            (648, 128),
            (144, 768),
            (192, 512),
            (18, 24, 128),
            (24, 32, 128),
            (FLAT, 128),
        ),
    )(
        velocity, direct, y1, y2, x1, x2,
        weight_in, bias_in[None], weight_out, bias_out[None], selection,
    )

    half = (keep + lax.ppermute(send, "core", swap)).reshape(parts, count, 128)
    got = lax.all_to_all(half, across, 0, 0)
    x1, x2 = exchange(m1, m2, GX)
    m1, m2 = call(side_kernel, (rows, rows), (rows, rows))(x1, x2, ylow, yhigh)
    cut = (depth, 1, short * 128)
    (part,) = call(across_kernel, (cut,), ((short * depth, 128),), "va", 12)(got, x2)
    got = lax.all_to_all(part, along, 0, 0)
    (part,) = call(along_kernel, (cut,), (), "v", 12)(got)
    got = lax.all_to_all(part, along, 0, 0)
    (half,) = call(spread_kernel, (half.shape,), ((short * depth, 128),), "v", 12)(got)
    mine = lax.all_to_all(half, across, 0, 0).reshape(HALF, 128)
    y1, y2 = exchange(m1, m2, GY)
    new_velocity, velocity_grad, done = call(
        end_kernel, (field, field, (8, 128)), ((4, 16, 128),), None, 12
    )(nv, vg, factor, x1, x2, y1, y2)
    mine = in_order(mine, done)
    other = lax.ppermute(mine, "core", swap)
    blocks = 128 * lax.axis_size(GX) * lax.axis_size(GY)
    scale = float(blocks) ** -0.5
    weight_in_grad, bias_in_grad, weight_out_grad, bias_out_grad = call(
        lambda *refs: weights_kernel(scale, *refs), ((648, 512), (1, 512), (512, 384), (1, 384))
    )(mine, other)
    return (
        new_velocity,
        velocity_grad,
        weight_in_grad,
        bias_in_grad[0],
        weight_out_grad,
        bias_out_grad[0],
    )


def solution(mesh):
    if mesh.devices.size == 512:
        mesh = Mesh(mesh.devices.reshape(4, 4, 4, 4, 2), GX + GY)
    placed = (
        P(None, GX, GY, None),
        P(GX, GY, None),
        P(),
        P(),
        P(),
        P(),
        P(None, GX, GY, None),
    )
    return jax.shard_map(
        on_device,
        mesh=mesh,
        in_specs=placed,
        out_specs=(P(None, GX, GY, None), P(None, GX, GY, None), P(), P(), P(), P()),
        check_vma=False,
    )
```

```python
import jax
import jax.numpy as jnp
import numpy as np
from jax import lax
from jax.experimental import pallas as pl
from jax.experimental.pallas import tpu as pltpu
from jax.sharding import Mesh, PartitionSpec as P

time_step = 0.25
viscosity = 0.2
penalty_eta = 0.05

GX = ("zh", "x", "y")
GY = ("zl", "core")
FLAT = 4352
HALF = FLAT // 2
WIN_ROWS = 648
WOUT_BASE = 4 * WIN_ROWS
BIAS_BASE = WOUT_BASE + 3 * 512
F32 = jnp.float32
BF16 = jnp.bfloat16


def selector():
    table = np.zeros((4, 128, 6, 4, 32), np.float32)
    for offset in range(6):
        for block in range(32):
            z = 4 * block + offset - 1
            if 0 <= z < 128:
                for row in range(4):
                    table[row, z, offset, row, block] = 1.0
    return table.reshape(512, 768).astype(jnp.bfloat16)


def z_next(field):
    lane = lax.broadcasted_iota(jnp.int32, field.shape, field.ndim - 1)
    return jnp.where(lane < 127, pltpu.roll(field, 127, field.ndim - 1), 0.0)


def z_before(field):
    lane = lax.broadcasted_iota(jnp.int32, field.shape, field.ndim - 1)
    return jnp.where(lane > 0, pltpu.roll(field, 1, field.ndim - 1), 0.0)


def split(value):
    high = value.astype(BF16)
    low = (value - high.astype(F32)).astype(BF16)
    return high, low


def dot(left, right, left_dim, right_dim):
    return lax.dot_general(
        left, right, (((left_dim,), (right_dim,)), ((), ())), preferred_element_type=F32
    )


def damping(canopy):
    return 1.0 + time_step * canopy.astype(F32) / penalty_eta


def start_kernel(v_ref, canopy_ref, cot_ref, direct_ref, factor_ref, m1_ref, m2_ref):
    core = lax.axis_index("core")
    factor = damping(canopy_ref[...])
    factor_ref[...] = factor
    for i in range(3):
        direct_ref[i] = cot_ref[i].astype(F32) / factor
    for out, row in ((m1_ref, 15 * (1 - core)), (m2_ref, 15 * core)):
        for i in range(3):
            for x in range(4):
                out[pl.ds(i * 4 + x, 1), :] = v_ref[i, x, pl.ds(row, 1), :]
                out[pl.ds(12 + i * 4 + x, 1), :] = (
                    direct_ref[i, x, pl.ds(row, 1), :] * time_step
                )


def weights_in_kernel(after, win_hbm, wout_hbm, sel_hbm, win_ref, wout_ref, sel_ref, sems):
    copies = [
        pltpu.make_async_copy(source, target, sems.at[i])
        for i, (source, target) in enumerate(
            ((win_hbm, win_ref), (wout_hbm, wout_ref), (sel_hbm, sel_ref))
        )
    ]
    for copy in copies:
        copy.start()
    for copy in copies:
        copy.wait()


def layer_kernel(v_ref, direct_ref, r1_ref, r2_ref, m1_ref, m2_ref):
    core = lax.axis_index("core")
    parity = lax.rem(lax.axis_index("y"), 2)
    for out, x in ((m1_ref, 3 * (1 - parity)), (m2_ref, 3 * parity)):
        for k in range(6):
            out[k, 16:24, :] = jnp.zeros((8, 128), F32)
            if k < 3:
                out[k, 1:17, :] = v_ref[k, x]
            else:
                out[k, 1:17, :] = direct_ref[k - 3, x] * time_step
            row1 = r1_ref[pl.ds(k * 4 + x, 1), :]
            row2 = r2_ref[pl.ds(k * 4 + x, 1), :]
            out[k, 0:1, :] = jnp.where(core == 0, row2, row1)
            out[k, 17:18, :] = jnp.where(core == 0, row1, row2)


def shifted(ext):
    def at(k, dx, dy):
        return ext[k * 6 + 1 + dx : k * 6 + 5 + dx, 1 + dy : 17 + dy, :]

    return at


def slopes(at):
    grad_x = [(at(3 + i, 1, 0) - at(3 + i, -1, 0)) * 0.5 for i in range(3)]
    grad_y = [(at(3 + i, 0, 1) - at(3 + i, 0, -1)) * 0.5 for i in range(3)]
    grad_z = [(z_next(at(3 + i, 0, 0)) - z_before(at(3 + i, 0, 0))) * 0.5 for i in range(3)]
    return grad_x, grad_y, grad_z


def main_kernel(
    v_ref, direct_ref, r1_ref, r2_ref, x1_ref, x2_ref,
    win_ref, bin_ref, wout_ref, sel_ref,
    keep_ref, send_ref, ext, hidden_ref, pre_low_ref, sgrad, cols, rows, flat,
):
    core = lax.axis_index("core")
    parity = lax.rem(lax.axis_index("y"), 2)

    for k in range(6):
        ext[k * 6] = jnp.where(parity == 0, x2_ref[k], x1_ref[k])
        ext[k * 6 + 5] = jnp.where(parity == 0, x1_ref[k], x2_ref[k])
        for x in range(4):
            spot = k * 6 + 1 + x
            ext[spot, 16:24, :] = jnp.zeros((8, 128), F32)
            ext[spot, 1:17, :] = v_ref[k, x] if k < 3 else direct_ref[k - 3, x] * time_step
            row1 = r1_ref[k * 4 + x : k * 4 + x + 1, :]
            row2 = r2_ref[k * 4 + x : k * 4 + x + 1, :]
            ext[spot, 0:1, :] = jnp.where(core == 0, row2, row1)
            ext[spot, 17:18, :] = jnp.where(core == 0, row1, row2)

    grad_x, grad_y, grad_z = slopes(shifted(ext))
    stress_grad = (
        grad_x[0],
        grad_y[1],
        grad_z[2],
        grad_y[0] + grad_x[1],
        grad_z[0] + grad_x[2],
        grad_z[1] + grad_y[2],
    )
    sgrad[:, 16:24, :] = jnp.zeros((24, 8, 128), F32)
    for s in range(6):
        sgrad[s * 4 : s * 4 + 4, 0:16, :] = -stress_grad[s]
    selection = sel_ref[...]
    inner = sel_ref[:, 128:640]

    parts = [sgrad[:, 4 * b : 4 * b + 8, :].reshape(192, 128) for b in range(4)]
    high, low = split(jnp.concatenate(parts, axis=1))
    picked = dot(high, inner, 1, 0) + dot(low, inner, 1, 0)
    for sa in range(24):
        for c in range(4):
            rows[pl.ds(sa * 16 + c, 4, stride=4), :] = picked[
                sa * 8 : sa * 8 + 4, c * 128 : c * 128 + 128
            ]
    rows_t = rows[...].T
    rows_low = rows_t.astype(BF16)
    bias_out_sum = jnp.sum(rows_t, axis=0, keepdims=True)

    parts = [
        ext[0:18, 4 * b : 4 * b + 8, :].reshape(144, 128).astype(BF16) for b in range(4)
    ]
    picked = dot(jnp.concatenate(parts, axis=1), selection, 1, 0)
    for g in range(18):
        for z in range(6):
            cols[pl.ds(g * 36 + z, 6, stride=6), :] = picked[
                g * 8 : g * 8 + 6, z * 128 : z * 128 + 128
            ]
    columns = cols[...].astype(BF16)

    pre_act = dot(columns, win_ref[...], 0, 0) + bin_ref[...]
    sigmoid_pre = jax.nn.sigmoid(pre_act)
    hidden = (pre_act * sigmoid_pre).astype(BF16)
    hidden_grad = dot(rows_low, wout_ref[...], 1, 1)
    pre_grad = hidden_grad * (sigmoid_pre * (1.0 + pre_act * (1.0 - sigmoid_pre)))
    pre_low = pre_grad.astype(BF16)
    hidden_ref[...] = hidden
    pre_low_ref[...] = pre_low
    bias_in_sum = jnp.sum(pre_grad, axis=0, keepdims=True)

    weight_in_sum = dot(columns, pre_low, 1, 0)
    for q in range(4):
        flat[q * WIN_ROWS : (q + 1) * WIN_ROWS, :] = weight_in_sum[:, q * 128 : q * 128 + 128]
    weight_out_sum = dot(hidden, rows_low, 0, 0)
    for q in range(3):
        flat[WOUT_BASE + q * 512 : WOUT_BASE + q * 512 + 512, :] = weight_out_sum[
            :, q * 128 : q * 128 + 128
        ]
    flat[BIAS_BASE:FLAT, :] = jnp.zeros((FLAT - BIAS_BASE, 128), F32)
    for q in range(4):
        flat[BIAS_BASE + q : BIAS_BASE + q + 1, :] = bias_in_sum[:, q * 128 : q * 128 + 128]
    for q in range(3):
        flat[BIAS_BASE + 4 + q : BIAS_BASE + 5 + q, :] = bias_out_sum[:, q * 128 : q * 128 + 128]
    keep_ref[...] = flat[pl.ds(pl.multiple_of(core * HALF, 8), HALF), :]
    send_ref[...] = flat[pl.ds(pl.multiple_of((1 - core) * HALF, 8), HALF), :]


def cells_kernel(
    direct_ref, ext, hidden_ref, pre_low_ref, win_ref, wout_ref, bout_ref, sel_ref,
    nv_ref, vg_ref, m1_ref, m2_ref, ylow_ref, yhigh_ref,
    cgrad, rows, cpad, opad, ghost, tau,
):
    parity = lax.rem(lax.axis_index("y"), 2)
    at = shifted(ext)
    grad_x, grad_y, grad_z = slopes(at)
    selection = sel_ref[...]
    inner = sel_ref[:, 128:640]

    def laplace(k):
        middle = at(k, 0, 0)
        total = at(k, 1, 0) + at(k, -1, 0) + at(k, 0, 1) + at(k, 0, -1)
        return total + z_next(middle) + z_before(middle) - 6.0 * middle

    for j in range(3):
        velocity = [at(i, 0, 0) for i in range(3)]
        slope = (grad_x, grad_y, grad_z)[j]
        total = direct_ref[j] + viscosity * laplace(3 + j)
        total = total + slope[0] * velocity[0] + slope[1] * velocity[1] + slope[2] * velocity[2]
        total = total + grad_x[j] * velocity[0] + grad_y[j] * velocity[1] + grad_z[j] * velocity[2]
        vg_ref[j] = total

    cgrad[...] = dot(win_ref[...], pre_low_ref[...], 1, 1)
    for g in range(18):
        for z in range(6):
            cpad[g * 8 : g * 8 + 6, z * 128 : z * 128 + 128] = cgrad[
                pl.ds(g * 36 + z, 6, stride=6), :
            ]
            cpad[g * 8 + 6 : g * 8 + 8, z * 128 : z * 128 + 128] = jnp.zeros((2, 128), F32)
    high, low = split(cpad[...])
    spread = dot(high, selection, 1, 1) + dot(low, selection, 1, 1)
    spread = spread.reshape(18, 8, 512)
    ghost[...] = jnp.zeros((18, 24, 128), F32)
    for b in range(4):
        ghost[:, 4 * b : 4 * b + 8, :] += spread[:, :, b * 128 : b * 128 + 128]
    for j in range(3):
        vg_ref[j] += ghost[j * 6 + 1 : j * 6 + 5, 1:17, :]

    outputs = dot(hidden_ref[...], wout_ref[...], 1, 0) + bout_ref[...]
    rows[...] = outputs.T
    for sa in range(24):
        for c in range(4):
            opad[sa * 8 : sa * 8 + 4, c * 128 : c * 128 + 128] = rows[
                pl.ds(sa * 16 + c, 4, stride=4), :
            ]
            opad[sa * 8 + 4 : sa * 8 + 8, c * 128 : c * 128 + 128] = jnp.zeros((4, 128), F32)
    high, low = split(opad[...])
    spread = dot(high, inner, 1, 1) + dot(low, inner, 1, 1)
    spread = spread.reshape(24, 8, 512)
    tau[:, 0:8, :] = jnp.zeros((24, 8, 128), F32)
    tau[:, 24:32, :] = jnp.zeros((24, 8, 128), F32)
    for b in range(4):
        tau[:, 8 + 4 * b : 12 + 4 * b, :] = spread[:, 0:4, b * 128 : b * 128 + 128]

    blank = jnp.zeros((1, 16, 128), F32)
    for i, (along_x, along_y, along_z) in enumerate(((0, 3, 4), (3, 1, 5), (4, 5, 2))):
        inside = tau[along_x * 4 : along_x * 4 + 4, 8:24, :]
        force = jnp.concatenate([inside[1:4], blank]) - jnp.concatenate([blank, inside[0:3]])
        force = force + tau[along_y * 4 : along_y * 4 + 4, 9:25, :]
        force = force - tau[along_y * 4 : along_y * 4 + 4, 7:23, :]
        inside = tau[along_z * 4 : along_z * 4 + 4, 8:24, :]
        force = (force + z_next(inside) - z_before(inside)) * 0.5
        product = at(2, 0, 0) * at(i, 0, 0)
        flow = at(0, 1, 0) * at(i, 1, 0) - at(0, -1, 0) * at(i, -1, 0)
        flow = flow + at(1, 0, 1) * at(i, 0, 1) - at(1, 0, -1) * at(i, 0, -1)
        flow = (flow + z_next(product) - z_before(product)) * 0.5
        nv_ref[i] = at(i, 0, 0) + time_step * (viscosity * laplace(i) - flow + force)

    for out, side in ((m1_ref, 1 - parity), (m2_ref, parity)):
        for j, s in enumerate((0, 3, 4)):
            out[j, 0:16, :] = tau[s * 4 + 3 * side, 8:24, :]
            out[j, 16:24, :] = jnp.zeros((8, 128), F32)
            out[3 + j] = ghost[j * 6 + 5 * side]
    for j, s in enumerate((3, 1, 5)):
        for x in range(4):
            spot = j * 4 + x
            ylow_ref[spot : spot + 1, :] = tau[s * 4 + x, 8:9, :]
            yhigh_ref[spot : spot + 1, :] = tau[s * 4 + x, 23:24, :]
            ylow_ref[12 + spot : 13 + spot, :] = ghost[j * 6 + 1 + x, 0:1, :]
            yhigh_ref[12 + spot : 13 + spot, :] = ghost[j * 6 + 1 + x, 17:18, :]


def side_kernel(x1_ref, x2_ref, ylow_ref, yhigh_ref, m1_ref, m2_ref, low, high):
    core = lax.axis_index("core")
    parity = lax.rem(lax.axis_index("y"), 2)
    low[...] = ylow_ref[...]
    high[...] = yhigh_ref[...]
    for j in range(3):
        from_low = jnp.where(parity == 0, x2_ref[3 + j], x1_ref[3 + j])
        from_high = jnp.where(parity == 0, x1_ref[3 + j], x2_ref[3 + j])
        first, last = 12 + j * 4, 15 + j * 4
        low[first : first + 1, :] += from_low[0:1]
        low[last : last + 1, :] += from_high[0:1]
        high[first : first + 1, :] += from_low[17:18]
        high[last : last + 1, :] += from_high[17:18]
    m1_ref[...] = jnp.where(core == 0, high[...], low[...])
    m2_ref[...] = jnp.where(core == 0, low[...], high[...])


def end_kernel(
    nv_ref, vg_ref, factor_ref, x1_ref, x2_ref, y1_ref, y2_ref, new_ref, grad_ref, part
):
    core = lax.axis_index("core")
    parity = lax.rem(lax.axis_index("y"), 2)
    factor = factor_ref[...]
    y_low = jnp.where(core == 0, y2_ref[...], y1_ref[...])
    y_high = jnp.where(core == 0, y1_ref[...], y2_ref[...])
    step = time_step * 0.5
    for i in range(3):
        part[...] = nv_ref[i]
        part[0] -= step * jnp.where(parity == 0, x2_ref[i, 0:16, :], x1_ref[i, 0:16, :])
        part[3] += step * jnp.where(parity == 0, x1_ref[i, 0:16, :], x2_ref[i, 0:16, :])
        for x in range(4):
            spot = i * 4 + x
            part[x, 0:1, :] -= step * y_low[spot : spot + 1]
            part[x, 15:16, :] += step * y_high[spot : spot + 1]
        new_ref[i] = part[...] / factor
        part[...] = vg_ref[i]
        part[0] += jnp.where(parity == 0, x2_ref[3 + i, 1:17, :], x1_ref[3 + i, 1:17, :])
        part[3] += jnp.where(parity == 0, x1_ref[3 + i, 1:17, :], x2_ref[3 + i, 1:17, :])
        for x in range(4):
            spot = 12 + i * 4 + x
            part[x, 0:1, :] += y_low[spot : spot + 1]
            part[x, 15:16, :] += y_high[spot : spot + 1]
        grad_ref[i] = part[...]


def weights_kernel(scale, mine_ref, other_ref, win_ref, bin_ref, wout_ref, bout_ref):
    core = lax.axis_index("core")

    def put(out, lanes, start, count, first, second):
        done = 0
        while done < count:
            spot = start + done
            source, spot, room = (
                (first, spot, HALF - spot) if spot < HALF else (second, spot - HALF, count)
            )
            size = min(count - done, room)
            out[done : done + size, lanes * 128 : lanes * 128 + 128] = (
                source[spot : spot + size, :] * scale
            )
            done += size

    def write(first, second):
        for q in range(4):
            put(win_ref, q, q * WIN_ROWS, WIN_ROWS, first, second)
            row = second[BIAS_BASE + q - HALF, :]
            bin_ref[q * 128 : q * 128 + 128] = row * scale
        for q in range(3):
            put(wout_ref, q, WOUT_BASE + q * 512, 512, first, second)
            row = second[BIAS_BASE + 4 + q - HALF, :]
            bout_ref[q * 128 : q * 128 + 128] = row * scale

    @pl.when(core == 0)
    def _():
        write(mine_ref, other_ref)

    @pl.when(core == 1)
    def _():
        write(other_ref, mine_ref)


def add_kernel(first_ref, second_ref, after, out_ref):
    out_ref[...] = first_ref[...] + second_ref[...]


def across_kernel(got_ref, *rest):
    out_ref, part = rest[-2:]
    count = got_ref.shape[1]
    depth, _, width = out_ref.shape
    short = width // 128
    part[...] = jnp.zeros(part.shape, F32)
    part[0:count, :] = jnp.sum(got_ref[...], axis=0)
    for i in range(depth):
        for j in range(short):
            out_ref[i, 0:1, j * 128 : j * 128 + 128] = part[i * short + j : i * short + j + 1, :]


def along_kernel(got_ref, *rest):
    out_ref = rest[-1]
    total = jnp.sum(got_ref[...], axis=0, keepdims=True)
    out_ref[...] = jnp.broadcast_to(total, out_ref.shape)


def spread_kernel(got_ref, *rest):
    out_ref, part = rest[-2:]
    depth, _, width = got_ref.shape
    short = width // 128
    count = out_ref.shape[1]
    for i in range(depth):
        for j in range(short):
            part[i * short + j : i * short + j + 1, :] = got_ref[i, 0:1, j * 128 : j * 128 + 128]
    for i in range(out_ref.shape[0]):
        out_ref[i] = part[0:count, :]


def call(kernel, outs, scratch=(), places=None, room=12):
    spaces = {"v": pltpu.VMEM, "h": pltpu.HBM, "a": pl.ANY}
    specs = {}
    if places is not None:
        specs["in_specs"] = [pl.BlockSpec(memory_space=spaces[place]) for place in places]
    return pl.pallas_call(
        kernel,
        out_shape=[
            out if hasattr(out, "dtype") else jax.ShapeDtypeStruct(out, F32) for out in outs
        ],
        scratch_shapes=[
            pltpu.VMEM(shape, F32) if isinstance(shape, tuple) else shape for shape in scratch
        ],
        compiler_params=pltpu.CompilerParams(vmem_limit_bytes=room * 1024 * 1024),
        **specs,
    )


def pairs(axes):
    count = lax.axis_size(axes)
    inner = [(i, i ^ 1) for i in range(count)]
    outer = [(i, (i + 1) % count if i % 2 else (i - 1) % count) for i in range(count)]
    return inner, outer


def exchange(first, second, axes):
    inner, outer = pairs(axes)
    return lax.ppermute(first, axes, inner), lax.ppermute(second, axes, outer)


def on_device(velocity, canopy, weight_in, bias_in, weight_out, bias_out, cotangent):
    field = (3, 4, 16, 128)
    rows = (24, 128)
    layers = (6, 24, 128)
    across, along = ("x", "y"), ("zh", "zl")
    swap = [(0, 1), (1, 0)]
    parts = lax.axis_size(across)
    depth = lax.axis_size(along)
    count = HALF // parts
    short = -(-count // depth)

    direct, factor, m1, m2 = call(start_kernel, (field, field[1:], rows, rows))(
        velocity, canopy, cotangent
    )
    y1, y2 = exchange(m1, m2, GY)
    m1, m2 = call(layer_kernel, (layers, layers))(velocity, direct, y1, y2)
    x1, x2 = exchange(m1, m2, GX)
    selection = jnp.asarray(selector())
    weight_in, weight_out, selection = call(
        weights_in_kernel,
        (weight_in, weight_out, selection),
        (pltpu.SemaphoreType.DMA((3,)),),
        "ahhh",
    )(m1, weight_in, weight_out, selection)
    hidden_type = jax.ShapeDtypeStruct((128, 512), BF16)
    keep, send, ext, hidden, pre_low = call(
        main_kernel,
        ((HALF, 128), (HALF, 128), (36, 24, 128), hidden_type, hidden_type),
        ((24, 24, 128), (648, 128), (384, 128), (FLAT, 128)),
        None,
        24,
    )(
        velocity, direct, y1, y2, x1, x2,
        weight_in, bias_in[None], weight_out, selection,
    )
    got = lax.ppermute(send, "core", swap)
    nv, vg, m1, m2, ylow, yhigh = call(
        cells_kernel,
        (field, field, layers, layers, rows, rows),
        (
            (648, 128),
            (384, 128),
            (144, 768),
            (192, 512),
            (18, 24, 128),
            (24, 32, 128),
        ),
        None,
        16,
    )(direct, ext, hidden, pre_low, weight_in, weight_out, bias_out[None], selection)

    (half,) = call(add_kernel, (keep.shape,), (), "vva", 16)(keep, got, ylow)
    half = half.reshape(parts, count, 128)
    got = lax.all_to_all(half, across, 0, 0)
    x1, x2 = exchange(m1, m2, GX)
    m1, m2 = call(side_kernel, (rows, rows), (rows, rows))(x1, x2, ylow, yhigh)
    cut = (depth, 1, short * 128)
    (part,) = call(across_kernel, (cut,), ((short * depth, 128),), "va", 12)(got, x2)
    got = lax.all_to_all(part, along, 0, 0)
    y1, y2 = exchange(m1, m2, GY)
    (part,) = call(along_kernel, (cut,), (), "vaa", 12)(got, y1, y2)
    got = lax.all_to_all(part, along, 0, 0)
    (half,) = call(spread_kernel, (half.shape,), ((short * depth, 128),), "v", 12)(got)
    mine = lax.all_to_all(half, across, 0, 0).reshape(HALF, 128)
    new_velocity, velocity_grad = call(
        end_kernel, (field, field), ((4, 16, 128),), None, 12
    )(nv, vg, factor, x1, x2, y1, y2)
    other = lax.ppermute(mine, "core", swap)
    blocks = 128 * lax.axis_size(GX) * lax.axis_size(GY)
    scale = float(blocks) ** -0.5
    weight_in_grad, bias_in_grad, weight_out_grad, bias_out_grad = call(
        lambda *refs: weights_kernel(scale, *refs), ((648, 512), (512,), (512, 384), (384,))
    )(mine, other)
    return (
        new_velocity,
        velocity_grad,
        weight_in_grad,
        bias_in_grad,
        weight_out_grad,
        bias_out_grad,
    )


def solution(mesh):
    if mesh.devices.size == 512:
        mesh = Mesh(mesh.devices.reshape(4, 4, 4, 4, 2), GX + GY)
    placed = (
        P(None, GX, GY, None),
        P(GX, GY, None),
        P(),
        P(),
        P(),
        P(),
        P(None, GX, GY, None),
    )
    return jax.shard_map(
        on_device,
        mesh=mesh,
        in_specs=placed,
        out_specs=(P(None, GX, GY, None), P(None, GX, GY, None), P(), P(), P(), P()),
        check_vma=False,
    )
```

```python
import jax
import jax.numpy as jnp
import numpy as np
from jax import lax
from jax.experimental import pallas as pl
from jax.experimental.pallas import tpu as pltpu
from jax.sharding import Mesh, PartitionSpec as P

time_step = 0.25
viscosity = 0.2
penalty_eta = 0.05

GX = ("zh", "x", "y")
GY = ("zl", "core")
FLAT = 4352
HALF = FLAT // 2
WIN_ROWS = 648
WOUT_BASE = 4 * WIN_ROWS
BIAS_BASE = WOUT_BASE + 3 * 512
F32 = jnp.float32
BF16 = jnp.bfloat16


def selector():
    table = np.zeros((4, 128, 6, 4, 32), np.float32)
    for offset in range(6):
        for block in range(32):
            z = 4 * block + offset - 1
            if 0 <= z < 128:
                for row in range(4):
                    table[row, z, offset, row, block] = 1.0
    return table.reshape(512, 768).astype(jnp.bfloat16)


def z_next(field):
    lane = lax.broadcasted_iota(jnp.int32, field.shape, field.ndim - 1)
    return jnp.where(lane < 127, pltpu.roll(field, 127, field.ndim - 1), 0.0)


def z_before(field):
    lane = lax.broadcasted_iota(jnp.int32, field.shape, field.ndim - 1)
    return jnp.where(lane > 0, pltpu.roll(field, 1, field.ndim - 1), 0.0)


def split(value):
    high = value.astype(BF16)
    low = (value - high.astype(F32)).astype(BF16)
    return high, low


def dot(left, right, left_dim, right_dim):
    return lax.dot_general(
        left, right, (((left_dim,), (right_dim,)), ((), ())), preferred_element_type=F32
    )


def damping(canopy):
    return 1.0 + time_step * canopy.astype(F32) / penalty_eta


def start_kernel(v_ref, canopy_ref, cot_ref, direct_ref, factor_ref, m1_ref, m2_ref):
    core = lax.axis_index("core")
    factor = damping(canopy_ref[...])
    factor_ref[...] = factor
    for i in range(3):
        direct_ref[i] = cot_ref[i].astype(F32) / factor
    for out, row in ((m1_ref, 15 * (1 - core)), (m2_ref, 15 * core)):
        for i in range(3):
            for x in range(4):
                out[pl.ds(i * 4 + x, 1), :] = v_ref[i, x, pl.ds(row, 1), :]
                out[pl.ds(12 + i * 4 + x, 1), :] = (
                    direct_ref[i, x, pl.ds(row, 1), :] * time_step
                )


def weights_in_kernel(after, win_hbm, wout_hbm, sel_hbm, win_ref, wout_ref, sel_ref, sems):
    copies = [
        pltpu.make_async_copy(source, target, sems.at[i])
        for i, (source, target) in enumerate(
            ((win_hbm, win_ref), (wout_hbm, wout_ref), (sel_hbm, sel_ref))
        )
    ]
    for copy in copies:
        copy.start()
    for copy in copies:
        copy.wait()


def layer_kernel(v_ref, direct_ref, r1_ref, r2_ref, m1_ref, m2_ref):
    core = lax.axis_index("core")
    parity = lax.rem(lax.axis_index("y"), 2)
    for out, x in ((m1_ref, 3 * (1 - parity)), (m2_ref, 3 * parity)):
        for k in range(6):
            out[k, 16:24, :] = jnp.zeros((8, 128), F32)
            if k < 3:
                out[k, 1:17, :] = v_ref[k, x]
            else:
                out[k, 1:17, :] = direct_ref[k - 3, x] * time_step
            row1 = r1_ref[pl.ds(k * 4 + x, 1), :]
            row2 = r2_ref[pl.ds(k * 4 + x, 1), :]
            out[k, 0:1, :] = jnp.where(core == 0, row2, row1)
            out[k, 17:18, :] = jnp.where(core == 0, row1, row2)


def shifted(ext):
    def at(k, dx, dy):
        return ext[k * 6 + 1 + dx : k * 6 + 5 + dx, 1 + dy : 17 + dy, :]

    return at


def slopes(at):
    grad_x = [(at(3 + i, 1, 0) - at(3 + i, -1, 0)) * 0.5 for i in range(3)]
    grad_y = [(at(3 + i, 0, 1) - at(3 + i, 0, -1)) * 0.5 for i in range(3)]
    grad_z = [(z_next(at(3 + i, 0, 0)) - z_before(at(3 + i, 0, 0))) * 0.5 for i in range(3)]
    return grad_x, grad_y, grad_z


def main_kernel(
    v_ref, direct_ref, r1_ref, r2_ref, x1_ref, x2_ref,
    win_ref, bin_ref, wout_ref, sel_ref,
    keep_ref, send_ref, ext, hidden_ref, pre_low_ref, sgrad, cols, rows, flat,
):
    core = lax.axis_index("core")
    parity = lax.rem(lax.axis_index("y"), 2)

    for k in range(6):
        ext[k * 6] = jnp.where(parity == 0, x2_ref[k], x1_ref[k])
        ext[k * 6 + 5] = jnp.where(parity == 0, x1_ref[k], x2_ref[k])
        for x in range(4):
            spot = k * 6 + 1 + x
            ext[spot, 16:24, :] = jnp.zeros((8, 128), F32)
            ext[spot, 1:17, :] = v_ref[k, x] if k < 3 else direct_ref[k - 3, x] * time_step
            row1 = r1_ref[k * 4 + x : k * 4 + x + 1, :]
            row2 = r2_ref[k * 4 + x : k * 4 + x + 1, :]
            ext[spot, 0:1, :] = jnp.where(core == 0, row2, row1)
            ext[spot, 17:18, :] = jnp.where(core == 0, row1, row2)

    grad_x, grad_y, grad_z = slopes(shifted(ext))
    stress_grad = (
        grad_x[0],
        grad_y[1],
        grad_z[2],
        grad_y[0] + grad_x[1],
        grad_z[0] + grad_x[2],
        grad_z[1] + grad_y[2],
    )
    sgrad[:, 16:24, :] = jnp.zeros((24, 8, 128), F32)
    for s in range(6):
        sgrad[s * 4 : s * 4 + 4, 0:16, :] = -stress_grad[s]
    selection = sel_ref[...]
    inner = sel_ref[:, 128:640]

    parts = [sgrad[:, 4 * b : 4 * b + 8, :].reshape(192, 128) for b in range(4)]
    high, low = split(jnp.concatenate(parts, axis=1))
    picked = dot(high, inner, 1, 0) + dot(low, inner, 1, 0)
    for sa in range(24):
        for c in range(4):
            rows[pl.ds(sa * 16 + c, 4, stride=4), :] = picked[
                sa * 8 : sa * 8 + 4, c * 128 : c * 128 + 128
            ]
    rows_t = rows[...].T
    rows_low = rows_t.astype(BF16)
    bias_out_sum = jnp.sum(rows_t, axis=0, keepdims=True)

    parts = [
        ext[0:18, 4 * b : 4 * b + 8, :].reshape(144, 128).astype(BF16) for b in range(4)
    ]
    picked = dot(jnp.concatenate(parts, axis=1), selection, 1, 0)
    for g in range(18):
        for z in range(6):
            cols[pl.ds(g * 36 + z, 6, stride=6), :] = picked[
                g * 8 : g * 8 + 6, z * 128 : z * 128 + 128
            ]
    columns = cols[...].astype(BF16)

    pre_act = dot(columns, win_ref[...], 0, 0) + bin_ref[...]
    sigmoid_pre = jax.nn.sigmoid(pre_act)
    hidden = (pre_act * sigmoid_pre).astype(BF16)
    hidden_grad = dot(rows_low, wout_ref[...], 1, 1)
    pre_grad = hidden_grad * (sigmoid_pre * (1.0 + pre_act * (1.0 - sigmoid_pre)))
    pre_low = pre_grad.astype(BF16)
    hidden_ref[...] = hidden
    pre_low_ref[...] = pre_low
    bias_in_sum = jnp.sum(pre_grad, axis=0, keepdims=True)

    weight_in_sum = dot(columns, pre_low, 1, 0)
    for q in range(4):
        flat[q * WIN_ROWS : (q + 1) * WIN_ROWS, :] = weight_in_sum[:, q * 128 : q * 128 + 128]
    weight_out_sum = dot(hidden, rows_low, 0, 0)
    for q in range(3):
        flat[WOUT_BASE + q * 512 : WOUT_BASE + q * 512 + 512, :] = weight_out_sum[
            :, q * 128 : q * 128 + 128
        ]
    flat[BIAS_BASE:FLAT, :] = jnp.zeros((FLAT - BIAS_BASE, 128), F32)
    for q in range(4):
        flat[BIAS_BASE + q : BIAS_BASE + q + 1, :] = bias_in_sum[:, q * 128 : q * 128 + 128]
    for q in range(3):
        flat[BIAS_BASE + 4 + q : BIAS_BASE + 5 + q, :] = bias_out_sum[:, q * 128 : q * 128 + 128]
    keep_ref[...] = flat[pl.ds(pl.multiple_of(core * HALF, 8), HALF), :]
    send_ref[...] = flat[pl.ds(pl.multiple_of((1 - core) * HALF, 8), HALF), :]


def cells_kernel(
    direct_ref, ext, hidden_ref, pre_low_ref, win_ref, wout_ref, bout_ref, sel_ref,
    nv_ref, vg_ref, m1_ref, m2_ref, ylow_ref, yhigh_ref,
    cgrad, rows, cpad, opad, ghost, tau,
):
    parity = lax.rem(lax.axis_index("y"), 2)
    at = shifted(ext)
    grad_x, grad_y, grad_z = slopes(at)
    selection = sel_ref[...]
    inner = sel_ref[:, 128:640]

    def laplace(k):
        middle = at(k, 0, 0)
        total = at(k, 1, 0) + at(k, -1, 0) + at(k, 0, 1) + at(k, 0, -1)
        return total + z_next(middle) + z_before(middle) - 6.0 * middle

    for j in range(3):
        velocity = [at(i, 0, 0) for i in range(3)]
        slope = (grad_x, grad_y, grad_z)[j]
        total = direct_ref[j] + viscosity * laplace(3 + j)
        total = total + slope[0] * velocity[0] + slope[1] * velocity[1] + slope[2] * velocity[2]
        total = total + grad_x[j] * velocity[0] + grad_y[j] * velocity[1] + grad_z[j] * velocity[2]
        vg_ref[j] = total

    cgrad[...] = dot(win_ref[...], pre_low_ref[...], 1, 1)
    for g in range(18):
        for z in range(6):
            cpad[g * 8 : g * 8 + 6, z * 128 : z * 128 + 128] = cgrad[
                pl.ds(g * 36 + z, 6, stride=6), :
            ]
            cpad[g * 8 + 6 : g * 8 + 8, z * 128 : z * 128 + 128] = jnp.zeros((2, 128), F32)
    high, low = split(cpad[...])
    spread = dot(high, selection, 1, 1) + dot(low, selection, 1, 1)
    spread = spread.reshape(18, 8, 512)
    ghost[...] = jnp.zeros((18, 24, 128), F32)
    for b in range(4):
        ghost[:, 4 * b : 4 * b + 8, :] += spread[:, :, b * 128 : b * 128 + 128]
    for j in range(3):
        vg_ref[j] += ghost[j * 6 + 1 : j * 6 + 5, 1:17, :]

    outputs = dot(hidden_ref[...], wout_ref[...], 1, 0) + bout_ref[...]
    rows[...] = outputs.T
    for sa in range(24):
        for c in range(4):
            opad[sa * 8 : sa * 8 + 4, c * 128 : c * 128 + 128] = rows[
                pl.ds(sa * 16 + c, 4, stride=4), :
            ]
            opad[sa * 8 + 4 : sa * 8 + 8, c * 128 : c * 128 + 128] = jnp.zeros((4, 128), F32)
    high, low = split(opad[...])
    spread = dot(high, inner, 1, 1) + dot(low, inner, 1, 1)
    spread = spread.reshape(24, 8, 512)
    tau[:, 0:8, :] = jnp.zeros((24, 8, 128), F32)
    tau[:, 24:32, :] = jnp.zeros((24, 8, 128), F32)
    for b in range(4):
        tau[:, 8 + 4 * b : 12 + 4 * b, :] = spread[:, 0:4, b * 128 : b * 128 + 128]

    blank = jnp.zeros((1, 16, 128), F32)
    for i, (along_x, along_y, along_z) in enumerate(((0, 3, 4), (3, 1, 5), (4, 5, 2))):
        inside = tau[along_x * 4 : along_x * 4 + 4, 8:24, :]
        force = jnp.concatenate([inside[1:4], blank]) - jnp.concatenate([blank, inside[0:3]])
        force = force + tau[along_y * 4 : along_y * 4 + 4, 9:25, :]
        force = force - tau[along_y * 4 : along_y * 4 + 4, 7:23, :]
        inside = tau[along_z * 4 : along_z * 4 + 4, 8:24, :]
        force = (force + z_next(inside) - z_before(inside)) * 0.5
        product = at(2, 0, 0) * at(i, 0, 0)
        flow = at(0, 1, 0) * at(i, 1, 0) - at(0, -1, 0) * at(i, -1, 0)
        flow = flow + at(1, 0, 1) * at(i, 0, 1) - at(1, 0, -1) * at(i, 0, -1)
        flow = (flow + z_next(product) - z_before(product)) * 0.5
        nv_ref[i] = at(i, 0, 0) + time_step * (viscosity * laplace(i) - flow + force)

    for out, side in ((m1_ref, 1 - parity), (m2_ref, parity)):
        for j, s in enumerate((0, 3, 4)):
            out[j, 0:16, :] = tau[s * 4 + 3 * side, 8:24, :]
            out[j, 16:24, :] = jnp.zeros((8, 128), F32)
            out[3 + j] = ghost[j * 6 + 5 * side]
    for j, s in enumerate((3, 1, 5)):
        for x in range(4):
            spot = j * 4 + x
            ylow_ref[spot : spot + 1, :] = tau[s * 4 + x, 8:9, :]
            yhigh_ref[spot : spot + 1, :] = tau[s * 4 + x, 23:24, :]
            ylow_ref[12 + spot : 13 + spot, :] = ghost[j * 6 + 1 + x, 0:1, :]
            yhigh_ref[12 + spot : 13 + spot, :] = ghost[j * 6 + 1 + x, 17:18, :]


def side_kernel(x1_ref, x2_ref, ylow_ref, yhigh_ref, m1_ref, m2_ref, low, high):
    core = lax.axis_index("core")
    parity = lax.rem(lax.axis_index("y"), 2)
    low[...] = ylow_ref[...]
    high[...] = yhigh_ref[...]
    for j in range(3):
        from_low = jnp.where(parity == 0, x2_ref[3 + j], x1_ref[3 + j])
        from_high = jnp.where(parity == 0, x1_ref[3 + j], x2_ref[3 + j])
        first, last = 12 + j * 4, 15 + j * 4
        low[first : first + 1, :] += from_low[0:1]
        low[last : last + 1, :] += from_high[0:1]
        high[first : first + 1, :] += from_low[17:18]
        high[last : last + 1, :] += from_high[17:18]
    m1_ref[...] = jnp.where(core == 0, high[...], low[...])
    m2_ref[...] = jnp.where(core == 0, low[...], high[...])


def end_kernel(
    nv_ref, vg_ref, factor_ref, x1_ref, x2_ref, y1_ref, y2_ref, new_ref, grad_ref, part
):
    core = lax.axis_index("core")
    parity = lax.rem(lax.axis_index("y"), 2)
    factor = factor_ref[...]
    y_low = jnp.where(core == 0, y2_ref[...], y1_ref[...])
    y_high = jnp.where(core == 0, y1_ref[...], y2_ref[...])
    step = time_step * 0.5
    for i in range(3):
        part[...] = nv_ref[i]
        part[0] -= step * jnp.where(parity == 0, x2_ref[i, 0:16, :], x1_ref[i, 0:16, :])
        part[3] += step * jnp.where(parity == 0, x1_ref[i, 0:16, :], x2_ref[i, 0:16, :])
        for x in range(4):
            spot = i * 4 + x
            part[x, 0:1, :] -= step * y_low[spot : spot + 1]
            part[x, 15:16, :] += step * y_high[spot : spot + 1]
        new_ref[i] = part[...] / factor
        part[...] = vg_ref[i]
        part[0] += jnp.where(parity == 0, x2_ref[3 + i, 1:17, :], x1_ref[3 + i, 1:17, :])
        part[3] += jnp.where(parity == 0, x1_ref[3 + i, 1:17, :], x2_ref[3 + i, 1:17, :])
        for x in range(4):
            spot = 12 + i * 4 + x
            part[x, 0:1, :] += y_low[spot : spot + 1]
            part[x, 15:16, :] += y_high[spot : spot + 1]
        grad_ref[i] = part[...]


def weights_kernel(scale, mine_ref, other_ref, win_ref, bin_ref, wout_ref, bout_ref):
    core = lax.axis_index("core")

    def put(out, lanes, start, count, first, second):
        done = 0
        while done < count:
            spot = start + done
            source, spot, room = (
                (first, spot, HALF - spot) if spot < HALF else (second, spot - HALF, count)
            )
            size = min(count - done, room)
            out[done : done + size, lanes * 128 : lanes * 128 + 128] = (
                source[spot : spot + size, :] * scale
            )
            done += size

    def write(first, second):
        for q in range(4):
            put(win_ref, q, q * WIN_ROWS, WIN_ROWS, first, second)
            row = second[BIAS_BASE + q - HALF, :]
            bin_ref[q * 128 : q * 128 + 128] = row * scale
        for q in range(3):
            put(wout_ref, q, WOUT_BASE + q * 512, 512, first, second)
            row = second[BIAS_BASE + 4 + q - HALF, :]
            bout_ref[q * 128 : q * 128 + 128] = row * scale

    @pl.when(core == 0)
    def _():
        write(mine_ref, other_ref)

    @pl.when(core == 1)
    def _():
        write(other_ref, mine_ref)


def add_kernel(first_ref, second_ref, after, out_ref):
    out_ref[...] = first_ref[...] + second_ref[...]


def across_kernel(got_ref, *rest):
    out_ref, part = rest[-2:]
    count = got_ref.shape[1]
    depth, _, width = out_ref.shape
    short = width // 128
    part[...] = jnp.zeros(part.shape, F32)
    part[0:count, :] = jnp.sum(got_ref[...], axis=0)
    for i in range(depth):
        for j in range(short):
            out_ref[i, 0:1, j * 128 : j * 128 + 128] = part[i * short + j : i * short + j + 1, :]


def along_kernel(got_ref, *rest):
    out_ref = rest[-1]
    total = jnp.sum(got_ref[...], axis=0, keepdims=True)
    out_ref[...] = jnp.broadcast_to(total, out_ref.shape)


def spread_kernel(got_ref, *rest):
    out_ref, part = rest[-2:]
    depth, _, width = got_ref.shape
    short = width // 128
    count = out_ref.shape[1]
    for i in range(depth):
        for j in range(short):
            part[i * short + j : i * short + j + 1, :] = got_ref[i, 0:1, j * 128 : j * 128 + 128]
    for i in range(out_ref.shape[0]):
        out_ref[i] = part[0:count, :]


def call(kernel, outs, scratch=(), places=None, room=12):
    spaces = {"v": pltpu.VMEM, "h": pltpu.HBM, "a": pl.ANY}
    specs = {}
    if places is not None:
        specs["in_specs"] = [pl.BlockSpec(memory_space=spaces[place]) for place in places]
    return pl.pallas_call(
        kernel,
        out_shape=[
            out if hasattr(out, "dtype") else jax.ShapeDtypeStruct(out, F32) for out in outs
        ],
        scratch_shapes=[
            pltpu.VMEM(shape, F32) if isinstance(shape, tuple) else shape for shape in scratch
        ],
        compiler_params=pltpu.CompilerParams(vmem_limit_bytes=room * 1024 * 1024),
        **specs,
    )


def pairs(axes):
    count = lax.axis_size(axes)
    inner = [(i, i ^ 1) for i in range(count)]
    outer = [(i, (i + 1) % count if i % 2 else (i - 1) % count) for i in range(count)]
    return inner, outer


def exchange(first, second, axes):
    inner, outer = pairs(axes)
    return lax.ppermute(first, axes, inner), lax.ppermute(second, axes, outer)


def on_device(velocity, canopy, weight_in, bias_in, weight_out, bias_out, cotangent):
    field = (3, 4, 16, 128)
    rows = (24, 128)
    layers = (6, 24, 128)
    across, along = ("x", "y"), ("zh", "zl")
    swap = [(0, 1), (1, 0)]
    parts = lax.axis_size(across)
    depth = lax.axis_size(along)
    count = HALF // parts
    short = -(-count // depth)

    direct, factor, m1, m2 = call(start_kernel, (field, field[1:], rows, rows))(
        velocity, canopy, cotangent
    )
    y1, y2 = exchange(m1, m2, GY)
    m1, m2 = call(layer_kernel, (layers, layers))(velocity, direct, y1, y2)
    x1, x2 = exchange(m1, m2, GX)
    selection = jnp.asarray(selector())
    weight_in, weight_out, selection = call(
        weights_in_kernel,
        (weight_in, weight_out, selection),
        (pltpu.SemaphoreType.DMA((3,)),),
        "ahhh",
    )(m1, weight_in, weight_out, selection)
    hidden_type = jax.ShapeDtypeStruct((128, 512), BF16)
    keep, send, ext, hidden, pre_low = call(
        main_kernel,
        ((HALF, 128), (HALF, 128), (36, 24, 128), hidden_type, hidden_type),
        ((24, 24, 128), (648, 128), (384, 128), (FLAT, 128)),
        None,
        24,
    )(
        velocity, direct, y1, y2, x1, x2,
        weight_in, bias_in[None], weight_out, selection,
    )
    got = lax.ppermute(send, "core", swap)
    nv, vg, m1, m2, ylow, yhigh = call(
        cells_kernel,
        (field, field, layers, layers, rows, rows),
        (
            (648, 128),
            (384, 128),
            (144, 768),
            (192, 512),
            (18, 24, 128),
            (24, 32, 128),
        ),
        None,
        16,
    )(direct, ext, hidden, pre_low, weight_in, weight_out, bias_out[None], selection)

    x1, x2 = exchange(m1, m2, GX)
    (half,) = call(add_kernel, (keep.shape,), (), "vva", 16)(keep, got, x1)
    half = half.reshape(parts, count, 128)
    got = lax.all_to_all(half, across, 0, 0)
    m1, m2 = call(side_kernel, (rows, rows), (rows, rows))(x1, x2, ylow, yhigh)
    cut = (depth, 1, short * 128)
    (part,) = call(across_kernel, (cut,), ((short * depth, 128),), "va", 12)(got, x2)
    got = lax.all_to_all(part, along, 0, 0)
    y1, y2 = exchange(m1, m2, GY)
    (part,) = call(along_kernel, (cut,), (), "vaa", 12)(got, y1, y2)
    got = lax.all_to_all(part, along, 0, 0)
    (half,) = call(spread_kernel, (half.shape,), ((short * depth, 128),), "v", 12)(got)
    mine = lax.all_to_all(half, across, 0, 0).reshape(HALF, 128)
    new_velocity, velocity_grad = call(
        end_kernel, (field, field), ((4, 16, 128),), None, 12
    )(nv, vg, factor, x1, x2, y1, y2)
    other = lax.ppermute(mine, "core", swap)
    blocks = 128 * lax.axis_size(GX) * lax.axis_size(GY)
    scale = float(blocks) ** -0.5
    weight_in_grad, bias_in_grad, weight_out_grad, bias_out_grad = call(
        lambda *refs: weights_kernel(scale, *refs), ((648, 512), (512,), (512, 384), (384,))
    )(mine, other)
    return (
        new_velocity,
        velocity_grad,
        weight_in_grad,
        bias_in_grad,
        weight_out_grad,
        bias_out_grad,
    )


def solution(mesh):
    if mesh.devices.size == 512:
        mesh = Mesh(mesh.devices.reshape(4, 4, 4, 4, 2), GX + GY)
    placed = (
        P(None, GX, GY, None),
        P(GX, GY, None),
        P(),
        P(),
        P(),
        P(),
        P(None, GX, GY, None),
    )
    return jax.shard_map(
        on_device,
        mesh=mesh,
        in_specs=placed,
        out_specs=(P(None, GX, GY, None), P(None, GX, GY, None), P(), P(), P(), P()),
        check_vma=False,
    )
```

```python
import functools

import jax
import jax.numpy as jnp
import numpy as np
from jax import lax
from jax.experimental import pallas as pl
from jax.experimental.pallas import tpu as pltpu
from jax.sharding import Mesh, PartitionSpec as P

time_step = 0.25
viscosity = 0.2
penalty_eta = 0.05

GX = ("zh", "x", "y")
GY = ("zl", "core")
FLAT = 4352
HALF = FLAT // 2
WIN_ROWS = 648
WOUT_BASE = 4 * WIN_ROWS
BIAS_BASE = WOUT_BASE + 3 * 512
F32 = jnp.float32
BF16 = jnp.bfloat16


def selector():
    table = np.zeros((4, 128, 6, 4, 32), np.float32)
    for offset in range(6):
        for block in range(32):
            z = 4 * block + offset - 1
            if 0 <= z < 128:
                for row in range(4):
                    table[row, z, offset, row, block] = 1.0
    return table.reshape(512, 768).astype(jnp.bfloat16)


def z_next(field):
    lane = lax.broadcasted_iota(jnp.int32, field.shape, field.ndim - 1)
    return jnp.where(lane < 127, pltpu.roll(field, 127, field.ndim - 1), 0.0)


def z_before(field):
    lane = lax.broadcasted_iota(jnp.int32, field.shape, field.ndim - 1)
    return jnp.where(lane > 0, pltpu.roll(field, 1, field.ndim - 1), 0.0)


def split(value):
    high = value.astype(BF16)
    low = (value - high.astype(F32)).astype(BF16)
    return high, low


def dot(left, right, left_dim, right_dim):
    return lax.dot_general(
        left, right, (((left_dim,), (right_dim,)), ((), ())), preferred_element_type=F32
    )


def damping(canopy):
    return 1.0 + time_step * canopy.astype(F32) / penalty_eta


def start_kernel(v_ref, canopy_ref, cot_ref, direct_ref, factor_ref, m1_ref, m2_ref):
    core = lax.axis_index("core")
    factor = damping(canopy_ref[...])
    factor_ref[...] = factor
    for i in range(3):
        direct_ref[i] = cot_ref[i].astype(F32) / factor
    for out, row in ((m1_ref, 15 * (1 - core)), (m2_ref, 15 * core)):
        for i in range(3):
            for x in range(4):
                out[pl.ds(i * 4 + x, 1), :] = v_ref[i, x, pl.ds(row, 1), :]
                out[pl.ds(12 + i * 4 + x, 1), :] = (
                    direct_ref[i, x, pl.ds(row, 1), :] * time_step
                )


def weights_in_kernel(after, win_hbm, wout_hbm, sel_hbm, win_ref, wout_ref, sel_ref, sems):
    copies = [
        pltpu.make_async_copy(source, target, sems.at[i])
        for i, (source, target) in enumerate(
            ((win_hbm, win_ref), (wout_hbm, wout_ref), (sel_hbm, sel_ref))
        )
    ]
    for copy in copies:
        copy.start()
    for copy in copies:
        copy.wait()


def layer_kernel(v_ref, direct_ref, r1_ref, r2_ref, m1_ref, m2_ref):
    core = lax.axis_index("core")
    parity = lax.rem(lax.axis_index("y"), 2)
    for out, x in ((m1_ref, 3 * (1 - parity)), (m2_ref, 3 * parity)):
        for k in range(6):
            out[k, 16:24, :] = jnp.zeros((8, 128), F32)
            if k < 3:
                out[k, 1:17, :] = v_ref[k, x]
            else:
                out[k, 1:17, :] = direct_ref[k - 3, x] * time_step
            row1 = r1_ref[pl.ds(k * 4 + x, 1), :]
            row2 = r2_ref[pl.ds(k * 4 + x, 1), :]
            out[k, 0:1, :] = jnp.where(core == 0, row2, row1)
            out[k, 17:18, :] = jnp.where(core == 0, row1, row2)


def shifted(ext):
    def at(k, dx, dy):
        return ext[k * 6 + 1 + dx : k * 6 + 5 + dx, 1 + dy : 17 + dy, :]

    return at


def slopes(at):
    grad_x = [(at(3 + i, 1, 0) - at(3 + i, -1, 0)) * 0.5 for i in range(3)]
    grad_y = [(at(3 + i, 0, 1) - at(3 + i, 0, -1)) * 0.5 for i in range(3)]
    grad_z = [(z_next(at(3 + i, 0, 0)) - z_before(at(3 + i, 0, 0))) * 0.5 for i in range(3)]
    return grad_x, grad_y, grad_z


def main_kernel(
    v_ref, direct_ref, r1_ref, r2_ref, x1_ref, x2_ref,
    win_ref, bin_ref, wout_ref, sel_ref,
    keep_ref, send_ref, ext, hidden_ref, pre_low_ref, sgrad, cols, rows, flat,
):
    core = lax.axis_index("core")
    parity = lax.rem(lax.axis_index("y"), 2)

    for k in range(6):
        ext[k * 6] = jnp.where(parity == 0, x2_ref[k], x1_ref[k])
        ext[k * 6 + 5] = jnp.where(parity == 0, x1_ref[k], x2_ref[k])
        for x in range(4):
            spot = k * 6 + 1 + x
            ext[spot, 16:24, :] = jnp.zeros((8, 128), F32)
            ext[spot, 1:17, :] = v_ref[k, x] if k < 3 else direct_ref[k - 3, x] * time_step
            row1 = r1_ref[k * 4 + x : k * 4 + x + 1, :]
            row2 = r2_ref[k * 4 + x : k * 4 + x + 1, :]
            ext[spot, 0:1, :] = jnp.where(core == 0, row2, row1)
            ext[spot, 17:18, :] = jnp.where(core == 0, row1, row2)

    grad_x, grad_y, grad_z = slopes(shifted(ext))
    stress_grad = (
        grad_x[0],
        grad_y[1],
        grad_z[2],
        grad_y[0] + grad_x[1],
        grad_z[0] + grad_x[2],
        grad_z[1] + grad_y[2],
    )
    sgrad[:, 16:24, :] = jnp.zeros((24, 8, 128), F32)
    for s in range(6):
        sgrad[s * 4 : s * 4 + 4, 0:16, :] = -stress_grad[s]
    selection = sel_ref[...]
    inner = sel_ref[:, 128:640]

    parts = [sgrad[:, 4 * b : 4 * b + 8, :].reshape(192, 128) for b in range(4)]
    high, low = split(jnp.concatenate(parts, axis=1))
    picked = dot(high, inner, 1, 0) + dot(low, inner, 1, 0)
    for sa in range(24):
        for c in range(4):
            rows[pl.ds(sa * 16 + c, 4, stride=4), :] = picked[
                sa * 8 : sa * 8 + 4, c * 128 : c * 128 + 128
            ]
    rows_t = rows[...].T
    rows_low = rows_t.astype(BF16)
    bias_out_sum = jnp.sum(rows_t, axis=0, keepdims=True)

    parts = [
        ext[0:18, 4 * b : 4 * b + 8, :].reshape(144, 128).astype(BF16) for b in range(4)
    ]
    picked = dot(jnp.concatenate(parts, axis=1), selection, 1, 0)
    for g in range(18):
        for z in range(6):
            cols[pl.ds(g * 36 + z, 6, stride=6), :] = picked[
                g * 8 : g * 8 + 6, z * 128 : z * 128 + 128
            ]
    columns = cols[...].astype(BF16)

    pre_act = dot(columns, win_ref[...], 0, 0) + bin_ref[...]
    sigmoid_pre = jax.nn.sigmoid(pre_act)
    hidden = (pre_act * sigmoid_pre).astype(BF16)
    hidden_grad = dot(rows_low, wout_ref[...], 1, 1)
    pre_grad = hidden_grad * (sigmoid_pre * (1.0 + pre_act * (1.0 - sigmoid_pre)))
    pre_low = pre_grad.astype(BF16)
    hidden_ref[...] = hidden
    pre_low_ref[...] = pre_low
    bias_in_sum = jnp.sum(pre_grad, axis=0, keepdims=True)

    weight_in_sum = dot(columns, pre_low, 1, 0)
    for q in range(4):
        flat[q * WIN_ROWS : (q + 1) * WIN_ROWS, :] = weight_in_sum[:, q * 128 : q * 128 + 128]
    weight_out_sum = dot(hidden, rows_low, 0, 0)
    for q in range(3):
        flat[WOUT_BASE + q * 512 : WOUT_BASE + q * 512 + 512, :] = weight_out_sum[
            :, q * 128 : q * 128 + 128
        ]
    flat[BIAS_BASE:FLAT, :] = jnp.zeros((FLAT - BIAS_BASE, 128), F32)
    for q in range(4):
        flat[BIAS_BASE + q : BIAS_BASE + q + 1, :] = bias_in_sum[:, q * 128 : q * 128 + 128]
    for q in range(3):
        flat[BIAS_BASE + 4 + q : BIAS_BASE + 5 + q, :] = bias_out_sum[:, q * 128 : q * 128 + 128]
    keep_ref[...] = flat[pl.ds(pl.multiple_of(core * HALF, 8), HALF), :]
    send_ref[...] = flat[pl.ds(pl.multiple_of((1 - core) * HALF, 8), HALF), :]


def cells_kernel(
    direct_ref, ext, hidden_ref, pre_low_ref, win_ref, wout_ref, bout_ref, sel_ref,
    nv_ref, vg_ref, m1_ref, m2_ref, ylow_ref, yhigh_ref,
    cgrad, rows, cpad, opad, ghost, tau,
):
    parity = lax.rem(lax.axis_index("y"), 2)
    at = shifted(ext)
    grad_x, grad_y, grad_z = slopes(at)
    selection = sel_ref[...]
    inner = sel_ref[:, 128:640]

    def laplace(k):
        middle = at(k, 0, 0)
        total = at(k, 1, 0) + at(k, -1, 0) + at(k, 0, 1) + at(k, 0, -1)
        return total + z_next(middle) + z_before(middle) - 6.0 * middle

    for j in range(3):
        velocity = [at(i, 0, 0) for i in range(3)]
        slope = (grad_x, grad_y, grad_z)[j]
        total = direct_ref[j] + viscosity * laplace(3 + j)
        total = total + slope[0] * velocity[0] + slope[1] * velocity[1] + slope[2] * velocity[2]
        total = total + grad_x[j] * velocity[0] + grad_y[j] * velocity[1] + grad_z[j] * velocity[2]
        vg_ref[j] = total

    cgrad[...] = dot(win_ref[...], pre_low_ref[...], 1, 1)
    for g in range(18):
        for z in range(6):
            cpad[g * 8 : g * 8 + 6, z * 128 : z * 128 + 128] = cgrad[
                pl.ds(g * 36 + z, 6, stride=6), :
            ]
            cpad[g * 8 + 6 : g * 8 + 8, z * 128 : z * 128 + 128] = jnp.zeros((2, 128), F32)
    high, low = split(cpad[...])
    spread = dot(high, selection, 1, 1) + dot(low, selection, 1, 1)
    spread = spread.reshape(18, 8, 512)
    ghost[...] = jnp.zeros((18, 24, 128), F32)
    for b in range(4):
        ghost[:, 4 * b : 4 * b + 8, :] += spread[:, :, b * 128 : b * 128 + 128]
    for j in range(3):
        vg_ref[j] += ghost[j * 6 + 1 : j * 6 + 5, 1:17, :]

    outputs = dot(hidden_ref[...], wout_ref[...], 1, 0) + bout_ref[...]
    rows[...] = outputs.T
    for sa in range(24):
        for c in range(4):
            opad[sa * 8 : sa * 8 + 4, c * 128 : c * 128 + 128] = rows[
                pl.ds(sa * 16 + c, 4, stride=4), :
            ]
            opad[sa * 8 + 4 : sa * 8 + 8, c * 128 : c * 128 + 128] = jnp.zeros((4, 128), F32)
    high, low = split(opad[...])
    spread = dot(high, inner, 1, 1) + dot(low, inner, 1, 1)
    spread = spread.reshape(24, 8, 512)
    tau[:, 0:8, :] = jnp.zeros((24, 8, 128), F32)
    tau[:, 24:32, :] = jnp.zeros((24, 8, 128), F32)
    for b in range(4):
        tau[:, 8 + 4 * b : 12 + 4 * b, :] = spread[:, 0:4, b * 128 : b * 128 + 128]

    blank = jnp.zeros((1, 16, 128), F32)
    for i, (along_x, along_y, along_z) in enumerate(((0, 3, 4), (3, 1, 5), (4, 5, 2))):
        inside = tau[along_x * 4 : along_x * 4 + 4, 8:24, :]
        force = jnp.concatenate([inside[1:4], blank]) - jnp.concatenate([blank, inside[0:3]])
        force = force + tau[along_y * 4 : along_y * 4 + 4, 9:25, :]
        force = force - tau[along_y * 4 : along_y * 4 + 4, 7:23, :]
        inside = tau[along_z * 4 : along_z * 4 + 4, 8:24, :]
        force = (force + z_next(inside) - z_before(inside)) * 0.5
        product = at(2, 0, 0) * at(i, 0, 0)
        flow = at(0, 1, 0) * at(i, 1, 0) - at(0, -1, 0) * at(i, -1, 0)
        flow = flow + at(1, 0, 1) * at(i, 0, 1) - at(1, 0, -1) * at(i, 0, -1)
        flow = (flow + z_next(product) - z_before(product)) * 0.5
        nv_ref[i] = at(i, 0, 0) + time_step * (viscosity * laplace(i) - flow + force)

    for out, side in ((m1_ref, 1 - parity), (m2_ref, parity)):
        for j, s in enumerate((0, 3, 4)):
            out[j, 0:16, :] = tau[s * 4 + 3 * side, 8:24, :]
            out[j, 16:24, :] = jnp.zeros((8, 128), F32)
            out[3 + j] = ghost[j * 6 + 5 * side]
    for j, s in enumerate((3, 1, 5)):
        for x in range(4):
            spot = j * 4 + x
            ylow_ref[spot : spot + 1, :] = tau[s * 4 + x, 8:9, :]
            yhigh_ref[spot : spot + 1, :] = tau[s * 4 + x, 23:24, :]
            ylow_ref[12 + spot : 13 + spot, :] = ghost[j * 6 + 1 + x, 0:1, :]
            yhigh_ref[12 + spot : 13 + spot, :] = ghost[j * 6 + 1 + x, 17:18, :]


def side_kernel(x1_ref, x2_ref, ylow_ref, yhigh_ref, m1_ref, m2_ref, low, high):
    core = lax.axis_index("core")
    parity = lax.rem(lax.axis_index("y"), 2)
    low[...] = ylow_ref[...]
    high[...] = yhigh_ref[...]
    for j in range(3):
        from_low = jnp.where(parity == 0, x2_ref[3 + j], x1_ref[3 + j])
        from_high = jnp.where(parity == 0, x1_ref[3 + j], x2_ref[3 + j])
        first, last = 12 + j * 4, 15 + j * 4
        low[first : first + 1, :] += from_low[0:1]
        low[last : last + 1, :] += from_high[0:1]
        high[first : first + 1, :] += from_low[17:18]
        high[last : last + 1, :] += from_high[17:18]
    m1_ref[...] = jnp.where(core == 0, high[...], low[...])
    m2_ref[...] = jnp.where(core == 0, low[...], high[...])


def end_kernel(
    nv_ref, vg_ref, factor_ref, x1_ref, x2_ref, y1_ref, y2_ref, new_ref, grad_ref, part
):
    core = lax.axis_index("core")
    parity = lax.rem(lax.axis_index("y"), 2)
    factor = factor_ref[...]
    y_low = jnp.where(core == 0, y2_ref[...], y1_ref[...])
    y_high = jnp.where(core == 0, y1_ref[...], y2_ref[...])
    step = time_step * 0.5
    for i in range(3):
        part[...] = nv_ref[i]
        part[0] -= step * jnp.where(parity == 0, x2_ref[i, 0:16, :], x1_ref[i, 0:16, :])
        part[3] += step * jnp.where(parity == 0, x1_ref[i, 0:16, :], x2_ref[i, 0:16, :])
        for x in range(4):
            spot = i * 4 + x
            part[x, 0:1, :] -= step * y_low[spot : spot + 1]
            part[x, 15:16, :] += step * y_high[spot : spot + 1]
        new_ref[i] = part[...] / factor
        part[...] = vg_ref[i]
        part[0] += jnp.where(parity == 0, x2_ref[3 + i, 1:17, :], x1_ref[3 + i, 1:17, :])
        part[3] += jnp.where(parity == 0, x1_ref[3 + i, 1:17, :], x2_ref[3 + i, 1:17, :])
        for x in range(4):
            spot = 12 + i * 4 + x
            part[x, 0:1, :] += y_low[spot : spot + 1]
            part[x, 15:16, :] += y_high[spot : spot + 1]
        grad_ref[i] = part[...]


def weights_kernel(mine_ref, other_ref, win_ref, bin_ref, wout_ref, bout_ref):
    core = lax.axis_index("core")

    def put(out, lanes, start, count, first, second):
        done = 0
        while done < count:
            spot = start + done
            source, spot, room = (
                (first, spot, HALF - spot) if spot < HALF else (second, spot - HALF, count)
            )
            size = min(count - done, room)
            out[done : done + size, lanes * 128 : lanes * 128 + 128] = source[
                spot : spot + size, :
            ]
            done += size

    def write(first, second):
        for q in range(4):
            put(win_ref, q, q * WIN_ROWS, WIN_ROWS, first, second)
            row = second[BIAS_BASE + q - HALF, :]
            bin_ref[q * 128 : q * 128 + 128] = row
        for q in range(3):
            put(wout_ref, q, WOUT_BASE + q * 512, 512, first, second)
            row = second[BIAS_BASE + 4 + q - HALF, :]
            bout_ref[q * 128 : q * 128 + 128] = row

    @pl.when(core == 0)
    def _():
        write(mine_ref, other_ref)

    @pl.when(core == 1)
    def _():
        write(other_ref, mine_ref)


def add_kernel(first_ref, second_ref, after, out_ref):
    out_ref[...] = first_ref[...] + second_ref[...]


def across_kernel(got_ref, *rest):
    out_ref, part = rest[-2:]
    count = got_ref.shape[1]
    depth, _, width = out_ref.shape
    short = width // 128
    part[...] = jnp.zeros(part.shape, F32)
    part[0:count, :] = jnp.sum(got_ref[...], axis=0)
    for i in range(depth):
        for j in range(short):
            out_ref[i, 0:1, j * 128 : j * 128 + 128] = part[i * short + j : i * short + j + 1, :]


def along_kernel(scale, got_ref, *rest):
    out_ref = rest[-1]
    total = jnp.sum(got_ref[...], axis=0, keepdims=True) * scale
    out_ref[...] = jnp.broadcast_to(total, out_ref.shape)


def spread_kernel(got_ref, *rest):
    out_ref, part = rest[-2:]
    depth, _, width = got_ref.shape
    short = width // 128
    count = out_ref.shape[1]
    for i in range(depth):
        for j in range(short):
            part[i * short + j : i * short + j + 1, :] = got_ref[i, 0:1, j * 128 : j * 128 + 128]
    for i in range(out_ref.shape[0]):
        out_ref[i] = part[0:count, :]


def call(kernel, outs, scratch=(), places=None, room=12):
    spaces = {"v": pltpu.VMEM, "h": pltpu.HBM, "a": pl.ANY}
    specs = {}
    if places is not None:
        specs["in_specs"] = [pl.BlockSpec(memory_space=spaces[place]) for place in places]
    return pl.pallas_call(
        kernel,
        out_shape=[
            out if hasattr(out, "dtype") else jax.ShapeDtypeStruct(out, F32) for out in outs
        ],
        scratch_shapes=[
            pltpu.VMEM(shape, F32) if isinstance(shape, tuple) else shape for shape in scratch
        ],
        compiler_params=pltpu.CompilerParams(vmem_limit_bytes=room * 1024 * 1024),
        **specs,
    )


def pairs(axes):
    count = lax.axis_size(axes)
    inner = [(i, i ^ 1) for i in range(count)]
    outer = [(i, (i + 1) % count if i % 2 else (i - 1) % count) for i in range(count)]
    return inner, outer


def exchange(first, second, axes):
    inner, outer = pairs(axes)
    return lax.ppermute(first, axes, inner), lax.ppermute(second, axes, outer)


def on_device(velocity, canopy, weight_in, bias_in, weight_out, bias_out, cotangent):
    field = (3, 4, 16, 128)
    rows = (24, 128)
    layers = (6, 24, 128)
    across, along = ("x", "y"), ("zh", "zl")
    swap = [(0, 1), (1, 0)]
    parts = lax.axis_size(across)
    depth = lax.axis_size(along)
    count = HALF // parts
    short = -(-count // depth)

    direct, factor, m1, m2 = call(start_kernel, (field, field[1:], rows, rows))(
        velocity, canopy, cotangent
    )
    y1, y2 = exchange(m1, m2, GY)
    m1, m2 = call(layer_kernel, (layers, layers))(velocity, direct, y1, y2)
    x1, x2 = exchange(m1, m2, GX)
    selection = jnp.asarray(selector())
    weight_in, weight_out, selection = call(
        weights_in_kernel,
        (weight_in, weight_out, selection),
        (pltpu.SemaphoreType.DMA((3,)),),
        "ahhh",
    )(m1, weight_in, weight_out, selection)
    hidden_type = jax.ShapeDtypeStruct((128, 512), BF16)
    keep, send, ext, hidden, pre_low = call(
        main_kernel,
        ((HALF, 128), (HALF, 128), (36, 24, 128), hidden_type, hidden_type),
        ((24, 24, 128), (648, 128), (384, 128), (FLAT, 128)),
        None,
        24,
    )(
        velocity, direct, y1, y2, x1, x2,
        weight_in, bias_in[None], weight_out, selection,
    )
    got = lax.ppermute(send, "core", swap)
    nv, vg, m1, m2, ylow, yhigh = call(
        cells_kernel,
        (field, field, layers, layers, rows, rows),
        (
            (648, 128),
            (384, 128),
            (144, 768),
            (192, 512),
            (18, 24, 128),
            (24, 32, 128),
        ),
        None,
        16,
    )(direct, ext, hidden, pre_low, weight_in, weight_out, bias_out[None], selection)

    inner, outer = pairs(GX)
    x2 = lax.ppermute(m2, GX, outer)
    x1 = lax.ppermute(m1, GX, inner)
    (half,) = call(add_kernel, (keep.shape,), (), "vva", 16)(keep, got, ylow)
    half = half.reshape(parts, count, 128)
    got = lax.all_to_all(half, across, 0, 0)
    m1, m2 = call(side_kernel, (rows, rows), (rows, rows))(x1, x2, ylow, yhigh)
    cut = (depth, 1, short * 128)
    (part,) = call(across_kernel, (cut,), ((short * depth, 128),), "vaa", 12)(got, x2, x1)
    got = lax.all_to_all(part, along, 0, 0)
    y1, y2 = exchange(m1, m2, GY)
    blocks = 128 * lax.axis_size(GX) * lax.axis_size(GY)
    scaled = functools.partial(along_kernel, float(blocks) ** -0.5)
    (part,) = call(scaled, (cut,), (), "vaa", 12)(got, y1, y2)
    got = lax.all_to_all(part, along, 0, 0)
    (half,) = call(spread_kernel, (half.shape,), ((short * depth, 128),), "v", 12)(got)
    mine = lax.all_to_all(half, across, 0, 0).reshape(HALF, 128)
    new_velocity, velocity_grad = call(
        end_kernel, (field, field), ((4, 16, 128),), None, 12
    )(nv, vg, factor, x1, x2, y1, y2)
    other = lax.ppermute(mine, "core", swap)
    weight_in_grad, bias_in_grad, weight_out_grad, bias_out_grad = call(
        weights_kernel, ((648, 512), (512,), (512, 384), (384,))
    )(mine, other)
    return (
        new_velocity,
        velocity_grad,
        weight_in_grad,
        bias_in_grad,
        weight_out_grad,
        bias_out_grad,
    )


def solution(mesh):
    if mesh.devices.size == 512:
        mesh = Mesh(mesh.devices.reshape(4, 4, 4, 4, 2), GX + GY)
    placed = (
        P(None, GX, GY, None),
        P(GX, GY, None),
        P(),
        P(),
        P(),
        P(),
        P(None, GX, GY, None),
    )
    return jax.shard_map(
        on_device,
        mesh=mesh,
        in_specs=placed,
        out_specs=(P(None, GX, GY, None), P(None, GX, GY, None), P(), P(), P(), P()),
        check_vma=False,
    )
```

```python
import functools

import jax
import jax.numpy as jnp
import numpy as np
from jax import lax
from jax.experimental import pallas as pl
from jax.experimental.pallas import tpu as pltpu
from jax.sharding import Mesh, PartitionSpec as P

time_step = 0.25
viscosity = 0.2
penalty_eta = 0.05

GX = ("zh", "x", "y")
GY = ("zl", "core")
FLAT = 4352
HALF = FLAT // 2
WIN_ROWS = 648
WOUT_BASE = 4 * WIN_ROWS
BIAS_BASE = WOUT_BASE + 3 * 512
F32 = jnp.float32
BF16 = jnp.bfloat16


def selector():
    table = np.zeros((4, 128, 6, 4, 32), np.float32)
    for offset in range(6):
        for block in range(32):
            z = 4 * block + offset - 1
            if 0 <= z < 128:
                for row in range(4):
                    table[row, z, offset, row, block] = 1.0
    return table.reshape(512, 768).astype(jnp.bfloat16)


def z_next(field):
    lane = lax.broadcasted_iota(jnp.int32, field.shape, field.ndim - 1)
    return jnp.where(lane < 127, pltpu.roll(field, 127, field.ndim - 1), 0.0)


def z_before(field):
    lane = lax.broadcasted_iota(jnp.int32, field.shape, field.ndim - 1)
    return jnp.where(lane > 0, pltpu.roll(field, 1, field.ndim - 1), 0.0)


def split(value):
    high = value.astype(BF16)
    low = (value - high.astype(F32)).astype(BF16)
    return high, low


def dot(left, right, left_dim, right_dim):
    return lax.dot_general(
        left, right, (((left_dim,), (right_dim,)), ((), ())), preferred_element_type=F32
    )


def damping(canopy):
    return 1.0 + time_step * canopy.astype(F32) / penalty_eta


def start_kernel(v_ref, canopy_ref, cot_ref, direct_ref, factor_ref, m1_ref, m2_ref):
    core = lax.axis_index("core")
    factor = damping(canopy_ref[...])
    factor_ref[...] = factor
    for i in range(3):
        direct_ref[i] = cot_ref[i].astype(F32) / factor
    for out, row in ((m1_ref, 15 * (1 - core)), (m2_ref, 15 * core)):
        for i in range(3):
            for x in range(4):
                out[pl.ds(i * 4 + x, 1), :] = v_ref[i, x, pl.ds(row, 1), :]
                out[pl.ds(12 + i * 4 + x, 1), :] = (
                    direct_ref[i, x, pl.ds(row, 1), :] * time_step
                )


def weights_in_kernel(after, win_hbm, wout_hbm, sel_hbm, win_ref, wout_ref, sel_ref, sems):
    copies = [
        pltpu.make_async_copy(source, target, sems.at[i])
        for i, (source, target) in enumerate(
            ((win_hbm, win_ref), (wout_hbm, wout_ref), (sel_hbm, sel_ref))
        )
    ]
    for copy in copies:
        copy.start()
    for copy in copies:
        copy.wait()


def layer_kernel(v_ref, direct_ref, r1_ref, r2_ref, m1_ref, m2_ref):
    core = lax.axis_index("core")
    parity = lax.rem(lax.axis_index("y"), 2)
    for out, x in ((m1_ref, 3 * (1 - parity)), (m2_ref, 3 * parity)):
        for k in range(6):
            out[k, 16:24, :] = jnp.zeros((8, 128), F32)
            if k < 3:
                out[k, 1:17, :] = v_ref[k, x]
            else:
                out[k, 1:17, :] = direct_ref[k - 3, x] * time_step
            row1 = r1_ref[pl.ds(k * 4 + x, 1), :]
            row2 = r2_ref[pl.ds(k * 4 + x, 1), :]
            out[k, 0:1, :] = jnp.where(core == 0, row2, row1)
            out[k, 17:18, :] = jnp.where(core == 0, row1, row2)


def shifted(ext):
    def at(k, dx, dy):
        return ext[k * 6 + 1 + dx : k * 6 + 5 + dx, 1 + dy : 17 + dy, :]

    return at


def slopes(at):
    grad_x = [(at(3 + i, 1, 0) - at(3 + i, -1, 0)) * 0.5 for i in range(3)]
    grad_y = [(at(3 + i, 0, 1) - at(3 + i, 0, -1)) * 0.5 for i in range(3)]
    grad_z = [(z_next(at(3 + i, 0, 0)) - z_before(at(3 + i, 0, 0))) * 0.5 for i in range(3)]
    return grad_x, grad_y, grad_z


def main_kernel(
    v_ref, direct_ref, r1_ref, r2_ref, x1_ref, x2_ref,
    win_ref, bin_ref, wout_ref, sel_ref,
    keep_ref, send_ref, ext, hidden_ref, pre_low_ref, sgrad, cols, rows, flat,
):
    core = lax.axis_index("core")
    parity = lax.rem(lax.axis_index("y"), 2)

    for k in range(6):
        ext[k * 6] = jnp.where(parity == 0, x2_ref[k], x1_ref[k])
        ext[k * 6 + 5] = jnp.where(parity == 0, x1_ref[k], x2_ref[k])
        for x in range(4):
            spot = k * 6 + 1 + x
            ext[spot, 16:24, :] = jnp.zeros((8, 128), F32)
            ext[spot, 1:17, :] = v_ref[k, x] if k < 3 else direct_ref[k - 3, x] * time_step
            row1 = r1_ref[k * 4 + x : k * 4 + x + 1, :]
            row2 = r2_ref[k * 4 + x : k * 4 + x + 1, :]
            ext[spot, 0:1, :] = jnp.where(core == 0, row2, row1)
            ext[spot, 17:18, :] = jnp.where(core == 0, row1, row2)

    grad_x, grad_y, grad_z = slopes(shifted(ext))
    stress_grad = (
        grad_x[0],
        grad_y[1],
        grad_z[2],
        grad_y[0] + grad_x[1],
        grad_z[0] + grad_x[2],
        grad_z[1] + grad_y[2],
    )
    sgrad[:, 16:24, :] = jnp.zeros((24, 8, 128), F32)
    for s in range(6):
        sgrad[s * 4 : s * 4 + 4, 0:16, :] = -stress_grad[s]
    selection = sel_ref[...]
    inner = sel_ref[:, 128:640]

    parts = [sgrad[:, 4 * b : 4 * b + 8, :].reshape(192, 128) for b in range(4)]
    high, low = split(jnp.concatenate(parts, axis=1))
    picked = dot(high, inner, 1, 0) + dot(low, inner, 1, 0)
    for sa in range(24):
        for c in range(4):
            rows[pl.ds(sa * 16 + c, 4, stride=4), :] = picked[
                sa * 8 : sa * 8 + 4, c * 128 : c * 128 + 128
            ]
    rows_t = rows[...].T
    rows_low = rows_t.astype(BF16)
    bias_out_sum = jnp.sum(rows_t, axis=0, keepdims=True)

    parts = [
        ext[0:18, 4 * b : 4 * b + 8, :].reshape(144, 128).astype(BF16) for b in range(4)
    ]
    picked = dot(jnp.concatenate(parts, axis=1), selection, 1, 0)
    for g in range(18):
        for z in range(6):
            cols[pl.ds(g * 36 + z, 6, stride=6), :] = picked[
                g * 8 : g * 8 + 6, z * 128 : z * 128 + 128
            ]
    columns = cols[...].astype(BF16)

    pre_act = dot(columns, win_ref[...], 0, 0) + bin_ref[...]
    sigmoid_pre = jax.nn.sigmoid(pre_act)
    hidden = (pre_act * sigmoid_pre).astype(BF16)
    hidden_grad = dot(rows_low, wout_ref[...], 1, 1)
    pre_grad = hidden_grad * (sigmoid_pre * (1.0 + pre_act * (1.0 - sigmoid_pre)))
    pre_low = pre_grad.astype(BF16)
    hidden_ref[...] = hidden
    pre_low_ref[...] = pre_low
    bias_in_sum = jnp.sum(pre_grad, axis=0, keepdims=True)

    weight_in_sum = dot(columns, pre_low, 1, 0)
    for q in range(4):
        flat[q * WIN_ROWS : (q + 1) * WIN_ROWS, :] = weight_in_sum[:, q * 128 : q * 128 + 128]
    weight_out_sum = dot(hidden, rows_low, 0, 0)
    for q in range(3):
        flat[WOUT_BASE + q * 512 : WOUT_BASE + q * 512 + 512, :] = weight_out_sum[
            :, q * 128 : q * 128 + 128
        ]
    flat[BIAS_BASE:FLAT, :] = jnp.zeros((FLAT - BIAS_BASE, 128), F32)
    for q in range(4):
        flat[BIAS_BASE + q : BIAS_BASE + q + 1, :] = bias_in_sum[:, q * 128 : q * 128 + 128]
    for q in range(3):
        flat[BIAS_BASE + 4 + q : BIAS_BASE + 5 + q, :] = bias_out_sum[:, q * 128 : q * 128 + 128]
    keep_ref[...] = flat[pl.ds(pl.multiple_of(core * HALF, 8), HALF), :]
    send_ref[...] = flat[pl.ds(pl.multiple_of((1 - core) * HALF, 8), HALF), :]


def cells_kernel(
    direct_ref, ext, hidden_ref, pre_low_ref, win_ref, wout_ref, bout_ref, sel_ref,
    nv_ref, vg_ref, m1_ref, m2_ref, ylow_ref, yhigh_ref,
    cgrad, rows, cpad, opad, ghost, tau,
):
    parity = lax.rem(lax.axis_index("y"), 2)
    at = shifted(ext)
    grad_x, grad_y, grad_z = slopes(at)
    selection = sel_ref[...]
    inner = sel_ref[:, 128:640]

    def laplace(k):
        middle = at(k, 0, 0)
        total = at(k, 1, 0) + at(k, -1, 0) + at(k, 0, 1) + at(k, 0, -1)
        return total + z_next(middle) + z_before(middle) - 6.0 * middle

    for j in range(3):
        velocity = [at(i, 0, 0) for i in range(3)]
        slope = (grad_x, grad_y, grad_z)[j]
        total = direct_ref[j] + viscosity * laplace(3 + j)
        total = total + slope[0] * velocity[0] + slope[1] * velocity[1] + slope[2] * velocity[2]
        total = total + grad_x[j] * velocity[0] + grad_y[j] * velocity[1] + grad_z[j] * velocity[2]
        vg_ref[j] = total

    cgrad[...] = dot(win_ref[...], pre_low_ref[...], 1, 1)
    for g in range(18):
        for z in range(6):
            cpad[g * 8 : g * 8 + 6, z * 128 : z * 128 + 128] = cgrad[
                pl.ds(g * 36 + z, 6, stride=6), :
            ]
            cpad[g * 8 + 6 : g * 8 + 8, z * 128 : z * 128 + 128] = jnp.zeros((2, 128), F32)
    high, low = split(cpad[...])
    spread = dot(high, selection, 1, 1) + dot(low, selection, 1, 1)
    spread = spread.reshape(18, 8, 512)
    ghost[...] = jnp.zeros((18, 24, 128), F32)
    for b in range(4):
        ghost[:, 4 * b : 4 * b + 8, :] += spread[:, :, b * 128 : b * 128 + 128]
    for j in range(3):
        vg_ref[j] += ghost[j * 6 + 1 : j * 6 + 5, 1:17, :]

    outputs = dot(hidden_ref[...], wout_ref[...], 1, 0) + bout_ref[...]
    rows[...] = outputs.T
    for sa in range(24):
        for c in range(4):
            opad[sa * 8 : sa * 8 + 4, c * 128 : c * 128 + 128] = rows[
                pl.ds(sa * 16 + c, 4, stride=4), :
            ]
            opad[sa * 8 + 4 : sa * 8 + 8, c * 128 : c * 128 + 128] = jnp.zeros((4, 128), F32)
    high, low = split(opad[...])
    spread = dot(high, inner, 1, 1) + dot(low, inner, 1, 1)
    spread = spread.reshape(24, 8, 512)
    tau[:, 0:8, :] = jnp.zeros((24, 8, 128), F32)
    tau[:, 24:32, :] = jnp.zeros((24, 8, 128), F32)
    for b in range(4):
        tau[:, 8 + 4 * b : 12 + 4 * b, :] = spread[:, 0:4, b * 128 : b * 128 + 128]

    blank = jnp.zeros((1, 16, 128), F32)
    for i, (along_x, along_y, along_z) in enumerate(((0, 3, 4), (3, 1, 5), (4, 5, 2))):
        inside = tau[along_x * 4 : along_x * 4 + 4, 8:24, :]
        force = jnp.concatenate([inside[1:4], blank]) - jnp.concatenate([blank, inside[0:3]])
        force = force + tau[along_y * 4 : along_y * 4 + 4, 9:25, :]
        force = force - tau[along_y * 4 : along_y * 4 + 4, 7:23, :]
        inside = tau[along_z * 4 : along_z * 4 + 4, 8:24, :]
        force = (force + z_next(inside) - z_before(inside)) * 0.5
        product = at(2, 0, 0) * at(i, 0, 0)
        flow = at(0, 1, 0) * at(i, 1, 0) - at(0, -1, 0) * at(i, -1, 0)
        flow = flow + at(1, 0, 1) * at(i, 0, 1) - at(1, 0, -1) * at(i, 0, -1)
        flow = (flow + z_next(product) - z_before(product)) * 0.5
        nv_ref[i] = at(i, 0, 0) + time_step * (viscosity * laplace(i) - flow + force)

    for out, side in ((m1_ref, 1 - parity), (m2_ref, parity)):
        for j, s in enumerate((0, 3, 4)):
            out[j, 0:16, :] = tau[s * 4 + 3 * side, 8:24, :]
            out[j, 16:24, :] = jnp.zeros((8, 128), F32)
            out[3 + j] = ghost[j * 6 + 5 * side]
    for j, s in enumerate((3, 1, 5)):
        for x in range(4):
            spot = j * 4 + x
            ylow_ref[spot : spot + 1, :] = tau[s * 4 + x, 8:9, :]
            yhigh_ref[spot : spot + 1, :] = tau[s * 4 + x, 23:24, :]
            ylow_ref[12 + spot : 13 + spot, :] = ghost[j * 6 + 1 + x, 0:1, :]
            yhigh_ref[12 + spot : 13 + spot, :] = ghost[j * 6 + 1 + x, 17:18, :]


def side_kernel(x1_ref, x2_ref, ylow_ref, yhigh_ref, m1_ref, m2_ref, low, high):
    core = lax.axis_index("core")
    parity = lax.rem(lax.axis_index("y"), 2)
    low[...] = ylow_ref[...]
    high[...] = yhigh_ref[...]
    for j in range(3):
        from_low = jnp.where(parity == 0, x2_ref[3 + j], x1_ref[3 + j])
        from_high = jnp.where(parity == 0, x1_ref[3 + j], x2_ref[3 + j])
        first, last = 12 + j * 4, 15 + j * 4
        low[first : first + 1, :] += from_low[0:1]
        low[last : last + 1, :] += from_high[0:1]
        high[first : first + 1, :] += from_low[17:18]
        high[last : last + 1, :] += from_high[17:18]
    m1_ref[...] = jnp.where(core == 0, high[...], low[...])
    m2_ref[...] = jnp.where(core == 0, low[...], high[...])


def end_kernel(
    nv_ref, vg_ref, factor_ref, x1_ref, x2_ref, y1_ref, y2_ref, new_ref, grad_ref, part
):
    core = lax.axis_index("core")
    parity = lax.rem(lax.axis_index("y"), 2)
    factor = factor_ref[...]
    y_low = jnp.where(core == 0, y2_ref[...], y1_ref[...])
    y_high = jnp.where(core == 0, y1_ref[...], y2_ref[...])
    step = time_step * 0.5
    for i in range(3):
        part[...] = nv_ref[i]
        part[0] -= step * jnp.where(parity == 0, x2_ref[i, 0:16, :], x1_ref[i, 0:16, :])
        part[3] += step * jnp.where(parity == 0, x1_ref[i, 0:16, :], x2_ref[i, 0:16, :])
        for x in range(4):
            spot = i * 4 + x
            part[x, 0:1, :] -= step * y_low[spot : spot + 1]
            part[x, 15:16, :] += step * y_high[spot : spot + 1]
        new_ref[i] = part[...] / factor
        part[...] = vg_ref[i]
        part[0] += jnp.where(parity == 0, x2_ref[3 + i, 1:17, :], x1_ref[3 + i, 1:17, :])
        part[3] += jnp.where(parity == 0, x1_ref[3 + i, 1:17, :], x2_ref[3 + i, 1:17, :])
        for x in range(4):
            spot = 12 + i * 4 + x
            part[x, 0:1, :] += y_low[spot : spot + 1]
            part[x, 15:16, :] += y_high[spot : spot + 1]
        grad_ref[i] = part[...]


def weights_kernel(mine_ref, other_ref, win_ref, bin_ref, wout_ref, bout_ref):
    core = lax.axis_index("core")

    def put(out, lanes, start, count, first, second):
        done = 0
        while done < count:
            spot = start + done
            source, spot, room = (
                (first, spot, HALF - spot) if spot < HALF else (second, spot - HALF, count)
            )
            size = min(count - done, room)
            out[done : done + size, lanes * 128 : lanes * 128 + 128] = source[
                spot : spot + size, :
            ]
            done += size

    def write(first, second):
        for q in range(4):
            put(win_ref, q, q * WIN_ROWS, WIN_ROWS, first, second)
            row = second[BIAS_BASE + q - HALF, :]
            bin_ref[q * 128 : q * 128 + 128] = row
        for q in range(3):
            put(wout_ref, q, WOUT_BASE + q * 512, 512, first, second)
            row = second[BIAS_BASE + 4 + q - HALF, :]
            bout_ref[q * 128 : q * 128 + 128] = row

    @pl.when(core == 0)
    def _():
        write(mine_ref, other_ref)

    @pl.when(core == 1)
    def _():
        write(other_ref, mine_ref)


def add_kernel(first_ref, second_ref, after, out_ref):
    out_ref[...] = first_ref[...] + second_ref[...]


def arrived_kernel(got_ref, out_ref):
    out_ref[...] = got_ref[0, 0:8, :]


def across_kernel(got_ref, *rest):
    out_ref, part = rest[-2:]
    count = got_ref.shape[1]
    depth, _, width = out_ref.shape
    short = width // 128
    part[...] = jnp.zeros(part.shape, F32)
    part[0:count, :] = jnp.sum(got_ref[...], axis=0)
    for i in range(depth):
        for j in range(short):
            out_ref[i, 0:1, j * 128 : j * 128 + 128] = part[i * short + j : i * short + j + 1, :]


def along_kernel(scale, got_ref, *rest):
    out_ref = rest[-1]
    total = jnp.sum(got_ref[...], axis=0, keepdims=True) * scale
    out_ref[...] = jnp.broadcast_to(total, out_ref.shape)


def spread_kernel(got_ref, *rest):
    out_ref, part = rest[-2:]
    depth, _, width = got_ref.shape
    short = width // 128
    count = out_ref.shape[1]
    for i in range(depth):
        for j in range(short):
            part[i * short + j : i * short + j + 1, :] = got_ref[i, 0:1, j * 128 : j * 128 + 128]
    for i in range(out_ref.shape[0]):
        out_ref[i] = part[0:count, :]


def call(kernel, outs, scratch=(), places=None, room=12):
    spaces = {"v": pltpu.VMEM, "h": pltpu.HBM, "a": pl.ANY}
    specs = {}
    if places is not None:
        specs["in_specs"] = [pl.BlockSpec(memory_space=spaces[place]) for place in places]
    return pl.pallas_call(
        kernel,
        out_shape=[
            out if hasattr(out, "dtype") else jax.ShapeDtypeStruct(out, F32) for out in outs
        ],
        scratch_shapes=[
            pltpu.VMEM(shape, F32) if isinstance(shape, tuple) else shape for shape in scratch
        ],
        compiler_params=pltpu.CompilerParams(vmem_limit_bytes=room * 1024 * 1024),
        **specs,
    )


def pairs(axes):
    count = lax.axis_size(axes)
    inner = [(i, i ^ 1) for i in range(count)]
    outer = [(i, (i + 1) % count if i % 2 else (i - 1) % count) for i in range(count)]
    return inner, outer


def exchange(first, second, axes):
    inner, outer = pairs(axes)
    return lax.ppermute(first, axes, inner), lax.ppermute(second, axes, outer)


def on_device(velocity, canopy, weight_in, bias_in, weight_out, bias_out, cotangent):
    field = (3, 4, 16, 128)
    rows = (24, 128)
    layers = (6, 24, 128)
    across, along = ("x", "y"), ("zh", "zl")
    swap = [(0, 1), (1, 0)]
    parts = lax.axis_size(across)
    depth = lax.axis_size(along)
    count = HALF // parts
    short = -(-count // depth)

    direct, factor, m1, m2 = call(start_kernel, (field, field[1:], rows, rows))(
        velocity, canopy, cotangent
    )
    y1, y2 = exchange(m1, m2, GY)
    m1, m2 = call(layer_kernel, (layers, layers))(velocity, direct, y1, y2)
    x1, x2 = exchange(m1, m2, GX)
    selection = jnp.asarray(selector())
    weight_in, weight_out, selection = call(
        weights_in_kernel,
        (weight_in, weight_out, selection),
        (pltpu.SemaphoreType.DMA((3,)),),
        "ahhh",
    )(m1, weight_in, weight_out, selection)
    hidden_type = jax.ShapeDtypeStruct((128, 512), BF16)
    keep, send, ext, hidden, pre_low = call(
        main_kernel,
        ((HALF, 128), (HALF, 128), (36, 24, 128), hidden_type, hidden_type),
        ((24, 24, 128), (648, 128), (384, 128), (FLAT, 128)),
        None,
        24,
    )(
        velocity, direct, y1, y2, x1, x2,
        weight_in, bias_in[None], weight_out, selection,
    )
    got = lax.ppermute(send, "core", swap)
    nv, vg, m1, m2, ylow, yhigh = call(
        cells_kernel,
        (field, field, layers, layers, rows, rows),
        (
            (648, 128),
            (384, 128),
            (144, 768),
            (192, 512),
            (18, 24, 128),
            (24, 32, 128),
        ),
        None,
        16,
    )(direct, ext, hidden, pre_low, weight_in, weight_out, bias_out[None], selection)

    inner, outer = pairs(GX)
    x2 = lax.ppermute(m2, GX, outer)
    x1 = lax.ppermute(m1, GX, inner)
    (arrived,) = call(arrived_kernel, ((8, 128),), (), "v", 12)(x2)
    (half,) = call(add_kernel, (keep.shape,), (), "vva", 16)(keep, got, ylow)
    half = half.reshape(parts, count, 128)
    got = lax.all_to_all(half, across, 0, 0)
    m1, m2 = call(side_kernel, (rows, rows), (rows, rows))(x1, x2, ylow, yhigh)
    cut = (depth, 1, short * 128)
    (part,) = call(across_kernel, (cut,), ((short * depth, 128),), "vaa", 12)(got, arrived, x1)
    got = lax.all_to_all(part, along, 0, 0)
    y1, y2 = exchange(m1, m2, GY)
    blocks = 128 * lax.axis_size(GX) * lax.axis_size(GY)
    scaled = functools.partial(along_kernel, float(blocks) ** -0.5)
    (part,) = call(scaled, (cut,), (), "vaa", 12)(got, y1, y2)
    got = lax.all_to_all(part, along, 0, 0)
    (half,) = call(spread_kernel, (half.shape,), ((short * depth, 128),), "v", 12)(got)
    mine = lax.all_to_all(half, across, 0, 0).reshape(HALF, 128)
    new_velocity, velocity_grad = call(
        end_kernel, (field, field), ((4, 16, 128),), None, 12
    )(nv, vg, factor, x1, x2, y1, y2)
    other = lax.ppermute(mine, "core", swap)
    weight_in_grad, bias_in_grad, weight_out_grad, bias_out_grad = call(
        weights_kernel, ((648, 512), (512,), (512, 384), (384,))
    )(mine, other)
    return (
        new_velocity,
        velocity_grad,
        weight_in_grad,
        bias_in_grad,
        weight_out_grad,
        bias_out_grad,
    )


def solution(mesh):
    if mesh.devices.size == 512:
        mesh = Mesh(mesh.devices.reshape(4, 4, 4, 4, 2), GX + GY)
    placed = (
        P(None, GX, GY, None),
        P(GX, GY, None),
        P(),
        P(),
        P(),
        P(),
        P(None, GX, GY, None),
    )
    return jax.shard_map(
        on_device,
        mesh=mesh,
        in_specs=placed,
        out_specs=(P(None, GX, GY, None), P(None, GX, GY, None), P(), P(), P(), P()),
        check_vma=False,
    )
```

```python
import functools

import jax
import jax.numpy as jnp
import numpy as np
from jax import lax
from jax.experimental import pallas as pl
from jax.experimental.pallas import tpu as pltpu
from jax.sharding import Mesh, PartitionSpec as P

time_step = 0.25
viscosity = 0.2
penalty_eta = 0.05

GX = ("zh", "x", "y")
GY = ("zl", "core")
FLAT = 4352
HALF = FLAT // 2
WIN_ROWS = 648
WOUT_BASE = 4 * WIN_ROWS
BIAS_BASE = WOUT_BASE + 3 * 512
F32 = jnp.float32
BF16 = jnp.bfloat16


def selector():
    table = np.zeros((4, 128, 6, 4, 32), np.float32)
    for offset in range(6):
        for block in range(32):
            z = 4 * block + offset - 1
            if 0 <= z < 128:
                for row in range(4):
                    table[row, z, offset, row, block] = 1.0
    return table.reshape(512, 768).astype(jnp.bfloat16)


def z_next(field):
    lane = lax.broadcasted_iota(jnp.int32, field.shape, field.ndim - 1)
    return jnp.where(lane < 127, pltpu.roll(field, 127, field.ndim - 1), 0.0)


def z_before(field):
    lane = lax.broadcasted_iota(jnp.int32, field.shape, field.ndim - 1)
    return jnp.where(lane > 0, pltpu.roll(field, 1, field.ndim - 1), 0.0)


def split(value):
    high = value.astype(BF16)
    low = (value - high.astype(F32)).astype(BF16)
    return high, low


def dot(left, right, left_dim, right_dim):
    return lax.dot_general(
        left, right, (((left_dim,), (right_dim,)), ((), ())), preferred_element_type=F32
    )


def damping(canopy):
    return 1.0 + time_step * canopy.astype(F32) / penalty_eta


def start_kernel(v_ref, canopy_ref, cot_ref, direct_ref, factor_ref, m1_ref, m2_ref):
    core = lax.axis_index("core")
    factor = damping(canopy_ref[...])
    factor_ref[...] = factor
    for i in range(3):
        direct_ref[i] = cot_ref[i].astype(F32) / factor
    for out, row in ((m1_ref, 15 * (1 - core)), (m2_ref, 15 * core)):
        for i in range(3):
            for x in range(4):
                out[pl.ds(i * 4 + x, 1), :] = v_ref[i, x, pl.ds(row, 1), :]
                out[pl.ds(12 + i * 4 + x, 1), :] = (
                    direct_ref[i, x, pl.ds(row, 1), :] * time_step
                )


def weights_in_kernel(after, win_hbm, wout_hbm, sel_hbm, win_ref, wout_ref, sel_ref, sems):
    copies = [
        pltpu.make_async_copy(source, target, sems.at[i])
        for i, (source, target) in enumerate(
            ((win_hbm, win_ref), (wout_hbm, wout_ref), (sel_hbm, sel_ref))
        )
    ]
    for copy in copies:
        copy.start()
    for copy in copies:
        copy.wait()


def layer_kernel(v_ref, direct_ref, r1_ref, r2_ref, m1_ref, m2_ref):
    core = lax.axis_index("core")
    parity = lax.rem(lax.axis_index("y"), 2)
    for out, x in ((m1_ref, 3 * (1 - parity)), (m2_ref, 3 * parity)):
        for k in range(6):
            out[k, 16:24, :] = jnp.zeros((8, 128), F32)
            if k < 3:
                out[k, 1:17, :] = v_ref[k, x]
            else:
                out[k, 1:17, :] = direct_ref[k - 3, x] * time_step
            row1 = r1_ref[pl.ds(k * 4 + x, 1), :]
            row2 = r2_ref[pl.ds(k * 4 + x, 1), :]
            out[k, 0:1, :] = jnp.where(core == 0, row2, row1)
            out[k, 17:18, :] = jnp.where(core == 0, row1, row2)


def shifted(ext):
    def at(k, dx, dy):
        return ext[k * 6 + 1 + dx : k * 6 + 5 + dx, 1 + dy : 17 + dy, :]

    return at


def slopes(at):
    grad_x = [(at(3 + i, 1, 0) - at(3 + i, -1, 0)) * 0.5 for i in range(3)]
    grad_y = [(at(3 + i, 0, 1) - at(3 + i, 0, -1)) * 0.5 for i in range(3)]
    grad_z = [(z_next(at(3 + i, 0, 0)) - z_before(at(3 + i, 0, 0))) * 0.5 for i in range(3)]
    return grad_x, grad_y, grad_z


def main_kernel(
    v_ref, direct_ref, r1_ref, r2_ref, x1_ref, x2_ref,
    win_ref, bin_ref, wout_ref, sel_ref,
    keep_ref, send_ref, ext, hidden_ref, pre_low_ref, sgrad, cols, rows, flat,
):
    core = lax.axis_index("core")
    parity = lax.rem(lax.axis_index("y"), 2)

    for k in range(6):
        ext[k * 6] = jnp.where(parity == 0, x2_ref[k], x1_ref[k])
        ext[k * 6 + 5] = jnp.where(parity == 0, x1_ref[k], x2_ref[k])
        for x in range(4):
            spot = k * 6 + 1 + x
            ext[spot, 16:24, :] = jnp.zeros((8, 128), F32)
            ext[spot, 1:17, :] = v_ref[k, x] if k < 3 else direct_ref[k - 3, x] * time_step
            row1 = r1_ref[k * 4 + x : k * 4 + x + 1, :]
            row2 = r2_ref[k * 4 + x : k * 4 + x + 1, :]
            ext[spot, 0:1, :] = jnp.where(core == 0, row2, row1)
            ext[spot, 17:18, :] = jnp.where(core == 0, row1, row2)

    grad_x, grad_y, grad_z = slopes(shifted(ext))
    stress_grad = (
        grad_x[0],
        grad_y[1],
        grad_z[2],
        grad_y[0] + grad_x[1],
        grad_z[0] + grad_x[2],
        grad_z[1] + grad_y[2],
    )
    sgrad[:, 16:24, :] = jnp.zeros((24, 8, 128), F32)
    for s in range(6):
        sgrad[s * 4 : s * 4 + 4, 0:16, :] = -stress_grad[s]
    selection = sel_ref[...]
    inner = sel_ref[:, 128:640]

    parts = [sgrad[:, 4 * b : 4 * b + 8, :].reshape(192, 128) for b in range(4)]
    high, low = split(jnp.concatenate(parts, axis=1))
    picked = dot(high, inner, 1, 0) + dot(low, inner, 1, 0)
    for sa in range(24):
        for c in range(4):
            rows[pl.ds(sa * 16 + c, 4, stride=4), :] = picked[
                sa * 8 : sa * 8 + 4, c * 128 : c * 128 + 128
            ]
    rows_t = rows[...].T
    rows_low = rows_t.astype(BF16)
    bias_out_sum = jnp.sum(rows_t, axis=0, keepdims=True)

    parts = [
        ext[0:18, 4 * b : 4 * b + 8, :].reshape(144, 128).astype(BF16) for b in range(4)
    ]
    picked = dot(jnp.concatenate(parts, axis=1), selection, 1, 0)
    for g in range(18):
        for z in range(6):
            cols[pl.ds(g * 36 + z, 6, stride=6), :] = picked[
                g * 8 : g * 8 + 6, z * 128 : z * 128 + 128
            ]
    columns = cols[...].astype(BF16)

    pre_act = dot(columns, win_ref[...], 0, 0) + bin_ref[...]
    sigmoid_pre = jax.nn.sigmoid(pre_act)
    hidden = (pre_act * sigmoid_pre).astype(BF16)
    hidden_grad = dot(rows_low, wout_ref[...], 1, 1)
    pre_grad = hidden_grad * (sigmoid_pre * (1.0 + pre_act * (1.0 - sigmoid_pre)))
    pre_low = pre_grad.astype(BF16)
    hidden_ref[...] = hidden
    pre_low_ref[...] = pre_low
    bias_in_sum = jnp.sum(pre_grad, axis=0, keepdims=True)

    weight_in_sum = dot(columns, pre_low, 1, 0)
    for q in range(4):
        flat[q * WIN_ROWS : (q + 1) * WIN_ROWS, :] = weight_in_sum[:, q * 128 : q * 128 + 128]
    weight_out_sum = dot(hidden, rows_low, 0, 0)
    for q in range(3):
        flat[WOUT_BASE + q * 512 : WOUT_BASE + q * 512 + 512, :] = weight_out_sum[
            :, q * 128 : q * 128 + 128
        ]
    flat[BIAS_BASE:FLAT, :] = jnp.zeros((FLAT - BIAS_BASE, 128), F32)
    for q in range(4):
        flat[BIAS_BASE + q : BIAS_BASE + q + 1, :] = bias_in_sum[:, q * 128 : q * 128 + 128]
    for q in range(3):
        flat[BIAS_BASE + 4 + q : BIAS_BASE + 5 + q, :] = bias_out_sum[:, q * 128 : q * 128 + 128]
    keep_ref[...] = flat[pl.ds(pl.multiple_of(core * HALF, 8), HALF), :]
    send_ref[...] = flat[pl.ds(pl.multiple_of((1 - core) * HALF, 8), HALF), :]


def cells_kernel(
    direct_ref, ext, hidden_ref, pre_low_ref, win_ref, wout_ref, bout_ref, sel_ref,
    nv_ref, vg_ref, m1_ref, m2_ref, ylow_ref, yhigh_ref,
    cgrad, rows, cpad, opad, ghost, tau,
):
    parity = lax.rem(lax.axis_index("y"), 2)
    at = shifted(ext)
    grad_x, grad_y, grad_z = slopes(at)
    selection = sel_ref[...]
    inner = sel_ref[:, 128:640]

    def laplace(k):
        middle = at(k, 0, 0)
        total = at(k, 1, 0) + at(k, -1, 0) + at(k, 0, 1) + at(k, 0, -1)
        return total + z_next(middle) + z_before(middle) - 6.0 * middle

    for j in range(3):
        velocity = [at(i, 0, 0) for i in range(3)]
        slope = (grad_x, grad_y, grad_z)[j]
        total = direct_ref[j] + viscosity * laplace(3 + j)
        total = total + slope[0] * velocity[0] + slope[1] * velocity[1] + slope[2] * velocity[2]
        total = total + grad_x[j] * velocity[0] + grad_y[j] * velocity[1] + grad_z[j] * velocity[2]
        vg_ref[j] = total

    cgrad[...] = dot(win_ref[...], pre_low_ref[...], 1, 1)
    for g in range(18):
        for z in range(6):
            cpad[g * 8 : g * 8 + 6, z * 128 : z * 128 + 128] = cgrad[
                pl.ds(g * 36 + z, 6, stride=6), :
            ]
            cpad[g * 8 + 6 : g * 8 + 8, z * 128 : z * 128 + 128] = jnp.zeros((2, 128), F32)
    high, low = split(cpad[...])
    spread = dot(high, selection, 1, 1) + dot(low, selection, 1, 1)
    spread = spread.reshape(18, 8, 512)
    ghost[...] = jnp.zeros((18, 24, 128), F32)
    for b in range(4):
        ghost[:, 4 * b : 4 * b + 8, :] += spread[:, :, b * 128 : b * 128 + 128]
    for j in range(3):
        vg_ref[j] += ghost[j * 6 + 1 : j * 6 + 5, 1:17, :]

    outputs = dot(hidden_ref[...], wout_ref[...], 1, 0) + bout_ref[...]
    rows[...] = outputs.T
    for sa in range(24):
        for c in range(4):
            opad[sa * 8 : sa * 8 + 4, c * 128 : c * 128 + 128] = rows[
                pl.ds(sa * 16 + c, 4, stride=4), :
            ]
            opad[sa * 8 + 4 : sa * 8 + 8, c * 128 : c * 128 + 128] = jnp.zeros((4, 128), F32)
    high, low = split(opad[...])
    spread = dot(high, inner, 1, 1) + dot(low, inner, 1, 1)
    spread = spread.reshape(24, 8, 512)
    tau[:, 0:8, :] = jnp.zeros((24, 8, 128), F32)
    tau[:, 24:32, :] = jnp.zeros((24, 8, 128), F32)
    for b in range(4):
        tau[:, 8 + 4 * b : 12 + 4 * b, :] = spread[:, 0:4, b * 128 : b * 128 + 128]

    blank = jnp.zeros((1, 16, 128), F32)
    for i, (along_x, along_y, along_z) in enumerate(((0, 3, 4), (3, 1, 5), (4, 5, 2))):
        inside = tau[along_x * 4 : along_x * 4 + 4, 8:24, :]
        force = jnp.concatenate([inside[1:4], blank]) - jnp.concatenate([blank, inside[0:3]])
        force = force + tau[along_y * 4 : along_y * 4 + 4, 9:25, :]
        force = force - tau[along_y * 4 : along_y * 4 + 4, 7:23, :]
        inside = tau[along_z * 4 : along_z * 4 + 4, 8:24, :]
        force = (force + z_next(inside) - z_before(inside)) * 0.5
        product = at(2, 0, 0) * at(i, 0, 0)
        flow = at(0, 1, 0) * at(i, 1, 0) - at(0, -1, 0) * at(i, -1, 0)
        flow = flow + at(1, 0, 1) * at(i, 0, 1) - at(1, 0, -1) * at(i, 0, -1)
        flow = (flow + z_next(product) - z_before(product)) * 0.5
        nv_ref[i] = at(i, 0, 0) + time_step * (viscosity * laplace(i) - flow + force)

    for out, side in ((m1_ref, 1 - parity), (m2_ref, parity)):
        for j, s in enumerate((0, 3, 4)):
            out[j, 0:16, :] = tau[s * 4 + 3 * side, 8:24, :]
            out[j, 16:24, :] = jnp.zeros((8, 128), F32)
            out[3 + j] = ghost[j * 6 + 5 * side]
    for j, s in enumerate((3, 1, 5)):
        for x in range(4):
            spot = j * 4 + x
            ylow_ref[spot : spot + 1, :] = tau[s * 4 + x, 8:9, :]
            yhigh_ref[spot : spot + 1, :] = tau[s * 4 + x, 23:24, :]
            ylow_ref[12 + spot : 13 + spot, :] = ghost[j * 6 + 1 + x, 0:1, :]
            yhigh_ref[12 + spot : 13 + spot, :] = ghost[j * 6 + 1 + x, 17:18, :]


def side_kernel(x1_ref, x2_ref, ylow_ref, yhigh_ref, m1_ref, m2_ref, low, high):
    core = lax.axis_index("core")
    parity = lax.rem(lax.axis_index("y"), 2)
    low[...] = ylow_ref[...]
    high[...] = yhigh_ref[...]
    for j in range(3):
        from_low = jnp.where(parity == 0, x2_ref[3 + j], x1_ref[3 + j])
        from_high = jnp.where(parity == 0, x1_ref[3 + j], x2_ref[3 + j])
        first, last = 12 + j * 4, 15 + j * 4
        low[first : first + 1, :] += from_low[0:1]
        low[last : last + 1, :] += from_high[0:1]
        high[first : first + 1, :] += from_low[17:18]
        high[last : last + 1, :] += from_high[17:18]
    m1_ref[...] = jnp.where(core == 0, high[...], low[...])
    m2_ref[...] = jnp.where(core == 0, low[...], high[...])


def end_kernel(
    nv_ref, vg_ref, factor_ref, x1_ref, x2_ref, y1_ref, y2_ref, new_ref, grad_ref, part
):
    core = lax.axis_index("core")
    parity = lax.rem(lax.axis_index("y"), 2)
    factor = factor_ref[...]
    y_low = jnp.where(core == 0, y2_ref[...], y1_ref[...])
    y_high = jnp.where(core == 0, y1_ref[...], y2_ref[...])
    step = time_step * 0.5
    for i in range(3):
        part[...] = nv_ref[i]
        part[0] -= step * jnp.where(parity == 0, x2_ref[i, 0:16, :], x1_ref[i, 0:16, :])
        part[3] += step * jnp.where(parity == 0, x1_ref[i, 0:16, :], x2_ref[i, 0:16, :])
        for x in range(4):
            spot = i * 4 + x
            part[x, 0:1, :] -= step * y_low[spot : spot + 1]
            part[x, 15:16, :] += step * y_high[spot : spot + 1]
        new_ref[i] = part[...] / factor
        part[...] = vg_ref[i]
        part[0] += jnp.where(parity == 0, x2_ref[3 + i, 1:17, :], x1_ref[3 + i, 1:17, :])
        part[3] += jnp.where(parity == 0, x1_ref[3 + i, 1:17, :], x2_ref[3 + i, 1:17, :])
        for x in range(4):
            spot = 12 + i * 4 + x
            part[x, 0:1, :] += y_low[spot : spot + 1]
            part[x, 15:16, :] += y_high[spot : spot + 1]
        grad_ref[i] = part[...]


def weights_kernel(mine_ref, other_ref, win_ref, bin_ref, wout_ref, bout_ref):
    core = lax.axis_index("core")

    def put(out, lanes, start, count, first, second):
        done = 0
        while done < count:
            spot = start + done
            source, spot, room = (
                (first, spot, HALF - spot) if spot < HALF else (second, spot - HALF, count)
            )
            size = min(count - done, room)
            out[done : done + size, lanes * 128 : lanes * 128 + 128] = source[
                spot : spot + size, :
            ]
            done += size

    def write(first, second):
        for q in range(4):
            put(win_ref, q, q * WIN_ROWS, WIN_ROWS, first, second)
            row = second[BIAS_BASE + q - HALF, :]
            bin_ref[q * 128 : q * 128 + 128] = row
        for q in range(3):
            put(wout_ref, q, WOUT_BASE + q * 512, 512, first, second)
            row = second[BIAS_BASE + 4 + q - HALF, :]
            bout_ref[q * 128 : q * 128 + 128] = row

    @pl.when(core == 0)
    def _():
        write(mine_ref, other_ref)

    @pl.when(core == 1)
    def _():
        write(other_ref, mine_ref)


def add_kernel(first_ref, second_ref, after, out_ref):
    out_ref[...] = first_ref[...] + second_ref[...]


def arrived_kernel(got_ref, out_ref):
    out_ref[...] = got_ref[0:8] if len(got_ref.shape) == 2 else got_ref[0, 0:8, :]


def across_kernel(got_ref, *rest):
    out_ref, part = rest[-2:]
    count = got_ref.shape[1]
    depth, _, width = out_ref.shape
    short = width // 128
    part[...] = jnp.zeros(part.shape, F32)
    part[0:count, :] = jnp.sum(got_ref[...], axis=0)
    for i in range(depth):
        for j in range(short):
            out_ref[i, 0:1, j * 128 : j * 128 + 128] = part[i * short + j : i * short + j + 1, :]


def along_kernel(scale, got_ref, *rest):
    out_ref = rest[-1]
    total = jnp.sum(got_ref[...], axis=0, keepdims=True) * scale
    out_ref[...] = jnp.broadcast_to(total, out_ref.shape)


def spread_kernel(got_ref, *rest):
    out_ref, part = rest[-2:]
    depth, _, width = got_ref.shape
    short = width // 128
    count = out_ref.shape[1]
    for i in range(depth):
        for j in range(short):
            part[i * short + j : i * short + j + 1, :] = got_ref[i, 0:1, j * 128 : j * 128 + 128]
    for i in range(out_ref.shape[0]):
        out_ref[i] = part[0:count, :]


def call(kernel, outs, scratch=(), places=None, room=12):
    spaces = {"v": pltpu.VMEM, "h": pltpu.HBM, "a": pl.ANY}
    specs = {}
    if places is not None:
        specs["in_specs"] = [pl.BlockSpec(memory_space=spaces[place]) for place in places]
    return pl.pallas_call(
        kernel,
        out_shape=[
            out if hasattr(out, "dtype") else jax.ShapeDtypeStruct(out, F32) for out in outs
        ],
        scratch_shapes=[
            pltpu.VMEM(shape, F32) if isinstance(shape, tuple) else shape for shape in scratch
        ],
        compiler_params=pltpu.CompilerParams(vmem_limit_bytes=room * 1024 * 1024),
        **specs,
    )


def pairs(axes):
    count = lax.axis_size(axes)
    inner = [(i, i ^ 1) for i in range(count)]
    outer = [(i, (i + 1) % count if i % 2 else (i - 1) % count) for i in range(count)]
    return inner, outer


def exchange(first, second, axes):
    inner, outer = pairs(axes)
    return lax.ppermute(first, axes, inner), lax.ppermute(second, axes, outer)


def on_device(velocity, canopy, weight_in, bias_in, weight_out, bias_out, cotangent):
    field = (3, 4, 16, 128)
    rows = (24, 128)
    layers = (6, 24, 128)
    across, along = ("x", "y"), ("zh", "zl")
    swap = [(0, 1), (1, 0)]
    parts = lax.axis_size(across)
    depth = lax.axis_size(along)
    count = HALF // parts
    short = -(-count // depth)

    direct, factor, m1, m2 = call(start_kernel, (field, field[1:], rows, rows))(
        velocity, canopy, cotangent
    )
    y1, y2 = exchange(m1, m2, GY)
    m1, m2 = call(layer_kernel, (layers, layers))(velocity, direct, y1, y2)
    x1, x2 = exchange(m1, m2, GX)
    selection = jnp.asarray(selector())
    weight_in, weight_out, selection = call(
        weights_in_kernel,
        (weight_in, weight_out, selection),
        (pltpu.SemaphoreType.DMA((3,)),),
        "ahhh",
    )(m1, weight_in, weight_out, selection)
    hidden_type = jax.ShapeDtypeStruct((128, 512), BF16)
    keep, send, ext, hidden, pre_low = call(
        main_kernel,
        ((HALF, 128), (HALF, 128), (36, 24, 128), hidden_type, hidden_type),
        ((24, 24, 128), (648, 128), (384, 128), (FLAT, 128)),
        None,
        24,
    )(
        velocity, direct, y1, y2, x1, x2,
        weight_in, bias_in[None], weight_out, selection,
    )
    got = lax.ppermute(send, "core", swap)
    nv, vg, m1, m2, ylow, yhigh = call(
        cells_kernel,
        (field, field, layers, layers, rows, rows),
        (
            (648, 128),
            (384, 128),
            (144, 768),
            (192, 512),
            (18, 24, 128),
            (24, 32, 128),
        ),
        None,
        16,
    )(direct, ext, hidden, pre_low, weight_in, weight_out, bias_out[None], selection)

    inner, outer = pairs(GX)
    x2 = lax.ppermute(m2, GX, outer)
    x1 = lax.ppermute(m1, GX, inner)
    (arrived,) = call(arrived_kernel, ((8, 128),), (), "v", 12)(x2)
    (half,) = call(add_kernel, (keep.shape,), (), "vva", 16)(keep, got, ylow)
    half = half.reshape(parts, count, 128)
    got = lax.all_to_all(half, across, 0, 0)
    m1, m2 = call(side_kernel, (rows, rows), (rows, rows))(x1, x2, ylow, yhigh)
    cut = (depth, 1, short * 128)
    (part,) = call(across_kernel, (cut,), ((short * depth, 128),), "vaa", 12)(got, arrived, x1)
    got = lax.all_to_all(part, along, 0, 0)
    y1, y2 = exchange(m1, m2, GY)
    (arrived,) = call(arrived_kernel, ((8, 128),), (), "v", 12)(y2)
    blocks = 128 * lax.axis_size(GX) * lax.axis_size(GY)
    scaled = functools.partial(along_kernel, float(blocks) ** -0.5)
    (part,) = call(scaled, (cut,), (), "vaa", 12)(got, arrived, y1)
    got = lax.all_to_all(part, along, 0, 0)
    (half,) = call(spread_kernel, (half.shape,), ((short * depth, 128),), "v", 12)(got)
    mine = lax.all_to_all(half, across, 0, 0).reshape(HALF, 128)
    new_velocity, velocity_grad = call(
        end_kernel, (field, field), ((4, 16, 128),), None, 12
    )(nv, vg, factor, x1, x2, y1, y2)
    other = lax.ppermute(mine, "core", swap)
    weight_in_grad, bias_in_grad, weight_out_grad, bias_out_grad = call(
        weights_kernel, ((648, 512), (512,), (512, 384), (384,))
    )(mine, other)
    return (
        new_velocity,
        velocity_grad,
        weight_in_grad,
        bias_in_grad,
        weight_out_grad,
        bias_out_grad,
    )


def solution(mesh):
    if mesh.devices.size == 512:
        mesh = Mesh(mesh.devices.reshape(4, 4, 4, 4, 2), GX + GY)
    placed = (
        P(None, GX, GY, None),
        P(GX, GY, None),
        P(),
        P(),
        P(),
        P(),
        P(None, GX, GY, None),
    )
    return jax.shard_map(
        on_device,
        mesh=mesh,
        in_specs=placed,
        out_specs=(P(None, GX, GY, None), P(None, GX, GY, None), P(), P(), P(), P()),
        check_vma=False,
    )
```
